256 devices in a mesh: grp: 4 (over y), dom: 64 (over z, x, core).
Axes of the slice: x: 4, y: 4, z: 8, core: 2. Of those that a mesh axis runs over, the one named last changes fastest.
Arguments:
- u_int: bfloat16 [131072, 192], P(('grp', 'dom')), may hold values from -1.59375 to 1.59375
- u_if: bfloat16 [5632, 192], P('dom'), may hold values from -1.59375 to 1.59375
- load_int: float32 [131072, 192], P(('grp', 'dom')), may hold values from -6 to 6
- load_if: float32 [5632, 192], P('dom'), may hold values from -6 to 6
- conn: int32 [524288, 8], P(('grp', 'dom')), may hold values from 0 to 727
- send_map: int32 [1024, 32], P(('grp', 'dom')), may hold values from 0 to 599
- counts: int32 [256], P(('grp', 'dom')), may hold values from 256 to 2048, as said below
- elem_size: float32 [524288], P(('grp', 'dom')), may hold values from 0.7 to 1.4
- stiffness: float32 [524288], P(('grp', 'dom')), may hold values from 0.5 to 2
- yield_stress: float32 [524288], P(('grp', 'dom')), may hold values from 0.5 to 2
- relax_rate: float32 [524288], P(('grp', 'dom')), may hold values from 0.02 to 0.5
- stress_init: float32 [48, 524288], P(None, ('grp', 'dom')), may hold values from -6 to 6
- kinv_int: bfloat16 [393216, 1536], P(('grp', 'dom')), may hold values from -0.15625 to 0.15625
- sinv: bfloat16 [16896, 16896], P('grp', 'dom'), may hold values from -0.125 to 0.125
Outputs:
- du_int: float32 [131072, 192], P(('grp', 'dom'))
- du_if: float32 [5632, 192], P(('grp', 'dom'))
- stress_end: float32 [48, 524288], P(None, ('grp', 'dom'))
The draws below stay inside these ranges and needn't reach their ends.
Inputs may be any that keep to these rules, and one draw needn't show every extreme that they name: `counts`: every partition has at least 256 live elements and some partition has exactly 2048.
All inputs are finite; a program needn't handle non-finite values.
Results may differ from the reference program's by a relative error of at most 0.0046.
Values may be sent and summed in bfloat16 or wider, within the bound.
A program may use at most 128 MiB of HBM per device.

```python
import math
import jax
import jax.numpy as jnp
import numpy as np
from jax import lax

FOURIER = 64
TIMES = 32
INT_NODES = 512
IF_NODES = 5632
ELEM_DEV = 2048
SLOT = 32
HOP = 2
STRESS_ROWS = 48
NBR = 4
PARTITIONS = 256
ELEMS = 524288
NODES = 131072
INT_DOF = 1536
IF_DOF = 16896
LOCAL = 600
BUFFER = 728
N_GRP = 4
N_DOM = 64


def draw_counts(key, part):
    keys = jax.random.split(jax.random.fold_in(key, 7), 4)
    base = jax.random.randint(keys[0], (PARTITIONS,), ELEM_DEV // 8, ELEM_DEV // 2 + 1)
    heavy = jax.random.randint(keys[1], (PARTITIONS,), 3 * ELEM_DEV // 4, ELEM_DEV + 1)
    choose = jax.random.randint(keys[2], (PARTITIONS,), 0, 8)
    fullest = jax.random.randint(keys[3], (), 0, PARTITIONS)
    result = jnp.where(choose == 0, heavy, base)
    result = jnp.where(jnp.arange(PARTITIONS) == fullest, ELEM_DEV, result)
    return result.astype(jnp.int32)


def place_ends(entries, key, low, largest):
    longest = entries.shape.index(max(entries.shape))
    spots = []
    for shift in (0, 1):
        where = [jax.random.randint(jax.random.fold_in(key, axis), (), 0, length) for axis, length in enumerate(entries.shape)]
        where[longest] = (where[longest] + shift) % entries.shape[longest]
        spots.append(tuple(where))
    return entries.at[spots[0]].set(low).at[spots[1]].set(largest)


def strengthened(array, key, source, target, shards_of, factor):
    def block_of(dim):
        return (jnp.arange(array.shape[dim]) // (array.shape[dim] // shards_of)).reshape((-1,) + (1,) * (array.ndim - 1 - dim))

    near = jax.random.permutation(key, shards_of)[block_of(target)]
    other_side = (block_of(target) + shards_of // 2) % shards_of
    return jnp.where((block_of(source) == near) | (block_of(source) == other_side), factor * array, array)


def level_of(own_key, extent, cuts, least, largest):
    def one(dim, blocks):
        draws = jax.random.uniform(jax.random.fold_in(jax.random.fold_in(own_key, 6), dim), (blocks,), jnp.float32, least / len(cuts), largest / len(cuts))
        return jnp.repeat(jnp.exp(draws), extent[dim] // blocks).reshape((-1,) + (1,) * (len(extent) - dim - 1))

    level = one(*cuts[0])
    for cut in cuts[1:]:
        level = level * one(*cut)
    return level


def scatter_about(rng, shape, deviation, most, cuts=(), kind=jnp.bfloat16):
    factor_of = level_of(rng, shape, cuts, -0.22, 0.18) if cuts else 1.0
    values = jax.random.normal(rng, shape, jnp.float32) * deviation * factor_of
    return jnp.minimum(jnp.maximum(values, -most), most).astype(kind)


def heavy_noise(stream_key, dims, scale, most, cuts, heavy, held_as=jnp.bfloat16):
    entries = scale * jax.random.normal(stream_key, dims, jnp.float32)
    if cuts:
        entries = entries * level_of(stream_key, dims, cuts, -0.22, 0.18)
    return jnp.clip(strengthened(entries, jax.random.fold_in(stream_key, 3), *heavy), -most, most).astype(held_as)


def setup_inputs(seed: int = 0) -> dict:
    arg_keys = jax.random.split(jax.random.key(seed), 15)
    u_int = scatter_about(arg_keys[0], (NODES, 3 * FOURIER), 0.2, 1.59375, ((0, 256),))
    u_if = scatter_about(arg_keys[1], (IF_NODES, 3 * FOURIER), 0.2, 1.59375, ((0, 64),))
    load_int = scatter_about(arg_keys[2], (NODES, 3 * FOURIER), 1.0, 6.0, ((0, 256),), jnp.float32)
    load_if = scatter_about(arg_keys[3], (IF_NODES, 3 * FOURIER), 1.0, 6.0, ((0, 64),), jnp.float32)
    conn = place_ends(jax.random.randint(arg_keys[4], (ELEMS, 8), 0, BUFFER), jax.random.fold_in(arg_keys[4], 1), 0, BUFFER - 1).astype(jnp.int32)
    send_map = place_ends(jax.random.randint(arg_keys[5], (PARTITIONS * NBR, SLOT), 0, LOCAL), jax.random.fold_in(arg_keys[5], 1), 0, LOCAL - 1).astype(jnp.int32)
    counts = draw_counts(jax.random.fold_in(arg_keys[14], 71), 0)
    elem_size = jnp.clip(jnp.exp(math.log(1.4) - 0.6931472 * jax.random.uniform(arg_keys[7], (ELEMS,), jnp.float32) ** level_of(arg_keys[7], (ELEMS,), ((0, 256),), -0.2, 0.2)), 0.7, 1.4)
    stiffness = jnp.clip(jnp.exp(math.log(2.0) - 1.3862944 * jax.random.uniform(arg_keys[8], (ELEMS,), jnp.float32) ** level_of(arg_keys[8], (ELEMS,), ((0, 256),), -0.2, 0.2)), 0.5, 2.0)
    yield_stress = jnp.clip(jnp.exp(math.log(2.0) - 1.3862944 * jax.random.uniform(arg_keys[9], (ELEMS,), jnp.float32) ** level_of(arg_keys[9], (ELEMS,), ((0, 256),), -0.2, 0.2)), 0.5, 2.0)
    relax_rate = jnp.clip(jnp.exp(math.log(0.5) - 3.218876 * jax.random.uniform(arg_keys[10], (ELEMS,), jnp.float32) ** level_of(arg_keys[10], (ELEMS,), ((0, 256),), -0.2, 0.2)), 0.02, 0.5)
    stress_init = scatter_about(arg_keys[11], (STRESS_ROWS, ELEMS), 1.0, 6.0, ((1, 256),), jnp.float32)
    kinv_int = scatter_about(arg_keys[12], (PARTITIONS * INT_DOF, INT_DOF), INT_DOF ** -0.5, 0.15625, ((0, 256),))
    sinv = heavy_noise(arg_keys[13], (IF_DOF, IF_DOF), IF_DOF ** -0.5, 0.125, ((0, 4), (1, 64)), (1, 0, 64, 4.0))
    return {"u_int": u_int, "u_if": u_if, "load_int": load_int, "load_if": load_if, "conn": conn, "send_map": send_map, "counts": counts, "elem_size": elem_size, "stiffness": stiffness, "yield_stress": yield_stress, "relax_rate": relax_rate, "stress_init": stress_init, "kinv_int": kinv_int, "sinv": sinv}


POISSON = 0.3
HIGHEST = lax.Precision.HIGHEST

def strain_table():
    gauss = 1.0 / math.sqrt(3.0)
    table = np.zeros((6, 8, 8, 3))
    for point in range(8):
        coords = [((point >> bit & 1) * 2 - 1) * gauss for bit in range(3)]
        for corner in range(8):
            signs = [(corner >> bit & 1) * 2 - 1 for bit in range(3)]
            deriv = []
            for axis in range(3):
                value = signs[axis] / 8.0
                for other in range(3):
                    if other != axis:
                        value = value * (1.0 + signs[other] * coords[other])
                deriv.append(value)
            table[0, point, corner, 0] = deriv[0]
            table[1, point, corner, 1] = deriv[1]
            table[2, point, corner, 2] = deriv[2]
            table[3, point, corner, 0] = deriv[1]
            table[3, point, corner, 1] = deriv[0]
            table[4, point, corner, 1] = deriv[2]
            table[4, point, corner, 2] = deriv[1]
            table[5, point, corner, 2] = deriv[0]
            table[5, point, corner, 0] = deriv[2]
    return jnp.asarray(table.reshape(48, 24), jnp.float32).astype(jnp.bfloat16)

def time_tables(times, fourier):
    theta = 2.0 * math.pi * (np.arange(times) + 0.3) / times
    synthesis = np.zeros((fourier, times))
    for column in range(fourier):
        harmonic = column // 2
        if column % 2 == 0:
            synthesis[column] = np.cos(harmonic * theta)
        else:
            synthesis[column] = np.sin((harmonic + 1) * theta)
    analysis = synthesis.T * (2.0 / times)
    analysis[:, 0] = 1.0 / times
    return (jnp.asarray(synthesis, jnp.float32), jnp.asarray(analysis, jnp.float32))

def element_update(rows, conn_dev, count, size_e, stiff_e, yield_e, rate_e, stress_zero):
    table = strain_table()
    fourier = rows.shape[1] // 3
    synthesis, analysis = time_tables(TIMES, fourier)
    elems = conn_dev.shape[0]
    gathered = jnp.take(rows, conn_dev.reshape(-1), axis=0).reshape(elems, 24, fourier)
    strain_hat = jnp.einsum('qk,ekf->qfe', table.astype(jnp.float32), gathered.astype(jnp.float32), precision=HIGHEST)
    strain = jnp.einsum('qfe,fm->mqe', strain_hat, synthesis, precision=HIGHEST) * (2.0 / size_e)
    delta = strain - jnp.roll(strain, 1, axis=0)
    lame_first = POISSON / ((1.0 + POISSON) * (1.0 - 2.0 * POISSON))
    shear_mod = 1.0 / (2.0 * (1.0 + POISSON))
    coef = jnp.asarray(np.concatenate([np.full(24, 2.0 * shear_mod), np.full(24, shear_mod)]).reshape(48, 1), jnp.float32)

    def advance(stress, step_delta):
        trace = step_delta[0:8] + step_delta[8:16] + step_delta[16:24]
        volume = jnp.concatenate([trace, trace, trace, jnp.zeros_like(step_delta[24:48])], axis=0)
        increment = coef * step_delta + lame_first * volume
        stress = stress + stiff_e * increment - rate_e * yield_e * jnp.tanh(stress / yield_e)
        return (stress, stress)
    final, history = lax.scan(advance, stress_zero, delta, unroll=8)
    live = (jnp.arange(elems) < count).astype(jnp.float32)
    stress_hat = jnp.einsum('mqe,mf->qfe', history, analysis, precision=HIGHEST)
    forces = jnp.einsum('qfe,qk->ekf', stress_hat, table.astype(jnp.float32), precision=HIGHEST)
    forces = forces * (size_e * size_e * 0.25 * live)[:, None, None]
    assembled = jax.ops.segment_sum(forces.reshape(elems * 8, 3 * fourier), conn_dev.reshape(-1), num_segments=rows.shape[0])
    return (final * live, assembled)

def reference(u_int, u_if, load_int, load_if, conn, send_map, counts, elem_size, stiffness, yield_stress, relax_rate, stress_init, kinv_int, sinv):
    width = 3 * FOURIER
    parts = N_GRP * N_DOM
    if_dev = IF_NODES // N_DOM
    offsets = list(range(-HOP, 0)) + list(range(1, HOP + 1))
    own_if = jnp.broadcast_to(u_if.reshape(1, N_DOM, if_dev, width), (N_GRP, N_DOM, if_dev, width))
    local = jnp.concatenate([u_int.reshape(N_GRP, N_DOM, INT_NODES, width), own_if], axis=2)
    smap = send_map.reshape(N_GRP, N_DOM, NBR, SLOT)

    def pick_rows(rows, index):
        return jnp.take(rows, index.reshape(-1), axis=0).reshape(NBR, SLOT, width)
    blocks = jax.vmap(jax.vmap(pick_rows))(local, smap)
    halo = jnp.stack([jnp.roll(blocks[:, :, slot_index], offsets[slot_index], axis=1) for slot_index in range(NBR)], axis=2)
    buffers = jnp.concatenate([local, halo.reshape(N_GRP, N_DOM, NBR * SLOT, width)], axis=2).reshape(parts, BUFFER, width)

    def one_part(inputs):
        rows, conn_dev, count, size_e, stiff_e, yield_e, rate_e, stress_zero = inputs
        return element_update(rows, conn_dev, count, size_e, stiff_e, yield_e, rate_e, stress_zero)
    stress_parts, assembled = lax.map(one_part, (buffers, conn.reshape(parts, ELEM_DEV, 8), counts, elem_size.reshape(parts, ELEM_DEV), stiffness.reshape(parts, ELEM_DEV), yield_stress.reshape(parts, ELEM_DEV), relax_rate.reshape(parts, ELEM_DEV), jnp.transpose(stress_init.reshape(STRESS_ROWS, parts, ELEM_DEV), (1, 0, 2))))
    assembled = assembled.reshape(N_GRP, N_DOM, BUFFER, width)
    owned = assembled[:, :, :LOCAL]
    back = assembled[:, :, LOCAL:].reshape(N_GRP, N_DOM, NBR, SLOT, width)
    returned = jnp.stack([jnp.roll(back[:, :, slot_index], -offsets[slot_index], axis=1) for slot_index in range(NBR)], axis=2)

    def add_back(values, index):
        return jax.ops.segment_sum(values.reshape(NBR * SLOT, width), index.reshape(-1), num_segments=LOCAL)
    owned = owned + jax.vmap(jax.vmap(add_back))(returned, smap)
    r_int = load_int - owned[:, :, :INT_NODES].reshape(NODES, width)
    r_if = load_if - lax.optimization_barrier(jnp.sum(owned[:, :, INT_NODES:], axis=0)).reshape(IF_NODES, width)
    rhs_int = r_int.astype(jnp.bfloat16)
    rhs_if = r_if.astype(jnp.bfloat16)

    def one_solve(inputs):
        block, rhs = inputs
        return jnp.dot(block, rhs.reshape(INT_DOF, FOURIER), preferred_element_type=jnp.float32).reshape(INT_NODES, width)
    du_int = lax.map(one_solve, (kinv_int.reshape(parts, INT_DOF, INT_DOF), rhs_int.reshape(parts, INT_NODES, width)))
    du_int = du_int.reshape(NODES, width)
    du_if = jnp.dot(sinv, rhs_if.reshape(IF_DOF, FOURIER), preferred_element_type=jnp.float32).reshape(IF_NODES, width)
    stress_end = jnp.transpose(stress_parts, (1, 0, 2)).reshape(STRESS_ROWS, ELEMS)
    return (du_int, du_if, stress_end)
```

```python
import functools
import math

import jax
import jax.numpy as jnp
import numpy as np
from jax import lax
from jax.experimental import pallas as pl
from jax.experimental.pallas import tpu as pltpu
from jax.sharding import PartitionSpec as P

TIMES = 32
GROUP = 8
POISSON = 0.3
BF16 = jnp.bfloat16
F32 = jnp.float32


def strain_table():
    gauss = 1.0 / math.sqrt(3.0)
    table = np.zeros((6, 8, 8, 3))
    for point in range(8):
        coords = [((point >> bit & 1) * 2 - 1) * gauss for bit in range(3)]
        for corner in range(8):
            signs = [(corner >> bit & 1) * 2 - 1 for bit in range(3)]
            deriv = []
            for axis in range(3):
                value = signs[axis] / 8.0
                for other in range(3):
                    if other != axis:
                        value = value * (1.0 + signs[other] * coords[other])
                deriv.append(value)
            table[0, point, corner, 0] = deriv[0]
            table[1, point, corner, 1] = deriv[1]
            table[2, point, corner, 2] = deriv[2]
            table[3, point, corner, 0] = deriv[1]
            table[3, point, corner, 1] = deriv[0]
            table[4, point, corner, 1] = deriv[2]
            table[4, point, corner, 2] = deriv[1]
            table[5, point, corner, 2] = deriv[0]
            table[5, point, corner, 0] = deriv[2]
    return np.asarray(np.asarray(table.reshape(48, 24), np.float32), BF16).astype(np.float64)


def time_tables(times, fourier):
    theta = 2.0 * math.pi * (np.arange(times) + 0.3) / times
    synthesis = np.zeros((fourier, times))
    for column in range(fourier):
        harmonic = column // 2
        if column % 2 == 0:
            synthesis[column] = np.cos(harmonic * theta)
        else:
            synthesis[column] = np.sin((harmonic + 1) * theta)
    analysis = synthesis.T * (2.0 / times)
    analysis[:, 0] = 1.0 / times
    return synthesis.astype(np.float32).astype(np.float64), analysis.astype(np.float32).astype(np.float64)


def two_parts(x):
    high = np.asarray(x, np.float32).astype(BF16)
    low = (np.asarray(x, np.float64) - high.astype(np.float64)).astype(BF16)
    return jnp.asarray(high), jnp.asarray(low)


@functools.lru_cache(None)
def host_tables(fourier):
    table = strain_table()
    synthesis, analysis = time_tables(TIMES, fourier)
    groups = TIMES // GROUP
    steps = synthesis - np.roll(synthesis, 1, axis=1)
    synth = np.zeros((groups, 3, GROUP, 3, fourier))
    analyse = np.zeros((groups, 3, 2, GROUP, 3, fourier))
    for g in range(groups):
        for i in range(3):
            for m in range(GROUP):
                synth[g, i, m, i] = steps[:, g * GROUP + m]
                analyse[g, i, :, m, i] = analysis[g * GROUP + m]
    strain = np.zeros((GROUP, 48, 8, 3, 2, GROUP))
    force = np.zeros((8, 3, GROUP, GROUP, 48))
    shaped = table.reshape(48, 8, 3)
    for m in range(GROUP):
        for part in range(2):
            strain[m, :, :, :, part, m] = shaped
        force[:, :, m, m, :] = np.transpose(shaped, (1, 2, 0))
    width = 3 * fourier
    return (
        synth.reshape(TIMES * 3, width),
        analyse.reshape(TIMES * 6, width),
        strain.reshape(GROUP * 48, GROUP * 48),
        force.reshape(GROUP * 24, GROUP * 48),
    )


def split_rows(x):
    rows, n = x.shape
    high = x.astype(BF16).astype(F32)
    low = x - high
    parts = jnp.concatenate(
        [high.reshape(rows // 8, 1, 8, n), low.reshape(rows // 8, 1, 8, n)], axis=1
    )
    return parts.reshape(rows * 2, n).astype(BF16)


def dot(a, b):
    return lax.dot_general(a, b, (((1,), (0,)), ((), ())), preferred_element_type=F32)


def dot_t(a, b):
    return lax.dot_general(a, b, (((1,), (1,)), ((), ())), preferred_element_type=F32)


LAME = POISSON / ((1.0 + POISSON) * (1.0 - 2.0 * POISSON))
SHEAR = 1.0 / (2.0 * (1.0 + POISSON))


def element_kernel(
    counts_ref, rows_ref, conn_ref, params_ref, stress_ref,
    synth_hi_ref, synth_lo_ref, an_hi_ref, an_lo_ref, strain_ref, force_ref,
    stress_out, force_out,
    nodal, onehot, gathered, stresses, forces, total,
):
    step = pl.program_id(0)
    block = conn_ref.shape[1]
    nodes = nodal.shape[1]
    groups = TIMES // GROUP

    @pl.when(step == 0)
    def _():
        rows = rows_ref[...]
        values = dot_t(synth_hi_ref[...], rows) + dot_t(synth_lo_ref[...], rows)
        nodal[...] = split_rows(values)
        total[...] = jnp.zeros_like(total)

    iota = lax.broadcasted_iota(jnp.int16, (nodes, block), 0)
    for a in range(8):
        index = conn_ref[a : a + 1, :].astype(jnp.int16)
        hit = iota == jnp.broadcast_to(index, (nodes, block))
        onehot[:, a * block : (a + 1) * block] = jnp.where(
            hit, jnp.ones((), BF16), jnp.zeros((), BF16)
        )
    table = nodal[...]
    for a in range(8):
        picked = dot(table, onehot[:, a * block : (a + 1) * block]).astype(BF16)
        for g in range(groups):
            gathered[g, a * 48 : (a + 1) * 48, :] = picked[g * 48 : (g + 1) * 48, :]

    size = params_ref[0:1, :]
    stiff = params_ref[1:2, :]
    yields = params_ref[2:3, :]
    rate8 = jnp.broadcast_to(params_ref[3:4, :], (8, block))
    inverse = 1.0 / yields
    weight = stiff * (2.0 / size) * inverse
    shear8 = jnp.broadcast_to(weight * SHEAR, (8, block))
    shear28 = shear8 * 2.0
    lame8 = jnp.broadcast_to(weight * LAME, (8, block))
    slot = lax.broadcasted_iota(jnp.int32, (1, block), 1) + step * block
    live = (slot < counts_ref[0]).astype(F32)
    scale = size * size * 0.25 * live * yields
    state = [stress_ref[c * 8 : (c + 1) * 8, :] * inverse for c in range(6)]
    for g in range(groups):
        delta = dot(strain_ref[...], gathered[g])
        for m in range(GROUP):
            d = [delta[m * 48 + c * 8 : m * 48 + c * 8 + 8, :] for c in range(6)]
            volume = (d[0] + d[1] + d[2]) * lame8
            for c in range(6):
                rise = d[c] * shear28 + volume if c < 3 else d[c] * shear8
                state[c] = state[c] + rise - rate8 * jnp.tanh(state[c])
            stresses[m * 48 : (m + 1) * 48, :] = jnp.concatenate(state, axis=0).astype(BF16)
        pushed = dot(force_ref[...], stresses[...]) * scale
        for a in range(8):
            forces[g * 48 : (g + 1) * 48, a * block : (a + 1) * block] = split_rows(
                pushed[a * 24 : (a + 1) * 24, :]
            )
    stress_out[...] = jnp.concatenate(state, axis=0) * (yields * live)
    total[...] += dot_t(onehot[...], forces[...])

    @pl.when(step == pl.num_programs(0) - 1)
    def _():
        summed = total[...]
        high = summed.astype(BF16)
        low = (summed - high.astype(F32)).astype(BF16)
        force_out[...] = (
            dot(high, an_hi_ref[...]) + dot(high, an_lo_ref[...]) + dot(low, an_hi_ref[...])
        )


def element_update(rows, conn_dev, count, params, stress_zero, block=256):
    elems = conn_dev.shape[0]
    nodes, width = rows.shape
    padded = -(-nodes // 256) * 256
    rows = jnp.pad(rows, ((0, padded - nodes), (0, 0)))
    synth, analyse, strain, force = host_tables(width // 3)
    synth_hi, synth_lo = two_parts(synth)
    an_hi, an_lo = two_parts(analyse)
    strain = jnp.asarray(strain, BF16)
    force = jnp.asarray(force, BF16)
    conn_t = jnp.transpose(conn_dev)
    whole = lambda x: pl.BlockSpec(x.shape, lambda s: (0,) * x.ndim)
    by_block = lambda r: pl.BlockSpec((r, block), lambda s: (0, s))
    return pl.pallas_call(
        element_kernel,
        grid=(elems // block,),
        out_shape=(
            jax.ShapeDtypeStruct(stress_zero.shape, F32),
            jax.ShapeDtypeStruct((padded, width), F32),
        ),
        in_specs=[
            pl.BlockSpec(memory_space=pltpu.SMEM),
            whole(rows), by_block(8), by_block(4), by_block(48),
            whole(synth_hi), whole(synth_lo), whole(an_hi), whole(an_lo),
            whole(strain), whole(force),
        ],
        out_specs=(by_block(48), pl.BlockSpec((padded, width), lambda s: (0, 0))),
        scratch_shapes=[
            pltpu.VMEM((6 * TIMES, padded), BF16),
            pltpu.VMEM((padded, 8 * block), BF16),
            pltpu.VMEM((TIMES // GROUP, GROUP * 48, block), BF16),
            pltpu.VMEM((GROUP * 48, block), BF16),
            pltpu.VMEM((6 * TIMES, 8 * block), BF16),
            pltpu.VMEM((padded, 6 * TIMES), F32),
        ],
        compiler_params=pltpu.CompilerParams(
            vmem_limit_bytes=40 * 1024 * 1024, dimension_semantics=("arbitrary",)
        ),
        name="elements",
    )(count, rows, conn_t, params, stress_zero, synth_hi, synth_lo, an_hi, an_lo, strain, force)


def passed_along(shard, axis, by):
    peers = lax.axis_size(axis)
    return lax.ppermute(shard, axis, [(i, (i + by) % peers) for i in range(peers)])


def per_device(
    u_int, u_if, load_int, load_if, conn, send_map, counts, elem_size, stiffness,
    yield_stress, relax_rate, stress_init, kinv_int, sinv,
):
    width = u_int.shape[1]
    fourier = width // 3
    int_nodes = u_int.shape[0]
    neighbours, slots = send_map.shape
    reach = neighbours // 2
    offsets = list(range(-reach, 0)) + list(range(1, reach + 1))
    local = jnp.concatenate([u_int, u_if], axis=0)
    local_rows = local.shape[0]
    blocks = jnp.take(local, send_map.reshape(-1), axis=0).reshape(neighbours, slots, width)
    halo = [passed_along(blocks[j], "dom", offsets[j]) for j in range(neighbours)]
    buffer = jnp.concatenate([local] + halo, axis=0)
    params = jnp.stack([elem_size, stiffness, yield_stress, relax_rate], axis=0)
    stress_end, assembled = element_update(buffer, conn, counts, params, stress_init)
    owned = assembled[:local_rows]
    back = assembled[local_rows : local_rows + neighbours * slots].reshape(neighbours, slots, width)
    returned = jnp.stack([passed_along(back[j], "dom", -offsets[j]) for j in range(neighbours)], axis=0)
    owned = owned + jax.ops.segment_sum(
        returned.reshape(neighbours * slots, width), send_map.reshape(-1), num_segments=local_rows
    )
    r_int = load_int - owned[:int_nodes]
    shared = owned[int_nodes:]
    group_force = lax.psum(shared, "grp")
    r_if = load_if - group_force
    rhs_int = r_int.astype(BF16).reshape(3 * int_nodes, fourier)
    rhs_if = r_if.astype(BF16).reshape(3 * r_if.shape[0], fourier)
    partial = jnp.dot(sinv, rhs_if, preferred_element_type=F32)
    du_if = lax.psum_scatter(partial, "dom", scatter_dimension=0, tiled=True)
    du_if = du_if.reshape(-1, width)
    du_int = jnp.dot(kinv_int, rhs_int, preferred_element_type=F32).reshape(int_nodes, width)
    return (du_int, du_if, stress_end)


def solution(mesh):
    both = ("grp", "dom")
    return jax.shard_map(
        per_device,
        mesh=mesh,
        in_specs=(
            P(both, None), P("dom", None), P(both, None), P("dom", None), P(both, None),
            P(both, None), P(both), P(both), P(both), P(both), P(both), P(None, both),
            P(both, None), P("grp", "dom"),
        ),
        out_specs=(P(both, None), P(both, None), P(None, both)),
        check_vma=False,
    )
```

```python
import functools
import math

import jax
import jax.numpy as jnp
import numpy as np
from jax import lax
from jax.experimental import pallas as pl
from jax.experimental.pallas import tpu as pltpu
from jax.sharding import PartitionSpec as P

TIMES = 32
GROUP = 8
POISSON = 0.3
BF16 = jnp.bfloat16
F32 = jnp.float32


def strain_table():
    gauss = 1.0 / math.sqrt(3.0)
    table = np.zeros((6, 8, 8, 3))
    for point in range(8):
        coords = [((point >> bit & 1) * 2 - 1) * gauss for bit in range(3)]
        for corner in range(8):
            signs = [(corner >> bit & 1) * 2 - 1 for bit in range(3)]
            deriv = []
            for axis in range(3):
                value = signs[axis] / 8.0
                for other in range(3):
                    if other != axis:
                        value = value * (1.0 + signs[other] * coords[other])
                deriv.append(value)
            table[0, point, corner, 0] = deriv[0]
            table[1, point, corner, 1] = deriv[1]
            table[2, point, corner, 2] = deriv[2]
            table[3, point, corner, 0] = deriv[1]
            table[3, point, corner, 1] = deriv[0]
            table[4, point, corner, 1] = deriv[2]
            table[4, point, corner, 2] = deriv[1]
            table[5, point, corner, 2] = deriv[0]
            table[5, point, corner, 0] = deriv[2]
    return np.asarray(np.asarray(table.reshape(48, 24), np.float32), BF16).astype(np.float64)


def time_tables(times, fourier):
    theta = 2.0 * math.pi * (np.arange(times) + 0.3) / times
    synthesis = np.zeros((fourier, times))
    for column in range(fourier):
        harmonic = column // 2
        if column % 2 == 0:
            synthesis[column] = np.cos(harmonic * theta)
        else:
            synthesis[column] = np.sin((harmonic + 1) * theta)
    analysis = synthesis.T * (2.0 / times)
    analysis[:, 0] = 1.0 / times
    return synthesis.astype(np.float32).astype(np.float64), analysis.astype(np.float32).astype(np.float64)


def two_parts(x):
    high = np.asarray(x, np.float32).astype(BF16)
    low = (np.asarray(x, np.float64) - high.astype(np.float64)).astype(BF16)
    return jnp.asarray(high), jnp.asarray(low)


@functools.lru_cache(None)
def host_tables(fourier):
    table = strain_table()
    synthesis, analysis = time_tables(TIMES, fourier)
    groups = TIMES // GROUP
    steps = synthesis - np.roll(synthesis, 1, axis=1)
    synth = np.zeros((groups, 3, GROUP, 3, fourier))
    analyse = np.zeros((groups, 3, 2, GROUP, 3, fourier))
    for g in range(groups):
        for i in range(3):
            for m in range(GROUP):
                synth[g, i, m, i] = steps[:, g * GROUP + m]
                analyse[g, i, :, m, i] = analysis[g * GROUP + m]
    strain = np.zeros((GROUP, 48, 8, 3, 2, GROUP))
    force = np.zeros((8, 3, GROUP, GROUP, 48))
    shaped = table.reshape(48, 8, 3)
    for m in range(GROUP):
        for part in range(2):
            strain[m, :, :, :, part, m] = shaped
        force[:, :, m, m, :] = np.transpose(shaped, (1, 2, 0))
    width = 3 * fourier
    return (
        synth.reshape(TIMES * 3, width),
        analyse.reshape(TIMES * 6, width),
        strain.reshape(GROUP * 48, GROUP * 48),
        force.reshape(GROUP * 24, GROUP * 48),
    )


def split_rows(x):
    rows, n = x.shape
    high = x.astype(BF16).astype(F32)
    low = x - high
    parts = jnp.concatenate(
        [high.reshape(rows // 8, 1, 8, n), low.reshape(rows // 8, 1, 8, n)], axis=1
    )
    return parts.reshape(rows * 2, n).astype(BF16)


def dot(a, b):
    return lax.dot_general(a, b, (((1,), (0,)), ((), ())), preferred_element_type=F32)


def dot_t(a, b):
    return lax.dot_general(a, b, (((1,), (1,)), ((), ())), preferred_element_type=F32)


LAME = POISSON / ((1.0 + POISSON) * (1.0 - 2.0 * POISSON))
SHEAR = 1.0 / (2.0 * (1.0 + POISSON))


def element_kernel(
    counts_ref, rows_ref, conn_ref, size_ref, stiff_ref, yield_ref, rate_ref, stress_ref,
    synth_hi_ref, synth_lo_ref, an_hi_ref, an_lo_ref, strain_ref, force_ref,
    stress_out, force_out,
    nodal, onehot, gathered, stresses, forces, total,
):
    step = pl.program_id(0)
    block = conn_ref.shape[1]
    nodes = nodal.shape[1]
    groups = TIMES // GROUP

    @pl.when(step == 0)
    def _():
        rows = rows_ref[...]
        values = dot_t(synth_hi_ref[...], rows) + dot_t(synth_lo_ref[...], rows)
        nodal[...] = split_rows(values)
        total[...] = jnp.zeros_like(total)

    iota = lax.broadcasted_iota(jnp.int16, (nodes, block), 0)
    for a in range(8):
        index = conn_ref[a : a + 1, :].astype(jnp.int16)
        hit = iota == jnp.broadcast_to(index, (nodes, block))
        onehot[:, a * block : (a + 1) * block] = jnp.where(
            hit, jnp.ones((), BF16), jnp.zeros((), BF16)
        )
    table = nodal[...]
    for a in range(8):
        picked = dot(table, onehot[:, a * block : (a + 1) * block]).astype(BF16)
        for g in range(groups):
            gathered[g, a * 48 : (a + 1) * 48, :] = picked[g * 48 : (g + 1) * 48, :]

    size = size_ref[...]
    stiff = stiff_ref[...]
    yields = yield_ref[...]
    rate8 = jnp.broadcast_to(rate_ref[...], (8, block))
    inverse = 1.0 / yields
    weight = stiff * (2.0 / size) * inverse
    shear8 = jnp.broadcast_to(weight * SHEAR, (8, block))
    shear28 = shear8 * 2.0
    lame8 = jnp.broadcast_to(weight * LAME, (8, block))
    slot = lax.broadcasted_iota(jnp.int32, (1, block), 1) + step * block
    live = (slot < counts_ref[0]).astype(F32)
    scale = size * size * 0.25 * live * yields
    state = [stress_ref[c * 8 : (c + 1) * 8, :] * inverse for c in range(6)]
    for g in range(groups):
        delta = dot(strain_ref[...], gathered[g])
        for m in range(GROUP):
            d = [delta[m * 48 + c * 8 : m * 48 + c * 8 + 8, :] for c in range(6)]
            volume = (d[0] + d[1] + d[2]) * lame8
            for c in range(6):
                rise = d[c] * shear28 + volume if c < 3 else d[c] * shear8
                state[c] = state[c] + rise - rate8 * jnp.tanh(state[c])
            stresses[m * 48 : (m + 1) * 48, :] = jnp.concatenate(state, axis=0).astype(BF16)
        pushed = dot(force_ref[...], stresses[...]) * scale
        for a in range(8):
            forces[g * 48 : (g + 1) * 48, a * block : (a + 1) * block] = split_rows(
                pushed[a * 24 : (a + 1) * 24, :]
            )
    stress_out[...] = jnp.concatenate(state, axis=0) * (yields * live)
    total[...] += dot_t(onehot[...], forces[...])

    @pl.when(step == pl.num_programs(0) - 1)
    def _():
        summed = total[...]
        high = summed.astype(BF16)
        low = (summed - high.astype(F32)).astype(BF16)
        force_out[...] = (
            dot(high, an_hi_ref[...]) + dot(high, an_lo_ref[...]) + dot(low, an_hi_ref[...])
        )


def element_update(rows, conn_t, count, params, stress_zero, block=256):
    elems = conn_t.shape[1]
    padded, width = rows.shape
    synth, analyse, strain, force = host_tables(width // 3)
    synth_hi, synth_lo = two_parts(synth)
    an_hi, an_lo = two_parts(analyse)
    strain = jnp.asarray(strain, BF16)
    force = jnp.asarray(force, BF16)
    whole = lambda x: pl.BlockSpec(x.shape, lambda s: (0,) * x.ndim)
    by_block = lambda r: pl.BlockSpec((r, block), lambda s: (0, s))
    return pl.pallas_call(
        element_kernel,
        grid=(elems // block,),
        out_shape=(
            jax.ShapeDtypeStruct(stress_zero.shape, F32),
            jax.ShapeDtypeStruct((padded, width), F32),
        ),
        in_specs=[
            pl.BlockSpec(memory_space=pltpu.SMEM),
            whole(rows), by_block(8), by_block(1), by_block(1), by_block(1), by_block(1), by_block(48),
            whole(synth_hi), whole(synth_lo), whole(an_hi), whole(an_lo),
            whole(strain), whole(force),
        ],
        out_specs=(by_block(48), pl.BlockSpec((padded, width), lambda s: (0, 0))),
        scratch_shapes=[
            pltpu.VMEM((6 * TIMES, padded), BF16),
            pltpu.VMEM((padded, 8 * block), BF16),
            pltpu.VMEM((TIMES // GROUP, GROUP * 48, block), BF16),
            pltpu.VMEM((GROUP * 48, block), BF16),
            pltpu.VMEM((6 * TIMES, 8 * block), BF16),
            pltpu.VMEM((padded, 6 * TIMES), F32),
        ],
        compiler_params=pltpu.CompilerParams(
            vmem_limit_bytes=40 * 1024 * 1024, dimension_semantics=("arbitrary",)
        ),
        name="elements",
    )(count, rows, conn_t, *params, stress_zero, synth_hi, synth_lo, an_hi, an_lo, strain, force)


MESH = pl.DeviceIdType.MESH


def pair_hits(map_ref, rows):
    neighbours, slots = map_ref.shape
    listed = jnp.concatenate([map_ref[j : j + 1, :] for j in range(neighbours)], axis=1)
    iota = lax.broadcasted_iota(jnp.int32, (rows, neighbours * slots), 0)
    return (iota == listed).astype(F32)


def greet(peers):
    barrier = pltpu.get_barrier_semaphore()
    for peer in peers:
        pl.semaphore_signal(barrier, inc=1, device_id=peer, device_id_type=MESH)
    pl.semaphore_wait(barrier, len(peers))


def send(src, dst, send_sem, recv_sem, peer):
    copy = pltpu.make_async_remote_copy(
        src_ref=src, dst_ref=dst, send_sem=send_sem, recv_sem=recv_sem,
        device_id=peer, device_id_type=MESH,
    )
    copy.start()
    return copy


def halo_kernel(dom, offsets, int_ref, if_ref, map_ref, conn_ref, rows_out, conn_out, out_block, in_block, send_sem, recv_sem):
    me = lax.axis_index("dom")
    near = [{"dom": lax.rem(me + off + dom, dom)} for off in offsets]
    int_nodes, width = int_ref.shape
    if_nodes = if_ref.shape[0]
    slots = map_ref.shape[1]
    owned = int_nodes + if_nodes
    local = jnp.concatenate([int_ref[...], if_ref[...]], axis=0)
    hits = jnp.transpose(pair_hits(map_ref, owned)).astype(BF16)
    picked = dot(hits, local).astype(BF16)
    for j in range(len(offsets)):
        out_block[j] = picked[j * slots : (j + 1) * slots]
    greet(near)
    copies = [
        send(out_block.at[j], in_block.at[j], send_sem.at[j], recv_sem.at[j], near[j])
        for j in range(len(offsets))
    ]
    conn_out[...] = jnp.transpose(conn_ref[...])
    rows_out[...] = jnp.zeros_like(rows_out)
    rows_out[0:owned] = local
    for j, copy in enumerate(copies):
        copy.wait()
        rows_out[owned + j * slots : owned + (j + 1) * slots] = in_block[j]


def halo(u_int, u_if, send_map, conn, offsets, dom):
    neighbours, slots = send_map.shape
    width = u_int.shape[1]
    used = u_int.shape[0] + u_if.shape[0] + neighbours * slots
    padded = -(-used // 256) * 256
    vmem = pl.BlockSpec(memory_space=pltpu.VMEM)
    return pl.pallas_call(
        functools.partial(halo_kernel, dom, offsets),
        out_shape=(
            jax.ShapeDtypeStruct((padded, width), BF16),
            jax.ShapeDtypeStruct((conn.shape[1], conn.shape[0]), jnp.int32),
        ),
        in_specs=[vmem] * 4,
        out_specs=(vmem, vmem),
        scratch_shapes=[
            pltpu.VMEM((neighbours, slots, width), BF16),
            pltpu.VMEM((neighbours, slots, width), BF16),
            pltpu.SemaphoreType.DMA((neighbours,)),
            pltpu.SemaphoreType.DMA((neighbours,)),
        ],
        compiler_params=pltpu.CompilerParams(
            collective_id=0, has_side_effects=True, vmem_limit_bytes=24 * 1024 * 1024
        ),
        name="halo",
    )(u_int, u_if, send_map, conn)


def finish_kernel(
    sizes, offsets,
    force_ref, map_ref, load_int_ref, load_if_ref, kinv_hbm, sinv_hbm,
    du_int_ref, du_if_ref,
    kinv, sinv, out_ret, in_ret, spread, spread_if, rhs_int,
    out_grp, in_grp, out_rhs, all_rhs, flat,
    own1, out1, in1, out2, in2, own3, out3, in3, last,
    local_sem, ret_sem, grp_sem, rhs_sem, sem1, sem2, sem3,
):
    zs, xs, cores, grps = sizes
    dom = zs * xs * cores
    me = lax.axis_index("dom")
    my_grp = lax.axis_index("grp")
    core = lax.rem(me, cores)
    x = lax.rem(me // cores, xs)
    z = me // (cores * xs)
    fetch_kinv = pltpu.make_async_copy(kinv_hbm, kinv, local_sem.at[0])
    fetch_sinv = pltpu.make_async_copy(sinv_hbm, sinv, local_sem.at[1])
    fetch_kinv.start()
    fetch_sinv.start()
    at = lambda zz, xx, cc: {"dom": (zz * xs + xx) * cores + cc}
    owners = [{"dom": lax.rem(me - off + dom, dom)} for off in offsets]
    groups = [{"grp": lax.rem(my_grp + s, grps)} for s in range(1, grps)]
    sibling = at(z, x, 1 - core)
    along_x = [at(z, lax.rem(x + s, xs), core) for s in range(1, xs)]
    along_z = [at(lax.rem(z + s, zs), x, core) for s in range(1, zs)]
    neighbours, slots = map_ref.shape
    int_nodes, width = load_int_ref.shape
    if_nodes = load_if_ref.shape[0]
    fourier = width // 3
    owned = int_nodes + if_nodes
    for j in range(neighbours):
        out_ret[j] = force_ref[owned + j * slots : owned + (j + 1) * slots, :]
    greet(owners + groups + [sibling] + along_x + along_z)
    copies = [
        send(out_ret.at[j], in_ret.at[j], ret_sem.at[0, j], ret_sem.at[1, j], owners[j])
        for j in range(neighbours)
    ]
    hits = pair_hits(map_ref, owned).astype(BF16)
    for copy in copies:
        copy.wait()
    back = jnp.concatenate([in_ret[j] for j in range(neighbours)], axis=0)
    high = back.astype(BF16)
    low = (back - high.astype(F32)).astype(BF16)
    force = force_ref[0:owned, :] + dot(hits, high) + dot(hits, low)
    share = out_grp.shape[1]
    pieces = jnp.concatenate(
        [force[int_nodes:], jnp.zeros((grps * share - if_nodes, width), F32)], axis=0
    )
    for q in range(grps):
        out_grp[q] = pieces[q * share : (q + 1) * share]
    copies = [
        send(out_grp.at[peer["grp"]], in_grp.at[s], grp_sem.at[0, s], grp_sem.at[1, s], peer)
        for s, peer in enumerate(groups)
    ]
    r_int = load_int_ref[...] - force[:int_nodes]
    for i in range(3):
        spread[pl.ds(i, int_nodes, stride=3), :] = r_int[:, i * fourier : (i + 1) * fourier]
    rhs_int[...] = spread[...].astype(BF16)
    fetch_kinv.wait()
    chunk = 256
    chunks = kinv.shape[0] // chunk

    def solve(c, _):
        rows = pl.ds(pl.multiple_of(c * chunk, chunk), chunk)
        spread[rows, :] = dot(kinv[rows, :], rhs_int[...])
        return 0

    lax.fori_loop(0, chunks // 2, solve, 0)
    loads = jnp.concatenate(
        [load_if_ref[...], jnp.zeros((grps * share - if_nodes, width), F32)], axis=0
    )
    mine = loads[0:share]
    for q in range(1, grps):
        mine = jnp.where(my_grp == q, loads[q * share : (q + 1) * share], mine)
    total = out_grp[my_grp]
    for s, copy in enumerate(copies):
        copy.wait()
        total = total + in_grp[s]
    out_rhs[...] = (mine - total).astype(BF16)
    copies = [
        send(out_rhs, all_rhs.at[my_grp], rhs_sem.at[0, s], rhs_sem.at[1, s], peer)
        for s, peer in enumerate(groups)
    ]
    all_rhs[my_grp] = out_rhs[...]
    lax.fori_loop(chunks // 2, chunks, solve, 0)
    for copy in copies:
        copy.wait()
    gathered = jnp.concatenate([all_rhs[q].astype(F32) for q in range(grps)], axis=0)[:if_nodes]
    for i in range(3):
        spread_if[pl.ds(i, if_nodes, stride=3), :] = gathered[:, i * fourier : (i + 1) * fourier]
    rhs_if = spread_if[...]
    empty = jnp.zeros_like(rhs_if)
    left = jnp.concatenate([rhs_if, empty], axis=1).astype(BF16)
    right = jnp.concatenate([empty, rhs_if], axis=1).astype(BF16)
    fetch_sinv.wait()
    half = zs // 2
    per_owner = sinv.shape[0] // dom
    per_z = per_owner * xs * cores
    for q in range(half):
        flat[q * per_z : (q + 1) * per_z, :] = dot(
            sinv[q * per_z : (q + 1) * per_z, :], left
        ) + dot(sinv[(half + q) * per_z : (half + q + 1) * per_z, :], right)
    fill = jnp.zeros((out1.shape[1] - half * per_owner, 2 * fourier), F32)
    for k in range(xs):
        by_core = []
        for c in range(cores):
            rows = [
                flat[q * per_z + (k * cores + c) * per_owner : q * per_z + (k * cores + c + 1) * per_owner, :]
                for q in range(half)
            ]
            by_core.append(jnp.concatenate(rows + [fill], axis=0))
        own1[k] = jnp.where(core == 0, by_core[0], by_core[1])
        out1[k] = jnp.where(core == 0, by_core[1], by_core[0]).astype(BF16)
    copy = send(out1, in1, sem1.at[0], sem1.at[1], sibling)
    for i in range(3):
        du_int_ref[:, i * fourier : (i + 1) * fourier] = spread[pl.ds(i, int_nodes, stride=3), :]
    copy.wait()
    for k in range(xs):
        summed = own1[k] + in1[k].astype(F32)
        own1[k] = summed
        out2[k] = summed.astype(BF16)
    copies = [
        send(out2.at[lax.rem(x + s + 1, xs)], in2.at[s], sem2.at[0, s], sem2.at[1, s], peer)
        for s, peer in enumerate(along_x)
    ]
    summed = own1[x]
    for s, copy in enumerate(copies):
        copy.wait()
        summed = summed + in2[s].astype(F32)
    turned = pltpu.roll(summed, fourier, 1)
    short = per_owner // 2
    first = lax.broadcasted_iota(jnp.int32, (short, 2 * fourier), 1) < fourier
    fill = jnp.zeros((out3.shape[1] - short, 2 * fourier), F32)
    for q in range(half):
        top = slice(q * per_owner, q * per_owner + short)
        low_rows = slice(q * per_owner + short, (q + 1) * per_owner)
        for h, (a, b) in enumerate(((summed, turned), (turned, summed))):
            block = jnp.concatenate([jnp.where(first, a[top], b[low_rows]), fill], axis=0)
            own3[h * half + q] = block
            out3[h * half + q] = block.astype(BF16)
    copies = [
        send(out3.at[lax.rem(z + s + 1, zs)], in3.at[s], sem3.at[0, s], sem3.at[1, s], peer)
        for s, peer in enumerate(along_z)
    ]
    summed = own3[z]
    for s, copy in enumerate(copies):
        copy.wait()
        summed = summed + in3[s].astype(F32)
    last[0] = summed
    last[1] = pltpu.roll(summed, fourier, 1)
    nodes = short // 3
    for h in range(2):
        for i in range(3):
            du_if_ref[h * nodes : (h + 1) * nodes, i * fourier : (i + 1) * fourier] = last[
                h, pl.ds(i, nodes, stride=3), :
            ][:, :fourier]


def finish(force, send_map, load_int, load_if, kinv_int, sinv, offsets, sizes):
    zs, xs, cores, grps = sizes
    neighbours, slots = send_map.shape
    int_nodes, width = load_int.shape
    if_nodes = load_if.shape[0]
    fourier = width // 3
    dom = zs * xs * cores
    per_owner = sinv.shape[0] // dom
    up = lambda n, k: -(-n // k) * k
    share = up(-(-if_nodes // grps), 8)
    rows1 = up(per_owner * (zs // 2), 16)
    rows3 = up(per_owner // 2, 16)
    vmem = pl.BlockSpec(memory_space=pltpu.VMEM)
    far = pl.BlockSpec(memory_space=pl.ANY)
    sems = pltpu.SemaphoreType.DMA
    lanes = 2 * fourier
    return pl.pallas_call(
        functools.partial(finish_kernel, sizes, offsets),
        out_shape=(
            jax.ShapeDtypeStruct((int_nodes, width), F32),
            jax.ShapeDtypeStruct((per_owner // 3, width), F32),
        ),
        in_specs=[vmem] * 4 + [far, far],
        out_specs=(vmem, vmem),
        scratch_shapes=[
            pltpu.VMEM(kinv_int.shape, BF16),
            pltpu.VMEM(sinv.shape, BF16),
            pltpu.VMEM((neighbours, slots, width), F32),
            pltpu.VMEM((neighbours, slots, width), F32),
            pltpu.VMEM((3 * int_nodes, fourier), F32),
            pltpu.VMEM((3 * if_nodes, fourier), F32),
            pltpu.VMEM((3 * int_nodes, fourier), BF16),
            pltpu.VMEM((grps, share, width), F32),
            pltpu.VMEM((grps - 1, share, width), F32),
            pltpu.VMEM((share, width), BF16),
            pltpu.VMEM((grps, share, width), BF16),
            pltpu.VMEM((sinv.shape[0] // 2, lanes), F32),
            pltpu.VMEM((xs, rows1, lanes), F32),
            pltpu.VMEM((xs, rows1, lanes), BF16),
            pltpu.VMEM((xs, rows1, lanes), BF16),
            pltpu.VMEM((xs, rows1, lanes), BF16),
            pltpu.VMEM((xs - 1, rows1, lanes), BF16),
            pltpu.VMEM((zs, rows3, lanes), F32),
            pltpu.VMEM((zs, rows3, lanes), BF16),
            pltpu.VMEM((zs - 1, rows3, lanes), BF16),
            pltpu.VMEM((2, rows3, lanes), F32),
            sems((2,)), sems((2, neighbours)), sems((2, grps - 1)), sems((2, grps - 1)),
            sems((2,)), sems((2, xs - 1)), sems((2, zs - 1)),
        ],
        compiler_params=pltpu.CompilerParams(
            collective_id=1, has_side_effects=True, vmem_limit_bytes=40 * 1024 * 1024
        ),
        name="finish",
    )(force, send_map, load_int, load_if, kinv_int, sinv)


def per_device(
    u_int, u_if, load_int, load_if, conn, send_map, counts, elem_size, stiffness,
    yield_stress, relax_rate, stress_init, kinv_int, sinv,
):
    reach = send_map.shape[0] // 2
    offsets = list(range(-reach, 0)) + list(range(1, reach + 1))
    dom, grps = lax.axis_size("dom"), lax.axis_size("grp")
    sizes = (dom // 8, 4, 2, grps)
    rows, conn_t = halo(u_int, u_if, send_map, conn, offsets, dom)
    params = [v.reshape(1, -1) for v in (elem_size, stiffness, yield_stress, relax_rate)]
    stress_end, force = element_update(rows, conn_t, counts, params, stress_init)
    du_int, du_if = finish(force, send_map, load_int, load_if, kinv_int, sinv, offsets, sizes)
    return (du_int, du_if, stress_end)


def solution(mesh):
    both = ("grp", "dom")
    return jax.shard_map(
        per_device,
        mesh=mesh,
        in_specs=(
            P(both, None), P("dom", None), P(both, None), P("dom", None), P(both, None),
            P(both, None), P(both), P(both), P(both), P(both), P(both), P(None, both),
            P(both, None), P("grp", "dom"),
        ),
        out_specs=(P(both, None), P(both, None), P(None, both)),
        check_vma=False,
    )
```

```python
import functools
import math

import jax
import jax.numpy as jnp
import numpy as np
from jax import lax
from jax.experimental import pallas as pl
from jax.experimental.pallas import tpu as pltpu
from jax.sharding import PartitionSpec as P

TIMES = 32
GROUP = 8
POISSON = 0.3
BF16 = jnp.bfloat16
F32 = jnp.float32


def strain_table():
    gauss = 1.0 / math.sqrt(3.0)
    table = np.zeros((6, 8, 8, 3))
    for point in range(8):
        coords = [((point >> bit & 1) * 2 - 1) * gauss for bit in range(3)]
        for corner in range(8):
            signs = [(corner >> bit & 1) * 2 - 1 for bit in range(3)]
            deriv = []
            for axis in range(3):
                value = signs[axis] / 8.0
                for other in range(3):
                    if other != axis:
                        value = value * (1.0 + signs[other] * coords[other])
                deriv.append(value)
            table[0, point, corner, 0] = deriv[0]
            table[1, point, corner, 1] = deriv[1]
            table[2, point, corner, 2] = deriv[2]
            table[3, point, corner, 0] = deriv[1]
            table[3, point, corner, 1] = deriv[0]
            table[4, point, corner, 1] = deriv[2]
            table[4, point, corner, 2] = deriv[1]
            table[5, point, corner, 2] = deriv[0]
            table[5, point, corner, 0] = deriv[2]
    return np.asarray(np.asarray(table.reshape(48, 24), np.float32), BF16).astype(np.float64)


def time_tables(times, fourier):
    theta = 2.0 * math.pi * (np.arange(times) + 0.3) / times
    synthesis = np.zeros((fourier, times))
    for column in range(fourier):
        harmonic = column // 2
        if column % 2 == 0:
            synthesis[column] = np.cos(harmonic * theta)
        else:
            synthesis[column] = np.sin((harmonic + 1) * theta)
    analysis = synthesis.T * (2.0 / times)
    analysis[:, 0] = 1.0 / times
    return synthesis.astype(np.float32).astype(np.float64), analysis.astype(np.float32).astype(np.float64)


def two_parts(x):
    high = np.asarray(x, np.float32).astype(BF16)
    low = (np.asarray(x, np.float64) - high.astype(np.float64)).astype(BF16)
    return jnp.asarray(high), jnp.asarray(low)


@functools.lru_cache(None)
def host_tables(fourier):
    table = strain_table()
    synthesis, analysis = time_tables(TIMES, fourier)
    groups = TIMES // GROUP
    steps = synthesis - np.roll(synthesis, 1, axis=1)
    synth = np.zeros((groups, 3, GROUP, 3, fourier))
    analyse = np.zeros((groups, 3, 2, GROUP, 3, fourier))
    for g in range(groups):
        for i in range(3):
            for m in range(GROUP):
                synth[g, i, m, i] = steps[:, g * GROUP + m]
                analyse[g, i, :, m, i] = analysis[g * GROUP + m]
    strain = np.zeros((GROUP, 48, 8, 3, 2, GROUP))
    force = np.zeros((8, 3, GROUP, GROUP, 48))
    shaped = table.reshape(48, 8, 3)
    for m in range(GROUP):
        for part in range(2):
            strain[m, :, :, :, part, m] = shaped
        force[:, :, m, m, :] = np.transpose(shaped, (1, 2, 0))
    width = 3 * fourier
    return (
        synth.reshape(TIMES * 3, width),
        analyse.reshape(TIMES * 6, width),
        strain.reshape(GROUP * 48, GROUP * 48),
        force.reshape(GROUP * 24, GROUP * 48),
    )


def split_rows(x):
    rows, n = x.shape
    high = x.astype(BF16).astype(F32)
    low = x - high
    parts = jnp.concatenate(
        [high.reshape(rows // 8, 1, 8, n), low.reshape(rows // 8, 1, 8, n)], axis=1
    )
    return parts.reshape(rows * 2, n).astype(BF16)


def dot(a, b):
    return lax.dot_general(a, b, (((1,), (0,)), ((), ())), preferred_element_type=F32)


def dot_t(a, b):
    return lax.dot_general(a, b, (((1,), (1,)), ((), ())), preferred_element_type=F32)


LAME = POISSON / ((1.0 + POISSON) * (1.0 - 2.0 * POISSON))
SHEAR = 1.0 / (2.0 * (1.0 + POISSON))


def element_kernel(
    counts_ref, int_ref, tail_ref, conn_ref, size_ref, stiff_ref, yield_ref, rate_ref, stress_ref,
    synth_hi_ref, synth_lo_ref, an_hi_ref, an_lo_ref, strain_ref, force_ref,
    stress_out, force_out,
    nodal, onehot, gathered, stresses, forces, total,
):
    step = pl.program_id(0)
    block = conn_ref.shape[1]
    nodes = nodal.shape[1]
    groups = TIMES // GROUP

    @pl.when(step == 0)
    def _():
        inner, tail = int_ref[...], tail_ref[...]
        first = inner.shape[1]
        high, low = synth_hi_ref[...], synth_lo_ref[...]
        nodal[:, :first] = split_rows(dot(high, inner) + dot(low, inner))
        nodal[:, first:] = split_rows(dot_t(high, tail) + dot_t(low, tail))
        total[...] = jnp.zeros_like(total)

    iota = lax.broadcasted_iota(jnp.int16, (nodes, block), 0)
    for a in range(8):
        index = conn_ref[a : a + 1, :].astype(jnp.int16)
        hit = iota == jnp.broadcast_to(index, (nodes, block))
        onehot[:, a * block : (a + 1) * block] = jnp.where(
            hit, jnp.ones((), BF16), jnp.zeros((), BF16)
        )
    table = nodal[...]
    for a in range(8):
        picked = dot(table, onehot[:, a * block : (a + 1) * block]).astype(BF16)
        for g in range(groups):
            gathered[g, a * 48 : (a + 1) * 48, :] = picked[g * 48 : (g + 1) * 48, :]

    size = size_ref[...]
    stiff = stiff_ref[...]
    yields = yield_ref[...]
    rate8 = jnp.broadcast_to(rate_ref[...], (8, block))
    inverse = 1.0 / yields
    weight = stiff * (2.0 / size) * inverse
    shear8 = jnp.broadcast_to(weight * SHEAR, (8, block))
    shear28 = shear8 * 2.0
    lame8 = jnp.broadcast_to(weight * LAME, (8, block))
    slot = lax.broadcasted_iota(jnp.int32, (1, block), 1) + step * block
    live = (slot < counts_ref[0]).astype(F32)
    scale = size * size * 0.25 * live * yields
    state = [stress_ref[c * 8 : (c + 1) * 8, :] * inverse for c in range(6)]
    for g in range(groups):
        delta = dot(strain_ref[...], gathered[g])
        for m in range(GROUP):
            d = [delta[m * 48 + c * 8 : m * 48 + c * 8 + 8, :] for c in range(6)]
            volume = (d[0] + d[1] + d[2]) * lame8
            for c in range(6):
                rise = d[c] * shear28 + volume if c < 3 else d[c] * shear8
                state[c] = state[c] + rise - rate8 * jnp.tanh(state[c])
            stresses[m * 48 : (m + 1) * 48, :] = jnp.concatenate(state, axis=0).astype(BF16)
        pushed = dot(force_ref[...], stresses[...]) * scale
        for a in range(8):
            forces[g * 48 : (g + 1) * 48, a * block : (a + 1) * block] = split_rows(
                pushed[a * 24 : (a + 1) * 24, :]
            )
    stress_out[...] = jnp.concatenate(state, axis=0) * (yields * live)
    total[...] += dot_t(onehot[...], forces[...])

    @pl.when(step == pl.num_programs(0) - 1)
    def _():
        summed = total[...]
        high = summed.astype(BF16)
        low = (summed - high.astype(F32)).astype(BF16)
        force_out[...] = (
            dot(high, an_hi_ref[...]) + dot(high, an_lo_ref[...]) + dot(low, an_hi_ref[...])
        )


def element_update(inner, tail, conn_t, count, params, stress_zero, block=256):
    elems = conn_t.shape[1]
    width = inner.shape[0]
    padded = inner.shape[1] + tail.shape[0]
    synth, analyse, strain, force = host_tables(width // 3)
    synth_hi, synth_lo = two_parts(synth)
    an_hi, an_lo = two_parts(analyse)
    strain = jnp.asarray(strain, BF16)
    force = jnp.asarray(force, BF16)
    whole = lambda x: pl.BlockSpec(x.shape, lambda s: (0,) * x.ndim)
    by_block = lambda r: pl.BlockSpec((r, block), lambda s: (0, s))
    return pl.pallas_call(
        element_kernel,
        grid=(elems // block,),
        out_shape=(
            jax.ShapeDtypeStruct(stress_zero.shape, F32),
            jax.ShapeDtypeStruct((padded, width), F32),
        ),
        in_specs=[
            pl.BlockSpec(memory_space=pltpu.SMEM),
            whole(inner), whole(tail), by_block(8), by_block(1), by_block(1), by_block(1), by_block(1), by_block(48),
            whole(synth_hi), whole(synth_lo), whole(an_hi), whole(an_lo),
            whole(strain), whole(force),
        ],
        out_specs=(by_block(48), pl.BlockSpec((padded, width), lambda s: (0, 0))),
        scratch_shapes=[
            pltpu.VMEM((6 * TIMES, padded), BF16),
            pltpu.VMEM((padded, 8 * block), BF16),
            pltpu.VMEM((TIMES // GROUP, GROUP * 48, block), BF16),
            pltpu.VMEM((GROUP * 48, block), BF16),
            pltpu.VMEM((6 * TIMES, 8 * block), BF16),
            pltpu.VMEM((padded, 6 * TIMES), F32),
        ],
        compiler_params=pltpu.CompilerParams(
            vmem_limit_bytes=24 * 1024 * 1024, dimension_semantics=("arbitrary",)
        ),
        cost_estimate=pl.CostEstimate(flops=25000000000, bytes_accessed=4000000, transcendentals=0),
        name="elements",
    )(count, inner, tail, conn_t, *params, stress_zero, synth_hi, synth_lo, an_hi, an_lo, strain, force)


MESH = pl.DeviceIdType.MESH


def pair_hits(map_ref, rows):
    neighbours, slots = map_ref.shape
    listed = jnp.concatenate([map_ref[j : j + 1, :] for j in range(neighbours)], axis=1)
    iota = lax.broadcasted_iota(jnp.int32, (rows, neighbours * slots), 0)
    return (iota == listed).astype(F32)


def greet(peers):
    barrier = pltpu.get_barrier_semaphore()
    for peer in peers:
        pl.semaphore_signal(barrier, inc=1, device_id=peer, device_id_type=MESH)
    pl.semaphore_wait(barrier, len(peers))


def send(src, dst, send_sem, recv_sem, peer):
    copy = pltpu.make_async_remote_copy(
        src_ref=src, dst_ref=dst, send_sem=send_sem, recv_sem=recv_sem,
        device_id=peer, device_id_type=MESH,
    )
    copy.start()
    return copy


def halo_kernel(dom, offsets, int_ref, if_ref, map_ref, tail_out, out_block, in_block, send_sem, recv_sem):
    me = lax.axis_index("dom")
    near = [{"dom": lax.rem(me + off + dom, dom)} for off in offsets]
    width, int_nodes = int_ref.shape
    if_nodes = if_ref.shape[0]
    slots = map_ref.shape[1]
    hits = jnp.transpose(pair_hits(map_ref, int_nodes + if_nodes)).astype(BF16)
    picked = (
        dot_t(hits[:, :int_nodes], int_ref[...]) + dot(hits[:, int_nodes:], if_ref[...])
    ).astype(BF16)
    for j in range(len(offsets)):
        out_block[j] = picked[j * slots : (j + 1) * slots]
    greet(near)
    copies = [
        send(out_block.at[j], in_block.at[j], send_sem.at[j], recv_sem.at[j], near[j])
        for j in range(len(offsets))
    ]
    for copy in copies:
        copy.wait()
    parts = [if_ref[...].astype(F32)] + [in_block[j].astype(F32) for j in range(len(offsets))]
    fill = tail_out.shape[0] - if_nodes - len(offsets) * slots
    tail_out[...] = jnp.concatenate(parts + [jnp.zeros((fill, width), F32)], axis=0).astype(BF16)


def halo(u_int_t, u_if, send_map, offsets, dom):
    neighbours, slots = send_map.shape
    width, int_nodes = u_int_t.shape
    used = int_nodes + u_if.shape[0] + neighbours * slots
    padded = -(-used // 256) * 256
    vmem = pl.BlockSpec(memory_space=pltpu.VMEM)
    return pl.pallas_call(
        functools.partial(halo_kernel, dom, offsets),
        out_shape=jax.ShapeDtypeStruct((padded - int_nodes, width), BF16),
        in_specs=[vmem] * 3,
        out_specs=vmem,
        scratch_shapes=[
            pltpu.VMEM((neighbours, slots, width), BF16),
            pltpu.VMEM((neighbours, slots, width), BF16),
            pltpu.SemaphoreType.DMA((neighbours,)),
            pltpu.SemaphoreType.DMA((neighbours,)),
        ],
        compiler_params=pltpu.CompilerParams(
            collective_id=0, has_side_effects=True, vmem_limit_bytes=12 * 1024 * 1024
        ),
        cost_estimate=pl.CostEstimate(flops=6000000000, bytes_accessed=1000000, transcendentals=0),
        name="halo",
    )(u_int_t, u_if, send_map)


def finish_kernel(
    sizes, offsets, stop,
    force_ref, map_ref, load_int_ref, load_if_ref, kinv, sinv_t,
    du_int_ref, du_if_ref,
    sinv, out_ret, in_ret, spread, spread_if, rhs_int,
    out_grp, in_grp, out_rhs, all_rhs, flat,
    own1, out1, in1, out2, in2, own3, out3, in3, last,
    ret_sem, grp_sem, rhs_sem, sem1, sem2, sem3,
):
    zs, xs, cores, grps = sizes
    dom = zs * xs * cores
    me = lax.axis_index("dom")
    my_grp = lax.axis_index("grp")
    core = lax.rem(me, cores)
    x = lax.rem(me // cores, xs)
    z = me // (cores * xs)
    at = lambda zz, xx, cc: {"dom": (zz * xs + xx) * cores + cc}
    owners = [{"dom": lax.rem(me - off + dom, dom)} for off in offsets]
    groups = [{"grp": lax.rem(my_grp + s, grps)} for s in range(1, grps)]
    sibling = at(z, x, 1 - core)
    along_x = [at(z, lax.rem(x + s, xs), core) for s in range(1, xs)]
    along_z = [at(lax.rem(z + s, zs), x, core) for s in range(1, zs)]
    neighbours, slots = map_ref.shape
    width, int_nodes = load_int_ref.shape
    if_nodes = load_if_ref.shape[0]
    fourier = width // 3
    owned = int_nodes + if_nodes
    for j in range(neighbours):
        out_ret[j] = force_ref[owned + j * slots : owned + (j + 1) * slots, :]
    greet(owners + groups + [sibling] + along_x + along_z)
    copies = [
        send(out_ret.at[j], in_ret.at[j], ret_sem.at[0, j], ret_sem.at[1, j], owners[j])
        for j in range(neighbours)
    ]
    hits = pair_hits(map_ref, owned).astype(BF16)
    load_int = jnp.transpose(load_int_ref[...])
    strip = 384
    for c in range(sinv.shape[0] // strip):
        sinv[c * strip : (c + 1) * strip, :] = jnp.transpose(sinv_t[:, c * strip : (c + 1) * strip])
    for copy in copies:
        copy.wait()
    back = jnp.concatenate([in_ret[j] for j in range(neighbours)], axis=0)
    high = back.astype(BF16)
    low = (back - high.astype(F32)).astype(BF16)
    force = force_ref[0:owned, :] + dot(hits, high) + dot(hits, low)
    share = out_grp.shape[1]
    pieces = jnp.concatenate(
        [force[int_nodes:], jnp.zeros((grps * share - if_nodes, width), F32)], axis=0
    )
    for q in range(grps):
        out_grp[q] = pieces[q * share : (q + 1) * share]
    copies = [
        send(out_grp.at[peer["grp"]], in_grp.at[s], grp_sem.at[0, s], grp_sem.at[1, s], peer)
        for s, peer in enumerate(groups)
    ]
    r_int = load_int - force[:int_nodes]
    for i in range(3):
        spread[pl.ds(i, int_nodes, stride=3), :] = r_int[:, i * fourier : (i + 1) * fourier]
    rhs_int[...] = spread[...].astype(BF16)
    chunk = 256
    chunks = kinv.shape[0] // chunk

    def solve(c, _):
        rows = pl.ds(pl.multiple_of(c * chunk, chunk), chunk)
        spread[rows, :] = dot(kinv[rows, :], rhs_int[...])
        return 0

    lax.fori_loop(0, chunks // 2, solve, 0)
    loads = jnp.concatenate(
        [load_if_ref[...], jnp.zeros((grps * share - if_nodes, width), F32)], axis=0
    )
    mine = loads[0:share]
    for q in range(1, grps):
        mine = jnp.where(my_grp == q, loads[q * share : (q + 1) * share], mine)
    total = out_grp[my_grp]
    for s, copy in enumerate(copies):
        copy.wait()
        total = total + in_grp[s]
    out_rhs[...] = (mine - total).astype(BF16)
    copies = [
        send(out_rhs, all_rhs.at[my_grp], rhs_sem.at[0, s], rhs_sem.at[1, s], peer)
        for s, peer in enumerate(groups)
    ]
    all_rhs[my_grp] = out_rhs[...]
    lax.fori_loop(chunks // 2, chunks, solve, 0)
    for copy in copies:
        copy.wait()
    gathered = jnp.concatenate([all_rhs[q].astype(F32) for q in range(grps)], axis=0)[:if_nodes]
    for i in range(3):
        spread_if[pl.ds(i, if_nodes, stride=3), :] = gathered[:, i * fourier : (i + 1) * fourier]
    rhs_if = spread_if[...]
    empty = jnp.zeros_like(rhs_if)
    left = jnp.concatenate([rhs_if, empty], axis=1).astype(BF16)
    right = jnp.concatenate([empty, rhs_if], axis=1).astype(BF16)
    half = zs // 2
    per_owner = sinv.shape[0] // dom
    per_z = per_owner * xs * cores
    for q in range(half):
        flat[q * per_z : (q + 1) * per_z, :] = dot(
            sinv[q * per_z : (q + 1) * per_z, :], left
        ) + dot(sinv[(half + q) * per_z : (half + q + 1) * per_z, :], right)
    fill = jnp.zeros((out1.shape[1] - half * per_owner, 2 * fourier), F32)
    for k in range(xs):
        by_core = []
        for c in range(cores):
            rows = [
                flat[q * per_z + (k * cores + c) * per_owner : q * per_z + (k * cores + c + 1) * per_owner, :]
                for q in range(half)
            ]
            by_core.append(jnp.concatenate(rows + [fill], axis=0))
        own1[k] = jnp.where(core == 0, by_core[0], by_core[1])
        out1[k] = jnp.where(core == 0, by_core[1], by_core[0]).astype(BF16)
    copy = send(out1, in1, sem1.at[0], sem1.at[1], sibling)
    for i in range(3):
        du_int_ref[i * fourier : (i + 1) * fourier, :] = jnp.transpose(
            spread[pl.ds(i, int_nodes, stride=3), :]
        )
    copy.wait()
    for k in range(xs):
        summed = own1[k] + in1[k].astype(F32)
        own1[k] = summed
        out2[k] = summed.astype(BF16)
    copies = [
        send(out2.at[lax.rem(x + s + 1, xs)], in2.at[s], sem2.at[0, s], sem2.at[1, s], peer)
        for s, peer in enumerate(along_x)
    ]
    summed = own1[x]
    for s, copy in enumerate(copies):
        copy.wait()
        summed = summed + in2[s].astype(F32)
    turned = pltpu.roll(summed, fourier, 1)
    short = per_owner // 2
    first = lax.broadcasted_iota(jnp.int32, (short, 2 * fourier), 1) < fourier
    fill = jnp.zeros((out3.shape[1] - short, 2 * fourier), F32)
    for q in range(half):
        top = slice(q * per_owner, q * per_owner + short)
        low_rows = slice(q * per_owner + short, (q + 1) * per_owner)
        for h, (a, b) in enumerate(((summed, turned), (turned, summed))):
            block = jnp.concatenate([jnp.where(first, a[top], b[low_rows]), fill], axis=0)
            own3[h * half + q] = block
            out3[h * half + q] = block.astype(BF16)
    copies = [
        send(out3.at[lax.rem(z + s + 1, zs)], in3.at[s], sem3.at[0, s], sem3.at[1, s], peer)
        for s, peer in enumerate(along_z)
    ]
    summed = own3[z]
    for s, copy in enumerate(copies):
        copy.wait()
        summed = summed + in3[s].astype(F32)
    last[0] = summed
    last[1] = pltpu.roll(summed, fourier, 1)
    nodes = short // 3
    for h in range(2):
        for i in range(3):
            du_if_ref[h * nodes : (h + 1) * nodes, i * fourier : (i + 1) * fourier] = last[
                h, pl.ds(i, nodes, stride=3), :
            ][:, :fourier]


def finish(force, send_map, load_int_t, load_if, kinv_int, sinv_t, offsets, sizes, stop=99):
    zs, xs, cores, grps = sizes
    neighbours, slots = send_map.shape
    width, int_nodes = load_int_t.shape
    sinv_rows = sinv_t.shape[1]
    if_nodes = load_if.shape[0]
    fourier = width // 3
    dom = zs * xs * cores
    per_owner = sinv_rows // dom
    up = lambda n, k: -(-n // k) * k
    share = up(-(-if_nodes // grps), 8)
    rows1 = up(per_owner * (zs // 2), 16)
    rows3 = up(per_owner // 2, 16)
    vmem = pl.BlockSpec(memory_space=pltpu.VMEM)
    sems = pltpu.SemaphoreType.DMA
    lanes = 2 * fourier
    return pl.pallas_call(
        functools.partial(finish_kernel, sizes, offsets, stop),
        out_shape=(
            jax.ShapeDtypeStruct((width, int_nodes), F32),
            jax.ShapeDtypeStruct((per_owner // 3, width), F32),
        ),
        in_specs=[vmem] * 6,
        out_specs=(vmem, vmem),
        scratch_shapes=[
            pltpu.VMEM((sinv_rows, sinv_t.shape[0]), BF16),
            pltpu.VMEM((neighbours, slots, width), F32),
            pltpu.VMEM((neighbours, slots, width), F32),
            pltpu.VMEM((3 * int_nodes, fourier), F32),
            pltpu.VMEM((3 * if_nodes, fourier), F32),
            pltpu.VMEM((3 * int_nodes, fourier), BF16),
            pltpu.VMEM((grps, share, width), F32),
            pltpu.VMEM((grps - 1, share, width), F32),
            pltpu.VMEM((share, width), BF16),
            pltpu.VMEM((grps, share, width), BF16),
            pltpu.VMEM((sinv_rows // 2, lanes), F32),
            pltpu.VMEM((xs, rows1, lanes), F32),
            pltpu.VMEM((xs, rows1, lanes), BF16),
            pltpu.VMEM((xs, rows1, lanes), BF16),
            pltpu.VMEM((xs, rows1, lanes), BF16),
            pltpu.VMEM((xs - 1, rows1, lanes), BF16),
            pltpu.VMEM((zs, rows3, lanes), F32),
            pltpu.VMEM((zs, rows3, lanes), BF16),
            pltpu.VMEM((zs - 1, rows3, lanes), BF16),
            pltpu.VMEM((2, rows3, lanes), F32),
            sems((2, neighbours)), sems((2, grps - 1)), sems((2, grps - 1)),
            sems((2,)), sems((2, xs - 1)), sems((2, zs - 1)),
        ],
        compiler_params=pltpu.CompilerParams(
            collective_id=1, has_side_effects=True, vmem_limit_bytes=20 * 1024 * 1024
        ),
        cost_estimate=pl.CostEstimate(flops=20000000000, bytes_accessed=9000000, transcendentals=0),
        name="finish",
    )(force, send_map, load_int_t, load_if, kinv_int, sinv_t)


def per_device(
    u_int, u_if, load_int, load_if, conn, send_map, counts, elem_size, stiffness,
    yield_stress, relax_rate, stress_init, kinv_int, sinv,
):
    reach = send_map.shape[0] // 2
    offsets = list(range(-reach, 0)) + list(range(1, reach + 1))
    dom, grps = lax.axis_size("dom"), lax.axis_size("grp")
    sizes = (dom // 8, 4, 2, grps)
    u_int_t, conn_t = jnp.transpose(u_int), jnp.transpose(conn)
    tail = halo(u_int_t, u_if, send_map, offsets, dom)
    params = [v.reshape(1, -1) for v in (elem_size, stiffness, yield_stress, relax_rate)]
    stress_end, force = element_update(u_int_t, tail, conn_t, counts, params, stress_init)
    du_int_t, du_if = finish(
        force, send_map, jnp.transpose(load_int), load_if, kinv_int, jnp.transpose(sinv), offsets, sizes
    )
    return (jnp.transpose(du_int_t), du_if, stress_end)


def solution(mesh):
    both = ("grp", "dom")
    return jax.shard_map(
        per_device,
        mesh=mesh,
        in_specs=(
            P(both, None), P("dom", None), P(both, None), P("dom", None), P(both, None),
            P(both, None), P(both), P(both), P(both), P(both), P(both), P(None, both),
            P(both, None), P("grp", "dom"),
        ),
        out_specs=(P(both, None), P(both, None), P(None, both)),
        check_vma=False,
    )
```

```python
import functools
import math

import jax
import jax.numpy as jnp
import numpy as np
from jax import lax
from jax.experimental import pallas as pl
from jax.experimental.pallas import tpu as pltpu
from jax.sharding import PartitionSpec as P

TIMES = 32
GROUP = 8
POISSON = 0.3
BF16 = jnp.bfloat16
F32 = jnp.float32


def strain_table():
    gauss = 1.0 / math.sqrt(3.0)
    table = np.zeros((6, 8, 8, 3))
    for point in range(8):
        coords = [((point >> bit & 1) * 2 - 1) * gauss for bit in range(3)]
        for corner in range(8):
            signs = [(corner >> bit & 1) * 2 - 1 for bit in range(3)]
            deriv = []
            for axis in range(3):
                value = signs[axis] / 8.0
                for other in range(3):
                    if other != axis:
                        value = value * (1.0 + signs[other] * coords[other])
                deriv.append(value)
            table[0, point, corner, 0] = deriv[0]
            table[1, point, corner, 1] = deriv[1]
            table[2, point, corner, 2] = deriv[2]
            table[3, point, corner, 0] = deriv[1]
            table[3, point, corner, 1] = deriv[0]
            table[4, point, corner, 1] = deriv[2]
            table[4, point, corner, 2] = deriv[1]
            table[5, point, corner, 2] = deriv[0]
            table[5, point, corner, 0] = deriv[2]
    return np.asarray(np.asarray(table.reshape(48, 24), np.float32), BF16).astype(np.float64)


def time_tables(times, fourier):
    theta = 2.0 * math.pi * (np.arange(times) + 0.3) / times
    synthesis = np.zeros((fourier, times))
    for column in range(fourier):
        harmonic = column // 2
        if column % 2 == 0:
            synthesis[column] = np.cos(harmonic * theta)
        else:
            synthesis[column] = np.sin((harmonic + 1) * theta)
    analysis = synthesis.T * (2.0 / times)
    analysis[:, 0] = 1.0 / times
    return synthesis.astype(np.float32).astype(np.float64), analysis.astype(np.float32).astype(np.float64)


def two_parts(x):
    high = np.asarray(x, np.float32).astype(BF16)
    low = (np.asarray(x, np.float64) - high.astype(np.float64)).astype(BF16)
    return jnp.asarray(high), jnp.asarray(low)


@functools.lru_cache(None)
def host_tables(fourier):
    table = strain_table()
    synthesis, analysis = time_tables(TIMES, fourier)
    groups = TIMES // GROUP
    steps = synthesis - np.roll(synthesis, 1, axis=1)
    synth = np.zeros((groups, 3, GROUP, 3, fourier))
    analyse = np.zeros((groups, 3, 2, GROUP, 3, fourier))
    for g in range(groups):
        for i in range(3):
            for m in range(GROUP):
                synth[g, i, m, i] = steps[:, g * GROUP + m]
                analyse[g, i, :, m, i] = analysis[g * GROUP + m]
    strain = np.zeros((GROUP, 48, 8, 3, 2, GROUP))
    force = np.zeros((8, 3, GROUP, GROUP, 48))
    shaped = table.reshape(48, 8, 3)
    for m in range(GROUP):
        for part in range(2):
            strain[m, :, :, :, part, m] = shaped
        force[:, :, m, m, :] = np.transpose(shaped, (1, 2, 0))
    width = 3 * fourier
    return (
        synth.reshape(TIMES * 3, width),
        analyse.reshape(TIMES * 6, width),
        strain.reshape(GROUP * 48, GROUP * 48),
        force.reshape(GROUP * 24, GROUP * 48),
    )


def split_rows(x):
    rows, n = x.shape
    high = x.astype(BF16).astype(F32)
    low = x - high
    parts = jnp.concatenate(
        [high.reshape(rows // 8, 1, 8, n), low.reshape(rows // 8, 1, 8, n)], axis=1
    )
    return parts.reshape(rows * 2, n).astype(BF16)


def dot(a, b):
    return lax.dot_general(a, b, (((1,), (0,)), ((), ())), preferred_element_type=F32)


def dot_t(a, b):
    return lax.dot_general(a, b, (((1,), (1,)), ((), ())), preferred_element_type=F32)


LAME = POISSON / ((1.0 + POISSON) * (1.0 - 2.0 * POISSON))
SHEAR = 1.0 / (2.0 * (1.0 + POISSON))


def element_kernel(
    counts_ref, int_ref, tail_ref, conn_ref, size_ref, stiff_ref, yield_ref, rate_ref, stress_ref,
    synth_hi_ref, synth_lo_ref, an_hi_ref, an_lo_ref, strain_ref, force_ref,
    stress_out, force_out,
    nodal, onehot, gathered, stresses, forces, total,
):
    step = pl.program_id(0)
    block = conn_ref.shape[1]
    nodes = nodal.shape[1]
    groups = TIMES // GROUP

    @pl.when(step == 0)
    def _():
        inner, tail = int_ref[...], tail_ref[...]
        first = inner.shape[1]
        high, low = synth_hi_ref[...], synth_lo_ref[...]
        nodal[:, :first] = split_rows(dot(high, inner) + dot(low, inner))
        nodal[:, first:] = split_rows(dot_t(high, tail) + dot_t(low, tail))
        total[...] = jnp.zeros_like(total)

    iota = lax.broadcasted_iota(jnp.int16, (nodes, block), 0)
    for a in range(8):
        index = conn_ref[a : a + 1, :].astype(jnp.int16)
        hit = iota == jnp.broadcast_to(index, (nodes, block))
        onehot[:, a * block : (a + 1) * block] = jnp.where(
            hit, jnp.ones((), BF16), jnp.zeros((), BF16)
        )
    table = nodal[...]
    chosen = dot(table, onehot[...]).astype(BF16)
    for a in range(8):
        picked = chosen[:, a * block : (a + 1) * block]
        for g in range(groups):
            gathered[g, a * 48 : (a + 1) * 48, :] = picked[g * 48 : (g + 1) * 48, :]

    size = size_ref[...]
    stiff = stiff_ref[...]
    yields = yield_ref[...]
    rate8 = jnp.broadcast_to(rate_ref[...], (8, block))
    inverse = 1.0 / yields
    weight = stiff * (2.0 / size) * inverse
    shear8 = jnp.broadcast_to(weight * SHEAR, (8, block))
    shear28 = shear8 * 2.0
    lame8 = jnp.broadcast_to(weight * LAME, (8, block))
    slot = lax.broadcasted_iota(jnp.int32, (1, block), 1) + step * block
    live = (slot < counts_ref[0]).astype(F32)
    scale = size * size * 0.25 * live * yields
    state = [stress_ref[c * 8 : (c + 1) * 8, :] * inverse for c in range(6)]
    deltas = [dot(strain_ref[...], gathered[g]) for g in range(groups)]
    for g in range(groups):
        delta = deltas[g]
        for m in range(GROUP):
            d = [delta[m * 48 + c * 8 : m * 48 + c * 8 + 8, :] for c in range(6)]
            volume = (d[0] + d[1] + d[2]) * lame8
            for c in range(6):
                rise = d[c] * shear28 + volume if c < 3 else d[c] * shear8
                state[c] = state[c] + rise - rate8 * jnp.tanh(state[c])
            stresses[g, m * 48 : (m + 1) * 48, :] = jnp.concatenate(state, axis=0).astype(BF16)
        pushed = dot(force_ref[...], stresses[g]) * scale
        for a in range(8):
            forces[g * 48 : (g + 1) * 48, a * block : (a + 1) * block] = split_rows(
                pushed[a * 24 : (a + 1) * 24, :]
            )
    stress_out[...] = jnp.concatenate(state, axis=0) * (yields * live)
    total[...] += dot_t(onehot[0 : total.shape[0], :], forces[...])

    @pl.when(step == pl.num_programs(0) - 1)
    def _():
        summed = total[...]
        high = summed.astype(BF16)
        low = (summed - high.astype(F32)).astype(BF16)
        force_out[...] = (
            dot(high, an_hi_ref[...]) + dot(high, an_lo_ref[...]) + dot(low, an_hi_ref[...])
        )


def element_update(inner, tail, conn_t, count, params, stress_zero, used=736, block=512):
    elems = conn_t.shape[1]
    width = inner.shape[0]
    padded = inner.shape[1] + tail.shape[0]
    synth, analyse, strain, force = host_tables(width // 3)
    synth_hi, synth_lo = two_parts(synth)
    an_hi, an_lo = two_parts(analyse)
    strain = jnp.asarray(strain, BF16)
    force = jnp.asarray(force, BF16)
    whole = lambda x: pl.BlockSpec(x.shape, lambda s: (0,) * x.ndim)
    by_block = lambda r: pl.BlockSpec((r, block), lambda s: (0, s))
    return pl.pallas_call(
        element_kernel,
        grid=(elems // block,),
        out_shape=(
            jax.ShapeDtypeStruct(stress_zero.shape, F32),
            jax.ShapeDtypeStruct((used, width), F32),
        ),
        in_specs=[
            pl.BlockSpec(memory_space=pltpu.SMEM),
            whole(inner), whole(tail), by_block(8), by_block(1), by_block(1), by_block(1), by_block(1), by_block(48),
            whole(synth_hi), whole(synth_lo), whole(an_hi), whole(an_lo),
            whole(strain), whole(force),
        ],
        out_specs=(by_block(48), pl.BlockSpec((used, width), lambda s: (0, 0))),
        scratch_shapes=[
            pltpu.VMEM((6 * TIMES, padded), BF16),
            pltpu.VMEM((padded, 8 * block), BF16),
            pltpu.VMEM((TIMES // GROUP, GROUP * 48, block), BF16),
            pltpu.VMEM((TIMES // GROUP, GROUP * 48, block), BF16),
            pltpu.VMEM((6 * TIMES, 8 * block), BF16),
            pltpu.VMEM((used, 6 * TIMES), F32),
        ],
        compiler_params=pltpu.CompilerParams(
            vmem_limit_bytes=28 * 1024 * 1024, dimension_semantics=("arbitrary",)
        ),
        cost_estimate=pl.CostEstimate(flops=25000000000, bytes_accessed=4000000, transcendentals=0),
        name="elements",
    )(count, inner, tail, conn_t, *params, stress_zero, synth_hi, synth_lo, an_hi, an_lo, strain, force)


MESH = pl.DeviceIdType.MESH


def pair_hits(map_ref, rows):
    neighbours, slots = map_ref.shape
    listed = jnp.concatenate([map_ref[j : j + 1, :] for j in range(neighbours)], axis=1)
    iota = lax.broadcasted_iota(jnp.int32, (rows, neighbours * slots), 0)
    return (iota == listed).astype(F32)


def greet(peers):
    barrier = pltpu.get_barrier_semaphore()
    for peer in peers:
        pl.semaphore_signal(barrier, inc=1, device_id=peer, device_id_type=MESH)
    pl.semaphore_wait(barrier, len(peers))


def send(src, dst, send_sem, recv_sem, peer):
    copy = pltpu.make_async_remote_copy(
        src_ref=src, dst_ref=dst, send_sem=send_sem, recv_sem=recv_sem,
        device_id=peer, device_id_type=MESH,
    )
    copy.start()
    return copy


def halo_kernel(dom, offsets, int_ref, if_ref, map_ref, tail_out, out_block, in_block, send_sem, recv_sem):
    me = lax.axis_index("dom")
    near = [{"dom": lax.rem(me + off + dom, dom)} for off in offsets]
    width, int_nodes = int_ref.shape
    if_nodes = if_ref.shape[0]
    slots = map_ref.shape[1]
    hits = jnp.transpose(pair_hits(map_ref, int_nodes + if_nodes)).astype(BF16)
    picked = (
        dot_t(hits[:, :int_nodes], int_ref[...]) + dot(hits[:, int_nodes:], if_ref[...])
    ).astype(BF16)
    for j in range(len(offsets)):
        out_block[j] = picked[j * slots : (j + 1) * slots]
    greet(near)
    copies = [
        send(out_block.at[j], in_block.at[j], send_sem.at[j], recv_sem.at[j], near[j])
        for j in range(len(offsets))
    ]
    for copy in copies:
        copy.wait()
    parts = [if_ref[...].astype(F32)] + [in_block[j].astype(F32) for j in range(len(offsets))]
    fill = tail_out.shape[0] - if_nodes - len(offsets) * slots
    tail_out[...] = jnp.concatenate(parts + [jnp.zeros((fill, width), F32)], axis=0).astype(BF16)


def halo(u_int_t, u_if, send_map, offsets, dom):
    neighbours, slots = send_map.shape
    width, int_nodes = u_int_t.shape
    used = int_nodes + u_if.shape[0] + neighbours * slots
    padded = -(-used // 256) * 256
    vmem = pl.BlockSpec(memory_space=pltpu.VMEM)
    return pl.pallas_call(
        functools.partial(halo_kernel, dom, offsets),
        out_shape=jax.ShapeDtypeStruct((padded - int_nodes, width), BF16),
        in_specs=[vmem] * 3,
        out_specs=vmem,
        scratch_shapes=[
            pltpu.VMEM((neighbours, slots, width), BF16),
            pltpu.VMEM((neighbours, slots, width), BF16),
            pltpu.SemaphoreType.DMA((neighbours,)),
            pltpu.SemaphoreType.DMA((neighbours,)),
        ],
        compiler_params=pltpu.CompilerParams(
            collective_id=0, has_side_effects=True, vmem_limit_bytes=12 * 1024 * 1024
        ),
        cost_estimate=pl.CostEstimate(flops=6000000000, bytes_accessed=1000000, transcendentals=0),
        name="halo",
    )(u_int_t, u_if, send_map)


def finish_kernel(
    sizes, offsets, stop,
    force_ref, map_ref, load_int_ref, load_if_ref, kinv, sinv_t,
    du_int_ref, du_if_ref,
    sinv, out_ret, in_ret, spread, spread_if, rhs_int,
    out_grp, in_grp, out_rhs, all_rhs, flat,
    own1, out1, in1, out2, in2, own3, out3, in3, last,
    ret_sem, grp_sem, rhs_sem, sem1, sem2, sem3,
):
    zs, xs, cores, grps = sizes
    started = []

    def launch(*where):
        started.append(send(*where))
        return started[-1]

    dom = zs * xs * cores
    me = lax.axis_index("dom")
    my_grp = lax.axis_index("grp")
    core = lax.rem(me, cores)
    x = lax.rem(me // cores, xs)
    z = me // (cores * xs)
    at = lambda zz, xx, cc: {"dom": (zz * xs + xx) * cores + cc}
    owners = [{"dom": lax.rem(me - off + dom, dom)} for off in offsets]
    groups = [{"grp": lax.rem(my_grp + s, grps)} for s in range(1, grps)]
    sibling = at(z, x, 1 - core)
    along_x = [at(z, lax.rem(x + s, xs), core) for s in range(1, xs)]
    along_z = [at(lax.rem(z + s, zs), x, core) for s in range(1, zs)]
    neighbours, slots = map_ref.shape
    width, int_nodes = load_int_ref.shape
    if_nodes = load_if_ref.shape[0]
    fourier = width // 3
    owned = int_nodes + if_nodes
    for j in range(neighbours):
        out_ret[j] = force_ref[owned + j * slots : owned + (j + 1) * slots, :]
    greet(owners + groups + [sibling] + along_x + along_z)
    copies = [
        launch(out_ret.at[j], in_ret.at[j], ret_sem.at[0, j], ret_sem.at[1, j], owners[j])
        for j in range(neighbours)
    ]
    hits = pair_hits(map_ref, owned).astype(BF16)
    load_int = jnp.transpose(load_int_ref[...])
    strip = 384
    for c in range(sinv.shape[0] // strip):
        sinv[c * strip : (c + 1) * strip, :] = jnp.transpose(sinv_t[:, c * strip : (c + 1) * strip])
    for copy in copies:
        copy.wait_recv()
    back = jnp.concatenate([in_ret[j] for j in range(neighbours)], axis=0)
    high = back.astype(BF16)
    low = (back - high.astype(F32)).astype(BF16)
    force = force_ref[0:owned, :] + dot(hits, high) + dot(hits, low)
    share = out_grp.shape[1]
    pieces = jnp.concatenate(
        [force[int_nodes:], jnp.zeros((grps * share - if_nodes, width), F32)], axis=0
    )
    for q in range(grps):
        out_grp[q] = pieces[q * share : (q + 1) * share]
    copies = [
        launch(out_grp.at[peer["grp"]], in_grp.at[s], grp_sem.at[0, s], grp_sem.at[1, s], peer)
        for s, peer in enumerate(groups)
    ]
    r_int = load_int - force[:int_nodes]
    for i in range(3):
        spread[pl.ds(i, int_nodes, stride=3), :] = r_int[:, i * fourier : (i + 1) * fourier]
    rhs_int[...] = spread[...].astype(BF16)
    chunk = 256
    chunks = kinv.shape[0] // chunk

    def solve(c, _):
        rows = pl.ds(pl.multiple_of(c * chunk, chunk), chunk)
        spread[rows, :] = dot(kinv[rows, :], rhs_int[...])
        return 0

    lax.fori_loop(0, 2, solve, 0)
    loads = jnp.concatenate(
        [load_if_ref[...], jnp.zeros((grps * share - if_nodes, width), F32)], axis=0
    )
    mine = loads[0:share]
    for q in range(1, grps):
        mine = jnp.where(my_grp == q, loads[q * share : (q + 1) * share], mine)
    total = out_grp[my_grp]
    for s, copy in enumerate(copies):
        copy.wait_recv()
        total = total + in_grp[s]
    out_rhs[...] = (mine - total).astype(BF16)
    copies = [
        launch(out_rhs, all_rhs.at[my_grp], rhs_sem.at[0, s], rhs_sem.at[1, s], peer)
        for s, peer in enumerate(groups)
    ]
    all_rhs[my_grp] = out_rhs[...]
    lax.fori_loop(2, 3, solve, 0)
    for copy in copies:
        copy.wait_recv()
    gathered = jnp.concatenate([all_rhs[q].astype(F32) for q in range(grps)], axis=0)[:if_nodes]
    for i in range(3):
        spread_if[pl.ds(i, if_nodes, stride=3), :] = gathered[:, i * fourier : (i + 1) * fourier]
    rhs_if = spread_if[...]
    empty = jnp.zeros_like(rhs_if)
    left = jnp.concatenate([rhs_if, empty], axis=1).astype(BF16)
    right = jnp.concatenate([empty, rhs_if], axis=1).astype(BF16)
    half = zs // 2
    parts = out1.shape[0]
    each = half // parts
    per_owner = sinv.shape[0] // dom
    per_z = per_owner * xs * cores
    fill = jnp.zeros((out1.shape[2] - each * per_owner, 2 * fourier), F32)
    first_copies = []
    for c in range(parts):
        for j in range(each):
            start = pl.multiple_of(lax.rem(z + c * each + j + 1, half) * per_z, 16)
            other = pl.multiple_of(start + half * per_z, 16)
            flat[(c * each + j) * per_z : (c * each + j + 1) * per_z, :] = dot(
                sinv[pl.ds(start, per_z), :], left
            ) + dot(sinv[pl.ds(other, per_z), :], right)
        for k in range(xs):
            by_core = []
            for cc in range(cores):
                rows = []
                for j in range(each):
                    at_row = (c * each + j) * per_z + (k * cores + cc) * per_owner
                    rows.append(flat[at_row : at_row + per_owner, :])
                by_core.append(jnp.concatenate(rows + [fill], axis=0))
            own1[c, k] = jnp.where(core == 0, by_core[0], by_core[1])
            out1[c, k] = jnp.where(core == 0, by_core[1], by_core[0]).astype(BF16)
        first_copies.append(launch(out1.at[c], in1.at[c], sem1.at[0, c], sem1.at[1, c], sibling))
    second_copies = []
    for c in range(parts):
        first_copies[c].wait_recv()
        for k in range(xs):
            summed = own1[c, k] + in1[c, k].astype(F32)
            own1[c, k] = summed
            out2[c, k] = summed.astype(BF16)
        second_copies.append([
            launch(out2.at[c, lax.rem(x + s + 1, xs)], in2.at[c, s], sem2.at[0, c, s], sem2.at[1, c, s], peer)
            for s, peer in enumerate(along_x)
        ])
    lax.fori_loop(3, chunks, solve, 0)
    short = per_owner // 2
    first = lax.broadcasted_iota(jnp.int32, (short, 2 * fourier), 1) < fourier
    fill = jnp.zeros((out3.shape[3] - short, 2 * fourier), F32)
    third_copies = []
    for c in range(parts):
        summed = own1[c, x]
        for s, copy in enumerate(second_copies[c]):
            copy.wait_recv()
            summed = summed + in2[c, s].astype(F32)
        turned = pltpu.roll(summed, fourier, 1)
        for j in range(each):
            top = slice(j * per_owner, j * per_owner + short)
            low_rows = slice(j * per_owner + short, (j + 1) * per_owner)
            o = c * each + j + 1
            for h, (a, b) in enumerate(((summed, turned), (turned, summed))):
                block = jnp.concatenate([jnp.where(first, a[top], b[low_rows]), fill], axis=0)
                if o == half:
                    own3[h] = block
                out3[c, j, h] = block.astype(BF16)
            for s in (o, o + half):
                if s < zs:
                    target = lax.rem(z + s, zs)
                    third_copies.append(launch(
                        out3.at[c, j, target // half], in3.at[s - 1],
                        sem3.at[0, s - 1], sem3.at[1, s - 1], along_z[s - 1],
                    ))
    for i in range(3):
        du_int_ref[i * fourier : (i + 1) * fourier, :] = jnp.transpose(
            spread[pl.ds(i, int_nodes, stride=3), :]
        )
    for copy in third_copies:
        copy.wait_recv()
    summed = own3[z // half]
    for s in range(zs - 1):
        summed = summed + in3[s].astype(F32)
    last[0] = summed
    last[1] = pltpu.roll(summed, fourier, 1)
    nodes = short // 3
    for h in range(2):
        for i in range(3):
            du_if_ref[h * nodes : (h + 1) * nodes, i * fourier : (i + 1) * fourier] = last[
                h, pl.ds(i, nodes, stride=3), :
            ][:, :fourier]
    for copy in started:
        copy.wait_send()


def finish(force, send_map, load_int_t, load_if, kinv_int, sinv_t, offsets, sizes, stop=99):
    zs, xs, cores, grps = sizes
    neighbours, slots = send_map.shape
    width, int_nodes = load_int_t.shape
    sinv_rows = sinv_t.shape[1]
    if_nodes = load_if.shape[0]
    fourier = width // 3
    dom = zs * xs * cores
    per_owner = sinv_rows // dom
    up = lambda n, k: -(-n // k) * k
    share = up(-(-if_nodes // grps), 8)
    parts = 2
    each = zs // 2 // parts
    rows1 = up(per_owner * each, 16)
    rows3 = up(per_owner // 2, 16)
    vmem = pl.BlockSpec(memory_space=pltpu.VMEM)
    sems = pltpu.SemaphoreType.DMA
    lanes = 2 * fourier
    return pl.pallas_call(
        functools.partial(finish_kernel, sizes, offsets, stop),
        out_shape=(
            jax.ShapeDtypeStruct((width, int_nodes), F32),
            jax.ShapeDtypeStruct((per_owner // 3, width), F32),
        ),
        in_specs=[vmem] * 6,
        out_specs=(vmem, vmem),
        scratch_shapes=[
            pltpu.VMEM((sinv_rows, sinv_t.shape[0]), BF16),
            pltpu.VMEM((neighbours, slots, width), F32),
            pltpu.VMEM((neighbours, slots, width), F32),
            pltpu.VMEM((3 * int_nodes, fourier), F32),
            pltpu.VMEM((3 * if_nodes, fourier), F32),
            pltpu.VMEM((3 * int_nodes, fourier), BF16),
            pltpu.VMEM((grps, share, width), F32),
            pltpu.VMEM((grps - 1, share, width), F32),
            pltpu.VMEM((share, width), BF16),
            pltpu.VMEM((grps, share, width), BF16),
            pltpu.VMEM((sinv_rows // 2, lanes), F32),
            pltpu.VMEM((parts, xs, rows1, lanes), F32),
            pltpu.VMEM((parts, xs, rows1, lanes), BF16),
            pltpu.VMEM((parts, xs, rows1, lanes), BF16),
            pltpu.VMEM((parts, xs, rows1, lanes), BF16),
            pltpu.VMEM((parts, xs - 1, rows1, lanes), BF16),
            pltpu.VMEM((2, rows3, lanes), F32),
            pltpu.VMEM((parts, each, 2, rows3, lanes), BF16),
            pltpu.VMEM((zs - 1, rows3, lanes), BF16),
            pltpu.VMEM((2, rows3, lanes), F32),
            sems((2, neighbours)), sems((2, grps - 1)), sems((2, grps - 1)),
            sems((2, parts)), sems((2, parts, xs - 1)), sems((2, zs - 1)),
        ],
        compiler_params=pltpu.CompilerParams(
            collective_id=1, has_side_effects=True, vmem_limit_bytes=20 * 1024 * 1024
        ),
        cost_estimate=pl.CostEstimate(flops=20000000000, bytes_accessed=9000000, transcendentals=0),
        name="finish",
    )(force, send_map, load_int_t, load_if, kinv_int, sinv_t)


def per_device(
    u_int, u_if, load_int, load_if, conn, send_map, counts, elem_size, stiffness,
    yield_stress, relax_rate, stress_init, kinv_int, sinv,
):
    reach = send_map.shape[0] // 2
    offsets = list(range(-reach, 0)) + list(range(1, reach + 1))
    dom, grps = lax.axis_size("dom"), lax.axis_size("grp")
    sizes = (dom // 8, 4, 2, grps)
    u_int_t, conn_t = jnp.transpose(u_int), jnp.transpose(conn)
    tail = halo(u_int_t, u_if, send_map, offsets, dom)
    params = [v.reshape(1, -1) for v in (elem_size, stiffness, yield_stress, relax_rate)]
    buffer_rows = u_int.shape[0] + u_if.shape[0] + send_map.size
    used = -(-buffer_rows // 16) * 16
    stress_end, force = element_update(u_int_t, tail, conn_t, counts, params, stress_init, used)
    du_int_t, du_if = finish(
        force, send_map, jnp.transpose(load_int), load_if, kinv_int, jnp.transpose(sinv), offsets, sizes
    )
    return (jnp.transpose(du_int_t), du_if, stress_end)


def solution(mesh):
    both = ("grp", "dom")
    return jax.shard_map(
        per_device,
        mesh=mesh,
        in_specs=(
            P(both, None), P("dom", None), P(both, None), P("dom", None), P(both, None),
            P(both, None), P(both), P(both), P(both), P(both), P(both), P(None, both),
            P(both, None), P("grp", "dom"),
        ),
        out_specs=(P(both, None), P(both, None), P(None, both)),
        check_vma=False,
    )
```

```python
import functools
import math

import jax
import jax.numpy as jnp
import numpy as np
from jax import lax
from jax.experimental import pallas as pl
from jax.experimental.pallas import tpu as pltpu
from jax.sharding import PartitionSpec as P

TIMES = 32
GROUP = 8
POISSON = 0.3
BF16 = jnp.bfloat16
F32 = jnp.float32


def strain_table():
    gauss = 1.0 / math.sqrt(3.0)
    table = np.zeros((6, 8, 8, 3))
    for point in range(8):
        coords = [((point >> bit & 1) * 2 - 1) * gauss for bit in range(3)]
        for corner in range(8):
            signs = [(corner >> bit & 1) * 2 - 1 for bit in range(3)]
            deriv = []
            for axis in range(3):
                value = signs[axis] / 8.0
                for other in range(3):
                    if other != axis:
                        value = value * (1.0 + signs[other] * coords[other])
                deriv.append(value)
            table[0, point, corner, 0] = deriv[0]
            table[1, point, corner, 1] = deriv[1]
            table[2, point, corner, 2] = deriv[2]
            table[3, point, corner, 0] = deriv[1]
            table[3, point, corner, 1] = deriv[0]
            table[4, point, corner, 1] = deriv[2]
            table[4, point, corner, 2] = deriv[1]
            table[5, point, corner, 2] = deriv[0]
            table[5, point, corner, 0] = deriv[2]
    return np.asarray(np.asarray(table.reshape(48, 24), np.float32), BF16).astype(np.float64)


def time_tables(times, fourier):
    theta = 2.0 * math.pi * (np.arange(times) + 0.3) / times
    synthesis = np.zeros((fourier, times))
    for column in range(fourier):
        harmonic = column // 2
        if column % 2 == 0:
            synthesis[column] = np.cos(harmonic * theta)
        else:
            synthesis[column] = np.sin((harmonic + 1) * theta)
    analysis = synthesis.T * (2.0 / times)
    analysis[:, 0] = 1.0 / times
    return synthesis.astype(np.float32).astype(np.float64), analysis.astype(np.float32).astype(np.float64)


def two_parts(x):
    high = np.asarray(x, np.float32).astype(BF16)
    low = (np.asarray(x, np.float64) - high.astype(np.float64)).astype(BF16)
    return jnp.asarray(high), jnp.asarray(low)


@functools.lru_cache(None)
def host_tables(fourier):
    table = strain_table()
    synthesis, analysis = time_tables(TIMES, fourier)
    groups = TIMES // GROUP
    steps = synthesis - np.roll(synthesis, 1, axis=1)
    synth = np.zeros((groups, 3, GROUP, 3, fourier))
    analyse = np.zeros((groups, 3, GROUP, 3, fourier))
    for g in range(groups):
        for i in range(3):
            for m in range(GROUP):
                synth[g, i, m, i] = steps[:, g * GROUP + m]
                analyse[g, i, m, i] = analysis[g * GROUP + m]
    strain = np.zeros((GROUP, 48, 8, 3, 2, GROUP))
    force = np.zeros((8, 3, GROUP, GROUP, 48))
    shaped = table.reshape(48, 8, 3)
    for m in range(GROUP):
        for part in range(2):
            strain[m, :, :, :, part, m] = shaped
        force[:, :, m, m, :] = np.transpose(shaped, (1, 2, 0))
    width = 3 * fourier
    return (
        synth.reshape(TIMES * 3, width),
        analyse.reshape(TIMES * 3, width),
        strain.reshape(GROUP * 48, GROUP * 48),
        force.reshape(GROUP * 24, GROUP * 48),
    )


def split_rows(x):
    rows, n = x.shape
    high = x.astype(BF16).astype(F32)
    low = x - high
    parts = jnp.concatenate(
        [high.reshape(rows // 8, 1, 8, n), low.reshape(rows // 8, 1, 8, n)], axis=1
    )
    return parts.reshape(rows * 2, n).astype(BF16)


def dot(a, b):
    return lax.dot_general(a, b, (((1,), (0,)), ((), ())), preferred_element_type=F32)


def dot_t(a, b):
    return lax.dot_general(a, b, (((1,), (1,)), ((), ())), preferred_element_type=F32)


LAME = POISSON / ((1.0 + POISSON) * (1.0 - 2.0 * POISSON))
SHEAR = 1.0 / (2.0 * (1.0 + POISSON))


def element_kernel(
    counts_ref, int_ref, tail_ref, conn_ref, size_ref, stiff_ref, yield_ref, rate_ref, stress_ref,
    synth_hi_ref, synth_lo_ref, strain_ref, force_ref,
    stress_out, total,
    nodal, onehot, folded, gathered, stresses, forces,
):
    step = pl.program_id(0)
    block = conn_ref.shape[1]
    nodes = nodal.shape[1]
    groups = TIMES // GROUP

    @pl.when(step == 0)
    def _():
        inner, tail = int_ref[...], tail_ref[...]
        first = inner.shape[1]
        high, low = synth_hi_ref[...], synth_lo_ref[...]
        nodal[:, :first] = split_rows(dot(high, inner) + dot(low, inner))
        nodal[:, first:] = split_rows(dot_t(high, tail) + dot_t(low, tail))
        total[...] = jnp.zeros_like(total)

    fold = total.shape[1]
    pages = total.shape[0] // (3 * TIMES)
    listed = jnp.transpose(conn_ref[...])
    lane = lax.broadcasted_iota(jnp.int32, (block, fold), 1)
    iota = lax.broadcasted_iota(jnp.int16, (nodes, block), 0)
    for a in range(8):
        index = conn_ref[a : a + 1, :].astype(jnp.int16)
        hit = iota == jnp.broadcast_to(index, (nodes, block))
        onehot[:, a * block : (a + 1) * block] = jnp.where(
            hit, jnp.ones((), BF16), jnp.zeros((), BF16)
        )
        place = jnp.broadcast_to((listed[:, a : a + 1] & (fold - 1)), (block, fold))
        folded[a * block : (a + 1) * block, :] = (place == lane).astype(F32).astype(BF16)
    table = nodal[...]
    for a in range(8):
        picked = dot(table, onehot[:, a * block : (a + 1) * block]).astype(BF16)
        for g in range(groups):
            gathered[g, a * 48 : (a + 1) * 48, :] = picked[g * 48 : (g + 1) * 48, :]

    size = size_ref[...]
    stiff = stiff_ref[...]
    yields = yield_ref[...]
    rate8 = jnp.broadcast_to(rate_ref[...], (8, block))
    inverse = 1.0 / yields
    weight = stiff * (2.0 / size) * inverse
    shear8 = jnp.broadcast_to(weight * SHEAR, (8, block))
    shear28 = shear8 * 2.0
    lame8 = jnp.broadcast_to(weight * LAME, (8, block))
    slot = lax.broadcasted_iota(jnp.int32, (1, block), 1) + step * block
    live = (slot < counts_ref[0]).astype(F32)
    scale = size * size * 0.25 * live * yields
    state = [stress_ref[c * 8 : (c + 1) * 8, :] * inverse for c in range(6)]
    deltas = [dot(strain_ref[...], gathered[g]) for g in range(groups)]
    for g in range(groups):
        delta = deltas[g]
        for m in range(GROUP):
            d = [delta[m * 48 + c * 8 : m * 48 + c * 8 + 8, :] for c in range(6)]
            volume = (d[0] + d[1] + d[2]) * lame8
            for c in range(6):
                rise = d[c] * shear28 + volume if c < 3 else d[c] * shear8
                state[c] = state[c] + rise - rate8 * jnp.tanh(state[c])
            stresses[g, m * 48 : (m + 1) * 48, :] = jnp.concatenate(state, axis=0).astype(BF16)
        pushed = dot(force_ref[...], stresses[g]) * scale
        if g % 2 == 0:
            before = pushed
            continue
        for a in range(8):
            rows = slice(a * 24, (a + 1) * 24)
            both = jnp.concatenate([before[rows, :], pushed[rows, :]], axis=0)
            page = lax.shift_right_logical(conn_ref[a : a + 1, :], 8)
            for t in range(pages):
                at_row = t * 3 * TIMES + (g - 1) * 24
                forces[at_row : at_row + 48, a * block : (a + 1) * block] = jnp.where(
                    page == t, both, 0.0
                ).astype(BF16)
    stress_out[...] = jnp.concatenate(state, axis=0) * (yields * live)
    rows = total.shape[0] // 2
    for half in (slice(0, rows), slice(rows, 2 * rows)):
        total[half, :] += dot(forces[half, :], folded[...])


def node_forces(total_ref, an_hi_ref, an_lo_ref, page):
    rows = 3 * TIMES
    total = jnp.transpose(total_ref[page * rows : (page + 1) * rows, :])
    high = total.astype(BF16)
    low = (total - high.astype(F32)).astype(BF16)
    return dot(high, an_hi_ref[...]) + dot(high, an_lo_ref[...]) + dot(low, an_hi_ref[...])


def element_update(inner, tail, conn_t, count, params, stress_zero, fold=256, block=512):
    elems = conn_t.shape[1]
    width = inner.shape[0]
    padded = inner.shape[1] + tail.shape[0]
    synth, _, strain, force = host_tables(width // 3)
    synth_hi, synth_lo = two_parts(synth)
    strain = jnp.asarray(strain, BF16)
    force = jnp.asarray(force, BF16)
    whole = lambda x: pl.BlockSpec(x.shape, lambda s: (0,) * x.ndim)
    by_block = lambda r: pl.BlockSpec((r, block), lambda s: (0, s))
    return pl.pallas_call(
        element_kernel,
        grid=(elems // block,),
        out_shape=(
            jax.ShapeDtypeStruct(stress_zero.shape, F32),
            jax.ShapeDtypeStruct((padded // fold * 3 * TIMES, fold), F32),
        ),
        in_specs=[
            pl.BlockSpec(memory_space=pltpu.SMEM),
            whole(inner), whole(tail), by_block(8), by_block(1), by_block(1), by_block(1), by_block(1), by_block(48),
            whole(synth_hi), whole(synth_lo),
            whole(strain), whole(force),
        ],
        out_specs=(by_block(48), pl.BlockSpec((padded // fold * 3 * TIMES, fold), lambda s: (0, 0))),
        scratch_shapes=[
            pltpu.VMEM((6 * TIMES, padded), BF16),
            pltpu.VMEM((padded, 8 * block), BF16),
            pltpu.VMEM((8 * block, fold), BF16),
            pltpu.VMEM((TIMES // GROUP, GROUP * 48, block), BF16),
            pltpu.VMEM((TIMES // GROUP, GROUP * 48, block), BF16),
            pltpu.VMEM((padded // fold * 3 * TIMES, 8 * block), BF16),
        ],
        compiler_params=pltpu.CompilerParams(
            vmem_limit_bytes=28 * 1024 * 1024, dimension_semantics=("arbitrary",)
        ),
        cost_estimate=pl.CostEstimate(flops=25000000000, bytes_accessed=4000000, transcendentals=0),
        name="elements",
    )(count, inner, tail, conn_t, *params, stress_zero, synth_hi, synth_lo, strain, force)


MESH = pl.DeviceIdType.MESH


def pair_hits(map_ref, rows):
    neighbours, slots = map_ref.shape
    listed = jnp.concatenate([map_ref[j : j + 1, :] for j in range(neighbours)], axis=1)
    iota = lax.broadcasted_iota(jnp.int32, (rows, neighbours * slots), 0)
    return (iota == listed).astype(F32)


def send(src, dst, send_sem, recv_sem, peer):
    copy = pltpu.make_async_remote_copy(
        src_ref=src, dst_ref=dst, send_sem=send_sem, recv_sem=recv_sem,
        device_id=peer, device_id_type=MESH,
    )
    copy.start()
    return copy


def halo_kernel(dom, offsets, int_ref, if_ref, map_ref, tail_out, out_block, in_block, send_sem, recv_sem):
    me = lax.axis_index("dom")
    near = [{"dom": lax.rem(me + off + dom, dom)} for off in offsets]
    barrier = pltpu.get_barrier_semaphore()
    for peer in near:
        pl.semaphore_signal(barrier, inc=1, device_id=peer, device_id_type=MESH)
    width, int_nodes = int_ref.shape
    if_nodes = if_ref.shape[0]
    slots = map_ref.shape[1]
    hits = jnp.transpose(pair_hits(map_ref, int_nodes + if_nodes)).astype(BF16)
    picked = (
        dot_t(hits[:, :int_nodes], int_ref[...]) + dot(hits[:, int_nodes:], if_ref[...])
    ).astype(BF16)
    for j in range(len(offsets)):
        out_block[j] = picked[j * slots : (j + 1) * slots]
    pl.semaphore_wait(barrier, len(near))
    copies = [
        send(out_block.at[j], in_block.at[j], send_sem.at[j], recv_sem.at[j], near[j])
        for j in range(len(offsets))
    ]
    for copy in copies:
        copy.wait()
    parts = [if_ref[...].astype(F32)] + [in_block[j].astype(F32) for j in range(len(offsets))]
    fill = tail_out.shape[0] - if_nodes - len(offsets) * slots
    tail_out[...] = jnp.concatenate(parts + [jnp.zeros((fill, width), F32)], axis=0).astype(BF16)


def halo(u_int_t, u_if, send_map, offsets, dom):
    neighbours, slots = send_map.shape
    width, int_nodes = u_int_t.shape
    used = int_nodes + u_if.shape[0] + neighbours * slots
    padded = -(-used // 256) * 256
    vmem = pl.BlockSpec(memory_space=pltpu.VMEM)
    return pl.pallas_call(
        functools.partial(halo_kernel, dom, offsets),
        out_shape=jax.ShapeDtypeStruct((padded - int_nodes, width), BF16),
        in_specs=[vmem] * 3,
        out_specs=vmem,
        scratch_shapes=[
            pltpu.VMEM((neighbours, slots, width), BF16),
            pltpu.VMEM((neighbours, slots, width), BF16),
            pltpu.SemaphoreType.DMA((neighbours,)),
            pltpu.SemaphoreType.DMA((neighbours,)),
        ],
        compiler_params=pltpu.CompilerParams(
            collective_id=0, has_side_effects=True, vmem_limit_bytes=12 * 1024 * 1024
        ),
        cost_estimate=pl.CostEstimate(flops=6000000000, bytes_accessed=1000000, transcendentals=0),
        name="halo",
    )(u_int_t, u_if, send_map)


def finish_kernel(
    sizes, offsets, stop,
    total_ref, an_hi_ref, an_lo_ref, map_ref, load_int_ref, load_if_ref, kinv, sinv_t,
    du_int_ref, du_if_ref,
    sinv, out_ret, in_ret, spread, spread_if, rhs_int,
    out_grp, in_grp, out_rhs, all_rhs, flat,
    own1, out1, in1, out2, in2, own3, out3, in3, last,
    ret_sem, grp_sem, rhs_sem, sem1, sem2, sem3,
):
    zs, xs, cores, grps = sizes
    started = []

    def launch(*where):
        started.append(send(*where))
        return started[-1]

    dom = zs * xs * cores
    me = lax.axis_index("dom")
    my_grp = lax.axis_index("grp")
    core = lax.rem(me, cores)
    x = lax.rem(me // cores, xs)
    z = me // (cores * xs)
    at = lambda zz, xx, cc: {"dom": (zz * xs + xx) * cores + cc}
    owners = [{"dom": lax.rem(me - off + dom, dom)} for off in offsets]
    groups = [{"grp": lax.rem(my_grp + s, grps)} for s in range(1, grps)]
    sibling = at(z, x, 1 - core)
    along_x = [at(z, lax.rem(x + s, xs), core) for s in range(1, xs)]
    along_z = [at(lax.rem(z + s, zs), x, core) for s in range(1, zs)]
    neighbours, slots = map_ref.shape
    width, int_nodes = load_int_ref.shape
    if_nodes = load_if_ref.shape[0]
    fourier = width // 3
    owned = int_nodes + if_nodes
    peers = owners + groups + [sibling] + along_x + along_z
    barrier = pltpu.get_barrier_semaphore()
    for peer in peers:
        pl.semaphore_signal(barrier, inc=1, device_id=peer, device_id_type=MESH)
    fold = total_ref.shape[1]
    inner = int_nodes // fold
    outer = node_forces(total_ref, an_hi_ref, an_lo_ref, inner)
    for j in range(neighbours):
        out_ret[j] = outer[if_nodes + j * slots : if_nodes + (j + 1) * slots]
    pl.semaphore_wait(barrier, len(peers))
    copies = [
        launch(out_ret.at[j], in_ret.at[j], ret_sem.at[0, j], ret_sem.at[1, j], owners[j])
        for j in range(neighbours)
    ]
    hits = pair_hits(map_ref, owned).astype(BF16)
    own = jnp.concatenate(
        [node_forces(total_ref, an_hi_ref, an_lo_ref, page) for page in range(inner)]
        + [outer[:if_nodes]],
        axis=0,
    )
    load_int = jnp.transpose(load_int_ref[...])
    strip = 384
    for c in range(sinv.shape[0] // strip):
        sinv[c * strip : (c + 1) * strip, :] = jnp.transpose(sinv_t[:, c * strip : (c + 1) * strip])
    for copy in copies:
        copy.wait_recv()
    back = jnp.concatenate([in_ret[j] for j in range(neighbours)], axis=0)
    high = back.astype(BF16)
    low = (back - high.astype(F32)).astype(BF16)
    force = own + dot(hits, high) + dot(hits, low)
    share = out_grp.shape[1]
    pieces = jnp.concatenate(
        [force[int_nodes:], jnp.zeros((grps * share - if_nodes, width), F32)], axis=0
    )
    for q in range(grps):
        out_grp[q] = pieces[q * share : (q + 1) * share]
    copies = [
        launch(out_grp.at[peer["grp"]], in_grp.at[s], grp_sem.at[0, s], grp_sem.at[1, s], peer)
        for s, peer in enumerate(groups)
    ]
    r_int = load_int - force[:int_nodes]
    for i in range(3):
        spread[pl.ds(i, int_nodes, stride=3), :] = r_int[:, i * fourier : (i + 1) * fourier]
    rhs_int[...] = spread[...].astype(BF16)
    chunk = 256
    chunks = kinv.shape[0] // chunk

    def solve(c, _):
        rows = pl.ds(pl.multiple_of(c * chunk, chunk), chunk)
        spread[rows, :] = dot(kinv[rows, :], rhs_int[...])
        return 0

    lax.fori_loop(0, 2, solve, 0)
    loads = jnp.concatenate(
        [load_if_ref[...], jnp.zeros((grps * share - if_nodes, width), F32)], axis=0
    )
    mine = loads[0:share]
    for q in range(1, grps):
        mine = jnp.where(my_grp == q, loads[q * share : (q + 1) * share], mine)
    total = out_grp[my_grp]
    for s, copy in enumerate(copies):
        copy.wait_recv()
        total = total + in_grp[s]
    out_rhs[...] = (mine - total).astype(BF16)
    copies = [
        launch(out_rhs, all_rhs.at[my_grp], rhs_sem.at[0, s], rhs_sem.at[1, s], peer)
        for s, peer in enumerate(groups)
    ]
    all_rhs[my_grp] = out_rhs[...]
    lax.fori_loop(2, 3, solve, 0)
    for copy in copies:
        copy.wait_recv()
    gathered = jnp.concatenate([all_rhs[q].astype(F32) for q in range(grps)], axis=0)[:if_nodes]
    for i in range(3):
        spread_if[pl.ds(i, if_nodes, stride=3), :] = gathered[:, i * fourier : (i + 1) * fourier]
    rhs_if = spread_if[...]
    empty = jnp.zeros_like(rhs_if)
    left = jnp.concatenate([rhs_if, empty], axis=1).astype(BF16)
    right = jnp.concatenate([empty, rhs_if], axis=1).astype(BF16)
    half = zs // 2
    parts = out1.shape[0]
    each = half // parts
    per_owner = sinv.shape[0] // dom
    per_z = per_owner * xs * cores
    fill = jnp.zeros((out1.shape[2] - each * per_owner, 2 * fourier), F32)
    first_copies = []
    for c in range(parts):
        for j in range(each):
            start = pl.multiple_of(lax.rem(z + c * each + j + 1, half) * per_z, 16)
            other = pl.multiple_of(start + half * per_z, 16)
            flat[(c * each + j) * per_z : (c * each + j + 1) * per_z, :] = dot(
                sinv[pl.ds(start, per_z), :], left
            ) + dot(sinv[pl.ds(other, per_z), :], right)
        for k in range(xs):
            by_core = []
            for cc in range(cores):
                rows = []
                for j in range(each):
                    at_row = (c * each + j) * per_z + (k * cores + cc) * per_owner
                    rows.append(flat[at_row : at_row + per_owner, :])
                by_core.append(jnp.concatenate(rows + [fill], axis=0))
            own1[c, k] = jnp.where(core == 0, by_core[0], by_core[1])
            out1[c, k] = jnp.where(core == 0, by_core[1], by_core[0]).astype(BF16)
        first_copies.append(launch(out1.at[c], in1.at[c], sem1.at[0, c], sem1.at[1, c], sibling))
    second_copies = []
    for c in range(parts):
        first_copies[c].wait_recv()
        for k in range(xs):
            summed = own1[c, k] + in1[c, k].astype(F32)
            own1[c, k] = summed
            out2[c, k] = summed.astype(BF16)
        second_copies.append([
            launch(out2.at[c, lax.rem(x + s + 1, xs)], in2.at[c, s], sem2.at[0, c, s], sem2.at[1, c, s], peer)
            for s, peer in enumerate(along_x)
        ])
    lax.fori_loop(3, chunks, solve, 0)
    short = per_owner // 2
    first = lax.broadcasted_iota(jnp.int32, (short, 2 * fourier), 1) < fourier
    fill = jnp.zeros((out3.shape[3] - short, 2 * fourier), F32)
    third_copies = []
    for c in range(parts):
        summed = own1[c, x]
        for s, copy in enumerate(second_copies[c]):
            copy.wait_recv()
            summed = summed + in2[c, s].astype(F32)
        turned = pltpu.roll(summed, fourier, 1)
        for j in range(each):
            top = slice(j * per_owner, j * per_owner + short)
            low_rows = slice(j * per_owner + short, (j + 1) * per_owner)
            o = c * each + j + 1
            for h, (a, b) in enumerate(((summed, turned), (turned, summed))):
                block = jnp.concatenate([jnp.where(first, a[top], b[low_rows]), fill], axis=0)
                if o == half:
                    own3[h] = block
                out3[c, j, h] = block.astype(BF16)
            for s in (o, o + half):
                if s < zs:
                    target = lax.rem(z + s, zs)
                    third_copies.append(launch(
                        out3.at[c, j, target // half], in3.at[s - 1],
                        sem3.at[0, s - 1], sem3.at[1, s - 1], along_z[s - 1],
                    ))
    for i in range(3):
        du_int_ref[i * fourier : (i + 1) * fourier, :] = jnp.transpose(
            spread[pl.ds(i, int_nodes, stride=3), :]
        )
    for copy in third_copies:
        copy.wait_recv()
    summed = own3[z // half]
    for s in range(zs - 1):
        summed = summed + in3[s].astype(F32)
    last[0] = summed
    last[1] = pltpu.roll(summed, fourier, 1)
    nodes = short // 3
    for h in range(2):
        for i in range(3):
            du_if_ref[h * nodes : (h + 1) * nodes, i * fourier : (i + 1) * fourier] = last[
                h, pl.ds(i, nodes, stride=3), :
            ][:, :fourier]
    for copy in started:
        copy.wait_send()


def finish(total, send_map, load_int_t, load_if, kinv_int, sinv_t, offsets, sizes, stop=99):
    zs, xs, cores, grps = sizes
    neighbours, slots = send_map.shape
    width, int_nodes = load_int_t.shape
    sinv_rows = sinv_t.shape[1]
    if_nodes = load_if.shape[0]
    fourier = width // 3
    dom = zs * xs * cores
    per_owner = sinv_rows // dom
    up = lambda n, k: -(-n // k) * k
    share = up(-(-if_nodes // grps), 8)
    parts = 2
    each = zs // 2 // parts
    rows1 = up(per_owner * each, 16)
    rows3 = up(per_owner // 2, 16)
    vmem = pl.BlockSpec(memory_space=pltpu.VMEM)
    sems = pltpu.SemaphoreType.DMA
    lanes = 2 * fourier
    an_hi, an_lo = two_parts(host_tables(fourier)[1])
    return pl.pallas_call(
        functools.partial(finish_kernel, sizes, offsets, stop),
        out_shape=(
            jax.ShapeDtypeStruct((width, int_nodes), F32),
            jax.ShapeDtypeStruct((per_owner // 3, width), F32),
        ),
        in_specs=[vmem] * 8,
        out_specs=(vmem, vmem),
        scratch_shapes=[
            pltpu.VMEM((sinv_rows, sinv_t.shape[0]), BF16),
            pltpu.VMEM((neighbours, slots, width), F32),
            pltpu.VMEM((neighbours, slots, width), F32),
            pltpu.VMEM((3 * int_nodes, fourier), F32),
            pltpu.VMEM((3 * if_nodes, fourier), F32),
            pltpu.VMEM((3 * int_nodes, fourier), BF16),
            pltpu.VMEM((grps, share, width), F32),
            pltpu.VMEM((grps - 1, share, width), F32),
            pltpu.VMEM((share, width), BF16),
            pltpu.VMEM((grps, share, width), BF16),
            pltpu.VMEM((sinv_rows // 2, lanes), F32),
            pltpu.VMEM((parts, xs, rows1, lanes), F32),
            pltpu.VMEM((parts, xs, rows1, lanes), BF16),
            pltpu.VMEM((parts, xs, rows1, lanes), BF16),
            pltpu.VMEM((parts, xs, rows1, lanes), BF16),
            pltpu.VMEM((parts, xs - 1, rows1, lanes), BF16),
            pltpu.VMEM((2, rows3, lanes), F32),
            pltpu.VMEM((parts, each, 2, rows3, lanes), BF16),
            pltpu.VMEM((zs - 1, rows3, lanes), BF16),
            pltpu.VMEM((2, rows3, lanes), F32),
            sems((2, neighbours)), sems((2, grps - 1)), sems((2, grps - 1)),
            sems((2, parts)), sems((2, parts, xs - 1)), sems((2, zs - 1)),
        ],
        compiler_params=pltpu.CompilerParams(
            collective_id=1, has_side_effects=True, vmem_limit_bytes=20 * 1024 * 1024
        ),
        cost_estimate=pl.CostEstimate(flops=20000000000, bytes_accessed=9000000, transcendentals=0),
        name="finish",
    )(total, an_hi, an_lo, send_map, load_int_t, load_if, kinv_int, sinv_t)


def per_device(
    u_int, u_if, load_int, load_if, conn, send_map, counts, elem_size, stiffness,
    yield_stress, relax_rate, stress_init, kinv_int, sinv,
):
    reach = send_map.shape[0] // 2
    offsets = list(range(-reach, 0)) + list(range(1, reach + 1))
    dom, grps = lax.axis_size("dom"), lax.axis_size("grp")
    sizes = (dom // 8, 4, 2, grps)
    u_int_t, conn_t = jnp.transpose(u_int), jnp.transpose(conn)
    tail = halo(u_int_t, u_if, send_map, offsets, dom)
    params = [v.reshape(1, -1) for v in (elem_size, stiffness, yield_stress, relax_rate)]
    stress_end, force = element_update(u_int_t, tail, conn_t, counts, params, stress_init)
    du_int_t, du_if = finish(
        force, send_map, jnp.transpose(load_int), load_if, kinv_int, jnp.transpose(sinv), offsets, sizes
    )
    return (jnp.transpose(du_int_t), du_if, stress_end)


def solution(mesh):
    both = ("grp", "dom")
    return jax.shard_map(
        per_device,
        mesh=mesh,
        in_specs=(
            P(both, None), P("dom", None), P(both, None), P("dom", None), P(both, None),
            P(both, None), P(both), P(both), P(both), P(both), P(both), P(None, both),
            P(both, None), P("grp", "dom"),
        ),
        out_specs=(P(both, None), P(both, None), P(None, both)),
        check_vma=False,
    )
```

```python
import functools
import math

import jax
import jax.numpy as jnp
import numpy as np
from jax import lax
from jax.experimental import pallas as pl
from jax.experimental.pallas import tpu as pltpu
from jax.sharding import PartitionSpec as P

TIMES = 32
GROUP = 8
POISSON = 0.3
BF16 = jnp.bfloat16
F32 = jnp.float32


def strain_table():
    gauss = 1.0 / math.sqrt(3.0)
    table = np.zeros((6, 8, 8, 3))
    for point in range(8):
        coords = [((point >> bit & 1) * 2 - 1) * gauss for bit in range(3)]
        for corner in range(8):
            signs = [(corner >> bit & 1) * 2 - 1 for bit in range(3)]
            deriv = []
            for axis in range(3):
                value = signs[axis] / 8.0
                for other in range(3):
                    if other != axis:
                        value = value * (1.0 + signs[other] * coords[other])
                deriv.append(value)
            table[0, point, corner, 0] = deriv[0]
            table[1, point, corner, 1] = deriv[1]
            table[2, point, corner, 2] = deriv[2]
            table[3, point, corner, 0] = deriv[1]
            table[3, point, corner, 1] = deriv[0]
            table[4, point, corner, 1] = deriv[2]
            table[4, point, corner, 2] = deriv[1]
            table[5, point, corner, 2] = deriv[0]
            table[5, point, corner, 0] = deriv[2]
    return np.asarray(np.asarray(table.reshape(48, 24), np.float32), BF16).astype(np.float64)


def time_tables(times, fourier):
    theta = 2.0 * math.pi * (np.arange(times) + 0.3) / times
    synthesis = np.zeros((fourier, times))
    for column in range(fourier):
        harmonic = column // 2
        if column % 2 == 0:
            synthesis[column] = np.cos(harmonic * theta)
        else:
            synthesis[column] = np.sin((harmonic + 1) * theta)
    analysis = synthesis.T * (2.0 / times)
    analysis[:, 0] = 1.0 / times
    return synthesis.astype(np.float32).astype(np.float64), analysis.astype(np.float32).astype(np.float64)


def two_parts(x):
    high = np.asarray(x, np.float32).astype(BF16)
    low = (np.asarray(x, np.float64) - high.astype(np.float64)).astype(BF16)
    return jnp.asarray(high), jnp.asarray(low)


@functools.lru_cache(None)
def host_tables(fourier):
    table = strain_table()
    synthesis, analysis = time_tables(TIMES, fourier)
    groups = TIMES // GROUP
    steps = synthesis - np.roll(synthesis, 1, axis=1)
    synth = np.zeros((groups, 3, GROUP, 3, fourier))
    analyse = np.zeros((groups, 3, GROUP, 3, fourier))
    for g in range(groups):
        for i in range(3):
            for m in range(GROUP):
                synth[g, i, m, i] = steps[:, g * GROUP + m]
                analyse[g, i, m, i] = analysis[g * GROUP + m]
    strain = np.zeros((GROUP, 48, 8, 3, 2, GROUP))
    force = np.zeros((8, 3, GROUP, GROUP, 48))
    shaped = table.reshape(48, 8, 3)
    for m in range(GROUP):
        for part in range(2):
            strain[m, :, :, :, part, m] = shaped
        force[:, :, m, m, :] = np.transpose(shaped, (1, 2, 0))
    width = 3 * fourier
    return (
        synth.reshape(TIMES * 3, width),
        analyse.reshape(TIMES * 3, width),
        strain.reshape(GROUP * 48, GROUP * 48),
        force.reshape(GROUP * 24, GROUP * 48),
    )


def split_rows(x):
    rows, n = x.shape
    high = x.astype(BF16).astype(F32)
    low = x - high
    parts = jnp.concatenate(
        [high.reshape(rows // 8, 1, 8, n), low.reshape(rows // 8, 1, 8, n)], axis=1
    )
    return parts.reshape(rows * 2, n).astype(BF16)


def dot(a, b):
    return lax.dot_general(a, b, (((1,), (0,)), ((), ())), preferred_element_type=F32)


def dot_t(a, b):
    return lax.dot_general(a, b, (((1,), (1,)), ((), ())), preferred_element_type=F32)


LAME = POISSON / ((1.0 + POISSON) * (1.0 - 2.0 * POISSON))
SHEAR = 1.0 / (2.0 * (1.0 + POISSON))


def element_kernel(
    counts_ref, int_ref, tail_ref, conn_ref, size_ref, stiff_ref, yield_ref, rate_ref, stress_ref,
    synth_hi_ref, synth_lo_ref, strain_ref, force_ref,
    stress_out, total,
    nodal, onehot, folded, gathered, stresses, forces,
):
    step = pl.program_id(0)
    block = conn_ref.shape[1]
    nodes = nodal.shape[1]
    groups = TIMES // GROUP

    @pl.when(step == 0)
    def _():
        inner, tail = int_ref[...], tail_ref[...]
        first = inner.shape[1]
        high, low = synth_hi_ref[...], synth_lo_ref[...]
        nodal[:, :first] = split_rows(dot(high, inner) + dot(low, inner))
        nodal[:, first:] = split_rows(dot_t(high, tail) + dot_t(low, tail))
        total[...] = jnp.zeros_like(total)

    fold = total.shape[1]
    pages = total.shape[0] // (3 * TIMES)
    listed = jnp.transpose(conn_ref[...])
    lane = lax.broadcasted_iota(jnp.int32, (block, fold), 1)
    iota = lax.broadcasted_iota(jnp.int16, (nodes, block), 0)
    for a in range(8):
        index = conn_ref[a : a + 1, :].astype(jnp.int16)
        hit = iota == jnp.broadcast_to(index, (nodes, block))
        onehot[:, a * block : (a + 1) * block] = jnp.where(
            hit, jnp.ones((), BF16), jnp.zeros((), BF16)
        )
        place = jnp.broadcast_to((listed[:, a : a + 1] & (fold - 1)), (block, fold))
        folded[a * block : (a + 1) * block, :] = (place == lane).astype(F32).astype(BF16)
    table = nodal[...]
    for a in range(8):
        picked = dot(table, onehot[:, a * block : (a + 1) * block]).astype(BF16)
        for g in range(groups):
            gathered[g, a * 48 : (a + 1) * 48, :] = picked[g * 48 : (g + 1) * 48, :]

    size = size_ref[...]
    stiff = stiff_ref[...]
    yields = yield_ref[...]
    rate8 = jnp.broadcast_to(rate_ref[...], (8, block))
    inverse = 1.0 / yields
    weight = stiff * (2.0 / size) * inverse
    shear8 = jnp.broadcast_to(weight * SHEAR, (8, block))
    shear28 = shear8 * 2.0
    lame8 = jnp.broadcast_to(weight * LAME, (8, block))
    slot = lax.broadcasted_iota(jnp.int32, (1, block), 1) + step * block
    live = (slot < counts_ref[0]).astype(F32)
    scale = size * size * 0.25 * live * yields
    state = [stress_ref[c * 8 : (c + 1) * 8, :] * inverse for c in range(6)]
    deltas = [dot(strain_ref[...], gathered[g]) for g in range(groups)]
    for g in range(groups):
        delta = deltas[g]
        for m in range(GROUP):
            d = [delta[m * 48 + c * 8 : m * 48 + c * 8 + 8, :] for c in range(6)]
            volume = (d[0] + d[1] + d[2]) * lame8
            for c in range(6):
                rise = d[c] * shear28 + volume if c < 3 else d[c] * shear8
                state[c] = state[c] + rise - rate8 * jnp.tanh(state[c])
            stresses[g, m * 48 : (m + 1) * 48, :] = jnp.concatenate(state, axis=0).astype(BF16)
        pushed = dot(force_ref[...], stresses[g]) * scale
        if g % 2 == 0:
            before = pushed
            continue
        for a in range(8):
            rows = slice(a * 24, (a + 1) * 24)
            both = jnp.concatenate([before[rows, :], pushed[rows, :]], axis=0)
            page = lax.shift_right_logical(conn_ref[a : a + 1, :], 8)
            for t in range(pages):
                at_row = t * 3 * TIMES + (g - 1) * 24
                forces[at_row : at_row + 48, a * block : (a + 1) * block] = jnp.where(
                    page == t, both, 0.0
                ).astype(BF16)
    stress_out[...] = jnp.concatenate(state, axis=0) * (yields * live)
    rows = total.shape[0] // 2
    for half in (slice(0, rows), slice(rows, 2 * rows)):
        total[half, :] += dot(forces[half, :], folded[...])


def node_forces(total_ref, an_hi_ref, an_lo_ref, page):
    rows = 3 * TIMES
    total = jnp.transpose(total_ref[page * rows : (page + 1) * rows, :])
    high = total.astype(BF16)
    low = (total - high.astype(F32)).astype(BF16)
    return dot(high, an_hi_ref[...]) + dot(high, an_lo_ref[...]) + dot(low, an_hi_ref[...])


def element_update(inner, tail, conn_t, count, params, stress_zero, fold=256, block=512):
    elems = conn_t.shape[1]
    width = inner.shape[0]
    padded = inner.shape[1] + tail.shape[0]
    synth, _, strain, force = host_tables(width // 3)
    synth_hi, synth_lo = two_parts(synth)
    strain = jnp.asarray(strain, BF16)
    force = jnp.asarray(force, BF16)
    whole = lambda x: pl.BlockSpec(x.shape, lambda s: (0,) * x.ndim)
    by_block = lambda r: pl.BlockSpec((r, block), lambda s: (0, s))
    return pl.pallas_call(
        element_kernel,
        grid=(elems // block,),
        out_shape=(
            jax.ShapeDtypeStruct(stress_zero.shape, F32),
            jax.ShapeDtypeStruct((padded // fold * 3 * TIMES, fold), F32),
        ),
        in_specs=[
            pl.BlockSpec(memory_space=pltpu.SMEM),
            whole(inner), whole(tail), by_block(8), by_block(1), by_block(1), by_block(1), by_block(1), by_block(48),
            whole(synth_hi), whole(synth_lo),
            whole(strain), whole(force),
        ],
        out_specs=(by_block(48), pl.BlockSpec((padded // fold * 3 * TIMES, fold), lambda s: (0, 0))),
        scratch_shapes=[
            pltpu.VMEM((6 * TIMES, padded), BF16),
            pltpu.VMEM((padded, 8 * block), BF16),
            pltpu.VMEM((8 * block, fold), BF16),
            pltpu.VMEM((TIMES // GROUP, GROUP * 48, block), BF16),
            pltpu.VMEM((TIMES // GROUP, GROUP * 48, block), BF16),
            pltpu.VMEM((padded // fold * 3 * TIMES, 8 * block), BF16),
        ],
        compiler_params=pltpu.CompilerParams(
            vmem_limit_bytes=28 * 1024 * 1024, dimension_semantics=("arbitrary",)
        ),
        cost_estimate=pl.CostEstimate(flops=25000000000, bytes_accessed=4000000, transcendentals=0),
        name="elements",
    )(count, inner, tail, conn_t, *params, stress_zero, synth_hi, synth_lo, strain, force)


MESH = pl.DeviceIdType.MESH


def pair_hits(map_ref, rows):
    neighbours, slots = map_ref.shape
    listed = jnp.concatenate([map_ref[j : j + 1, :] for j in range(neighbours)], axis=1)
    iota = lax.broadcasted_iota(jnp.int32, (rows, neighbours * slots), 0)
    return (iota == listed).astype(F32)


def send(src, dst, send_sem, recv_sem, peer):
    copy = pltpu.make_async_remote_copy(
        src_ref=src, dst_ref=dst, send_sem=send_sem, recv_sem=recv_sem,
        device_id=peer, device_id_type=MESH,
    )
    copy.start()
    return copy


def halo_kernel(dom, offsets, int_far, if_far, map_far, tail_out, int_ref, if_ref, map_ref, out_block, in_block, fetch_sem, send_sem, recv_sem):
    me = lax.axis_index("dom")
    near = [{"dom": lax.rem(me + off + dom, dom)} for off in offsets]
    fetches = [
        pltpu.make_async_copy(src, dst, fetch_sem.at[n])
        for n, (src, dst) in enumerate(((map_far, map_ref), (if_far, if_ref), (int_far, int_ref)))
    ]
    for fetch in fetches:
        fetch.start()
    barrier = pltpu.get_barrier_semaphore()
    for peer in near:
        pl.semaphore_signal(barrier, inc=1, device_id=peer, device_id_type=MESH)
    width, int_nodes = int_ref.shape
    if_nodes = if_ref.shape[0]
    slots = map_ref.shape[1]
    fetches[0].wait()
    hits = jnp.transpose(pair_hits(map_ref, int_nodes + if_nodes)).astype(BF16)
    fetches[1].wait()
    fetches[2].wait()
    picked = (
        dot_t(hits[:, :int_nodes], int_ref[...]) + dot(hits[:, int_nodes:], if_ref[...])
    ).astype(BF16)
    for j in range(len(offsets)):
        out_block[j] = picked[j * slots : (j + 1) * slots]
    pl.semaphore_wait(barrier, len(near))
    copies = [
        send(out_block.at[j], in_block.at[j], send_sem.at[j], recv_sem.at[j], near[j])
        for j in range(len(offsets))
    ]
    for copy in copies:
        copy.wait()
    parts = [if_ref[...].astype(F32)] + [in_block[j].astype(F32) for j in range(len(offsets))]
    fill = tail_out.shape[0] - if_nodes - len(offsets) * slots
    tail_out[...] = jnp.concatenate(parts + [jnp.zeros((fill, width), F32)], axis=0).astype(BF16)


def halo(u_int_t, u_if, send_map, offsets, dom):
    neighbours, slots = send_map.shape
    width, int_nodes = u_int_t.shape
    used = int_nodes + u_if.shape[0] + neighbours * slots
    padded = -(-used // 256) * 256
    vmem = pl.BlockSpec(memory_space=pltpu.VMEM)
    return pl.pallas_call(
        functools.partial(halo_kernel, dom, offsets),
        out_shape=jax.ShapeDtypeStruct((padded - int_nodes, width), BF16),
        in_specs=[pl.BlockSpec(memory_space=pltpu.HBM)] * 3,
        out_specs=vmem,
        scratch_shapes=[
            pltpu.VMEM(u_int_t.shape, BF16),
            pltpu.VMEM(u_if.shape, BF16),
            pltpu.VMEM(send_map.shape, jnp.int32),
            pltpu.VMEM((neighbours, slots, width), BF16),
            pltpu.VMEM((neighbours, slots, width), BF16),
            pltpu.SemaphoreType.DMA((3,)),
            pltpu.SemaphoreType.DMA((neighbours,)),
            pltpu.SemaphoreType.DMA((neighbours,)),
        ],
        compiler_params=pltpu.CompilerParams(
            collective_id=0, has_side_effects=True, vmem_limit_bytes=56 * 1024 * 1024
        ),
        cost_estimate=pl.CostEstimate(flops=6000000000, bytes_accessed=1000000, transcendentals=0),
        name="halo",
    )(u_int_t, u_if, send_map)


def finish_kernel(
    sizes, offsets, stop,
    total_ref, an_hi_ref, an_lo_ref, map_ref, load_int_ref, load_if_ref, kinv, sinv_t,
    du_int_ref, du_if_ref,
    sinv, out_ret, in_ret, spread, spread_if, rhs_int,
    out_grp, in_grp, flat,
    own1, out1, in1, out2, in2, own3, out3, in3, last,
    ret_sem, grp_sem, sem1, sem2, sem3,
):
    zs, xs, cores, grps = sizes
    started = []

    def launch(*where):
        started.append(send(*where))
        return started[-1]

    dom = zs * xs * cores
    me = lax.axis_index("dom")
    my_grp = lax.axis_index("grp")
    core = lax.rem(me, cores)
    x = lax.rem(me // cores, xs)
    z = me // (cores * xs)
    at = lambda zz, xx, cc: {"dom": (zz * xs + xx) * cores + cc}
    owners = [{"dom": lax.rem(me - off + dom, dom)} for off in offsets]
    groups = [{"grp": lax.rem(my_grp + s, grps)} for s in range(1, grps)]
    sibling = at(z, x, 1 - core)
    along_x = [at(z, lax.rem(x + s, xs), core) for s in range(1, xs)]
    along_z = [at(lax.rem(z + s, zs), x, core) for s in range(1, zs)]
    neighbours, slots = map_ref.shape
    width, int_nodes = load_int_ref.shape
    if_nodes = load_if_ref.shape[0]
    fourier = width // 3
    owned = int_nodes + if_nodes
    peers = owners + groups + [sibling] + along_x + along_z
    barrier = pltpu.get_barrier_semaphore()
    for peer in peers:
        pl.semaphore_signal(barrier, inc=1, device_id=peer, device_id_type=MESH)
    fold = total_ref.shape[1]
    inner = int_nodes // fold
    outer = node_forces(total_ref, an_hi_ref, an_lo_ref, inner)
    for j in range(neighbours):
        out_ret[j] = outer[if_nodes + j * slots : if_nodes + (j + 1) * slots]
    pl.semaphore_wait(barrier, len(peers))
    copies = [
        launch(out_ret.at[j], in_ret.at[j], ret_sem.at[0, j], ret_sem.at[1, j], owners[j])
        for j in range(neighbours)
    ]
    hits = pair_hits(map_ref, owned).astype(BF16)
    own = jnp.concatenate(
        [node_forces(total_ref, an_hi_ref, an_lo_ref, page) for page in range(inner)]
        + [outer[:if_nodes]],
        axis=0,
    )
    load_int = jnp.transpose(load_int_ref[...])
    strip = 384
    for c in range(sinv.shape[0] // strip):
        sinv[c * strip : (c + 1) * strip, :] = jnp.transpose(sinv_t[:, c * strip : (c + 1) * strip])
    for copy in copies:
        copy.wait_recv()
    back = jnp.concatenate([in_ret[j] for j in range(neighbours)], axis=0)
    high = back.astype(BF16)
    low = (back - high.astype(F32)).astype(BF16)
    force = own + dot(hits, high) + dot(hits, low)
    shared = force[int_nodes:]
    out_grp[...] = jnp.concatenate(
        [shared, jnp.zeros((out_grp.shape[0] - if_nodes, width), F32)], axis=0
    ).astype(BF16)
    copies = [
        launch(out_grp, in_grp.at[s], grp_sem.at[0, s], grp_sem.at[1, s], peer)
        for s, peer in enumerate(groups)
    ]
    r_int = load_int - force[:int_nodes]
    for i in range(3):
        spread[pl.ds(i, int_nodes, stride=3), :] = r_int[:, i * fourier : (i + 1) * fourier]
    rhs_int[...] = spread[...].astype(BF16)
    chunk = 256
    chunks = kinv.shape[0] // chunk

    def solve(c, _):
        rows = pl.ds(pl.multiple_of(c * chunk, chunk), chunk)
        spread[rows, :] = dot(kinv[rows, :], rhs_int[...])
        return 0

    lax.fori_loop(0, 3, solve, 0)
    for s, copy in enumerate(copies):
        copy.wait_recv()
        shared = shared + in_grp[s][:if_nodes].astype(F32)
    gathered = (load_if_ref[...] - shared).astype(BF16).astype(F32)
    for i in range(3):
        spread_if[pl.ds(i, if_nodes, stride=3), :] = gathered[:, i * fourier : (i + 1) * fourier]
    rhs_if = spread_if[...]
    empty = jnp.zeros_like(rhs_if)
    left = jnp.concatenate([rhs_if, empty], axis=1).astype(BF16)
    right = jnp.concatenate([empty, rhs_if], axis=1).astype(BF16)
    half = zs // 2
    parts = out1.shape[0]
    each = half // parts
    per_owner = sinv.shape[0] // dom
    per_z = per_owner * xs * cores
    fill = jnp.zeros((out1.shape[2] - each * per_owner, 2 * fourier), F32)
    first_copies = []
    for c in range(parts):
        for j in range(each):
            start = pl.multiple_of(lax.rem(z + c * each + j + 1, half) * per_z, 16)
            other = pl.multiple_of(start + half * per_z, 16)
            flat[(c * each + j) * per_z : (c * each + j + 1) * per_z, :] = dot(
                sinv[pl.ds(start, per_z), :], left
            ) + dot(sinv[pl.ds(other, per_z), :], right)
        for k in range(xs):
            by_core = []
            for cc in range(cores):
                rows = []
                for j in range(each):
                    at_row = (c * each + j) * per_z + (k * cores + cc) * per_owner
                    rows.append(flat[at_row : at_row + per_owner, :])
                by_core.append(jnp.concatenate(rows + [fill], axis=0))
            own1[c, k] = jnp.where(core == 0, by_core[0], by_core[1])
            out1[c, k] = jnp.where(core == 0, by_core[1], by_core[0]).astype(BF16)
        first_copies.append(launch(out1.at[c], in1.at[c], sem1.at[0, c], sem1.at[1, c], sibling))
    second_copies = []
    for c in range(parts):
        first_copies[c].wait_recv()
        for k in range(xs):
            summed = own1[c, k] + in1[c, k].astype(F32)
            own1[c, k] = summed
            out2[c, k] = summed.astype(BF16)
        second_copies.append([
            launch(out2.at[c, lax.rem(x + s + 1, xs)], in2.at[c, s], sem2.at[0, c, s], sem2.at[1, c, s], peer)
            for s, peer in enumerate(along_x)
        ])
    lax.fori_loop(3, chunks, solve, 0)
    short = per_owner // 2
    first = lax.broadcasted_iota(jnp.int32, (short, 2 * fourier), 1) < fourier
    fill = jnp.zeros((out3.shape[3] - short, 2 * fourier), F32)
    third_copies = []
    for c in range(parts):
        summed = own1[c, x]
        for s, copy in enumerate(second_copies[c]):
            copy.wait_recv()
            summed = summed + in2[c, s].astype(F32)
        turned = pltpu.roll(summed, fourier, 1)
        for j in range(each):
            top = slice(j * per_owner, j * per_owner + short)
            low_rows = slice(j * per_owner + short, (j + 1) * per_owner)
            o = c * each + j + 1
            for h, (a, b) in enumerate(((summed, turned), (turned, summed))):
                block = jnp.concatenate([jnp.where(first, a[top], b[low_rows]), fill], axis=0)
                if o == half:
                    own3[h] = block
                out3[c, j, h] = block.astype(BF16)
            for s in (o, o + half):
                if s < zs:
                    target = lax.rem(z + s, zs)
                    third_copies.append(launch(
                        out3.at[c, j, target // half], in3.at[s - 1],
                        sem3.at[0, s - 1], sem3.at[1, s - 1], along_z[s - 1],
                    ))
    for i in range(3):
        du_int_ref[i * fourier : (i + 1) * fourier, :] = jnp.transpose(
            spread[pl.ds(i, int_nodes, stride=3), :]
        )
    for copy in third_copies:
        copy.wait_recv()
    summed = own3[z // half]
    for s in range(zs - 1):
        summed = summed + in3[s].astype(F32)
    last[0] = summed
    last[1] = pltpu.roll(summed, fourier, 1)
    nodes = short // 3
    for h in range(2):
        for i in range(3):
            du_if_ref[h * nodes : (h + 1) * nodes, i * fourier : (i + 1) * fourier] = last[
                h, pl.ds(i, nodes, stride=3), :
            ][:, :fourier]
    for copy in started:
        copy.wait_send()


def finish(total, send_map, load_int_t, load_if, kinv_int, sinv_t, offsets, sizes, stop=99):
    zs, xs, cores, grps = sizes
    neighbours, slots = send_map.shape
    width, int_nodes = load_int_t.shape
    sinv_rows = sinv_t.shape[1]
    if_nodes = load_if.shape[0]
    fourier = width // 3
    dom = zs * xs * cores
    per_owner = sinv_rows // dom
    up = lambda n, k: -(-n // k) * k
    share = up(if_nodes, 16)
    parts = 2
    each = zs // 2 // parts
    rows1 = up(per_owner * each, 16)
    rows3 = up(per_owner // 2, 16)
    vmem = pl.BlockSpec(memory_space=pltpu.VMEM)
    sems = pltpu.SemaphoreType.DMA
    lanes = 2 * fourier
    an_hi, an_lo = two_parts(host_tables(fourier)[1])
    return pl.pallas_call(
        functools.partial(finish_kernel, sizes, offsets, stop),
        out_shape=(
            jax.ShapeDtypeStruct((width, int_nodes), F32),
            jax.ShapeDtypeStruct((per_owner // 3, width), F32),
        ),
        in_specs=[vmem] * 8,
        out_specs=(vmem, vmem),
        scratch_shapes=[
            pltpu.VMEM((sinv_rows, sinv_t.shape[0]), BF16),
            pltpu.VMEM((neighbours, slots, width), F32),
            pltpu.VMEM((neighbours, slots, width), F32),
            pltpu.VMEM((3 * int_nodes, fourier), F32),
            pltpu.VMEM((3 * if_nodes, fourier), F32),
            pltpu.VMEM((3 * int_nodes, fourier), BF16),
            pltpu.VMEM((share, width), BF16),
            pltpu.VMEM((grps - 1, share, width), BF16),
            pltpu.VMEM((sinv_rows // 2, lanes), F32),
            pltpu.VMEM((parts, xs, rows1, lanes), F32),
            pltpu.VMEM((parts, xs, rows1, lanes), BF16),
            pltpu.VMEM((parts, xs, rows1, lanes), BF16),
            pltpu.VMEM((parts, xs, rows1, lanes), BF16),
            pltpu.VMEM((parts, xs - 1, rows1, lanes), BF16),
            pltpu.VMEM((2, rows3, lanes), F32),
            pltpu.VMEM((parts, each, 2, rows3, lanes), BF16),
            pltpu.VMEM((zs - 1, rows3, lanes), BF16),
            pltpu.VMEM((2, rows3, lanes), F32),
            sems((2, neighbours)), sems((2, grps - 1)),
            sems((2, parts)), sems((2, parts, xs - 1)), sems((2, zs - 1)),
        ],
        compiler_params=pltpu.CompilerParams(
            collective_id=1, has_side_effects=True, vmem_limit_bytes=20 * 1024 * 1024
        ),
        cost_estimate=pl.CostEstimate(flops=20000000000, bytes_accessed=9000000, transcendentals=0),
        name="finish",
    )(total, an_hi, an_lo, send_map, load_int_t, load_if, kinv_int, sinv_t)


def per_device(
    u_int, u_if, load_int, load_if, conn, send_map, counts, elem_size, stiffness,
    yield_stress, relax_rate, stress_init, kinv_int, sinv,
):
    reach = send_map.shape[0] // 2
    offsets = list(range(-reach, 0)) + list(range(1, reach + 1))
    dom, grps = lax.axis_size("dom"), lax.axis_size("grp")
    sizes = (dom // 8, 4, 2, grps)
    u_int_t, conn_t = jnp.transpose(u_int), jnp.transpose(conn)
    tail = halo(u_int_t, u_if, send_map, offsets, dom)
    params = [v.reshape(1, -1) for v in (elem_size, stiffness, yield_stress, relax_rate)]
    stress_end, force = element_update(u_int_t, tail, conn_t, counts, params, stress_init)
    du_int_t, du_if = finish(
        force, send_map, jnp.transpose(load_int), load_if, kinv_int, jnp.transpose(sinv), offsets, sizes
    )
    return (jnp.transpose(du_int_t), du_if, stress_end)


def solution(mesh):
    both = ("grp", "dom")
    return jax.shard_map(
        per_device,
        mesh=mesh,
        in_specs=(
            P(both, None), P("dom", None), P(both, None), P("dom", None), P(both, None),
            P(both, None), P(both), P(both), P(both), P(both), P(both), P(None, both),
            P(both, None), P("grp", "dom"),
        ),
        out_specs=(P(both, None), P(both, None), P(None, both)),
        check_vma=False,
    )
```

```python
import functools
import math

import jax
import jax.numpy as jnp
import numpy as np
from jax import lax
from jax.experimental import pallas as pl
from jax.experimental.pallas import tpu as pltpu
from jax.sharding import PartitionSpec as P

TIMES = 32
GROUP = 8
POISSON = 0.3
BF16 = jnp.bfloat16
F32 = jnp.float32


def strain_table():
    gauss = 1.0 / math.sqrt(3.0)
    table = np.zeros((6, 8, 8, 3))
    for point in range(8):
        coords = [((point >> bit & 1) * 2 - 1) * gauss for bit in range(3)]
        for corner in range(8):
            signs = [(corner >> bit & 1) * 2 - 1 for bit in range(3)]
            deriv = []
            for axis in range(3):
                value = signs[axis] / 8.0
                for other in range(3):
                    if other != axis:
                        value = value * (1.0 + signs[other] * coords[other])
                deriv.append(value)
            table[0, point, corner, 0] = deriv[0]
            table[1, point, corner, 1] = deriv[1]
            table[2, point, corner, 2] = deriv[2]
            table[3, point, corner, 0] = deriv[1]
            table[3, point, corner, 1] = deriv[0]
            table[4, point, corner, 1] = deriv[2]
            table[4, point, corner, 2] = deriv[1]
            table[5, point, corner, 2] = deriv[0]
            table[5, point, corner, 0] = deriv[2]
    return np.asarray(np.asarray(table.reshape(48, 24), np.float32), BF16).astype(np.float64)


def time_tables(times, fourier):
    theta = 2.0 * math.pi * (np.arange(times) + 0.3) / times
    synthesis = np.zeros((fourier, times))
    for column in range(fourier):
        harmonic = column // 2
        if column % 2 == 0:
            synthesis[column] = np.cos(harmonic * theta)
        else:
            synthesis[column] = np.sin((harmonic + 1) * theta)
    analysis = synthesis.T * (2.0 / times)
    analysis[:, 0] = 1.0 / times
    return synthesis.astype(np.float32).astype(np.float64), analysis.astype(np.float32).astype(np.float64)


def two_parts(x):
    high = np.asarray(x, np.float32).astype(BF16)
    low = (np.asarray(x, np.float64) - high.astype(np.float64)).astype(BF16)
    return jnp.asarray(high), jnp.asarray(low)


@functools.lru_cache(None)
def host_tables(fourier):
    table = strain_table()
    synthesis, analysis = time_tables(TIMES, fourier)
    groups = TIMES // GROUP
    steps = synthesis - np.roll(synthesis, 1, axis=1)
    synth = np.zeros((groups, 3, GROUP, 3, fourier))
    analyse = np.zeros((groups, 3, GROUP, 3, fourier))
    for g in range(groups):
        for i in range(3):
            for m in range(GROUP):
                synth[g, i, m, i] = steps[:, g * GROUP + m]
                analyse[g, i, m, i] = analysis[g * GROUP + m]
    strain = np.zeros((GROUP, 48, 8, 3, 2, GROUP))
    force = np.zeros((8, 3, GROUP, GROUP, 48))
    shaped = table.reshape(48, 8, 3)
    for m in range(GROUP):
        for part in range(2):
            strain[m, :, :, :, part, m] = shaped
        force[:, :, m, m, :] = np.transpose(shaped, (1, 2, 0))
    width = 3 * fourier
    return (
        synth.reshape(TIMES * 3, width),
        analyse.reshape(TIMES * 3, width),
        strain.reshape(GROUP * 48, GROUP * 48),
        force.reshape(GROUP * 24, GROUP * 48),
    )


def split_rows(x):
    rows, n = x.shape
    high = x.astype(BF16).astype(F32)
    low = x - high
    parts = jnp.concatenate(
        [high.reshape(rows // 8, 1, 8, n), low.reshape(rows // 8, 1, 8, n)], axis=1
    )
    return parts.reshape(rows * 2, n).astype(BF16)


def dot(a, b):
    return lax.dot_general(a, b, (((1,), (0,)), ((), ())), preferred_element_type=F32)


def dot_t(a, b):
    return lax.dot_general(a, b, (((1,), (1,)), ((), ())), preferred_element_type=F32)


LAME = POISSON / ((1.0 + POISSON) * (1.0 - 2.0 * POISSON))
SHEAR = 1.0 / (2.0 * (1.0 + POISSON))


def element_kernel(
    counts_ref, int_ref, tail_ref, conn_ref, size_ref, stiff_ref, yield_ref, rate_ref, stress_ref,
    synth_hi_ref, synth_lo_ref, strain_ref, force_ref,
    stress_out, total,
    nodal, onehot, folded, gathered, stresses, forces,
):
    step = pl.program_id(0)
    block = conn_ref.shape[1]
    nodes = nodal.shape[1]
    groups = TIMES // GROUP

    @pl.when(step == 0)
    def _():
        inner, tail = int_ref[...], tail_ref[...]
        first = inner.shape[1]
        high, low = synth_hi_ref[...], synth_lo_ref[...]
        nodal[:, :first] = split_rows(dot(high, inner) + dot(low, inner))
        nodal[:, first:] = split_rows(dot_t(high, tail) + dot_t(low, tail))
        total[...] = jnp.zeros_like(total)

    @pl.when(step * block >= counts_ref[0])
    def _():
        stress_out[...] = jnp.zeros_like(stress_out)

    @pl.when(step * block < counts_ref[0])
    def _():
        fold = total.shape[1]
        pages = total.shape[0] // (3 * TIMES)
        listed = jnp.transpose(conn_ref[...])
        lane = lax.broadcasted_iota(jnp.int32, (block, fold), 1)
        iota = lax.broadcasted_iota(jnp.int16, (nodes, block), 0)
        for a in range(8):
            index = conn_ref[a : a + 1, :].astype(jnp.int16)
            hit = iota == jnp.broadcast_to(index, (nodes, block))
            onehot[:, a * block : (a + 1) * block] = jnp.where(
                hit, jnp.ones((), BF16), jnp.zeros((), BF16)
            )
            place = jnp.broadcast_to((listed[:, a : a + 1] & (fold - 1)), (block, fold))
            folded[a * block : (a + 1) * block, :] = (place == lane).astype(F32).astype(BF16)
        table = nodal[...]
        for a in range(8):
            picked = dot(table, onehot[:, a * block : (a + 1) * block]).astype(BF16)
            for g in range(groups):
                gathered[g, a * 48 : (a + 1) * 48, :] = picked[g * 48 : (g + 1) * 48, :]

        size = size_ref[...]
        stiff = stiff_ref[...]
        yields = yield_ref[...]
        rate8 = jnp.broadcast_to(rate_ref[...], (8, block))
        inverse = 1.0 / yields
        weight = stiff * (2.0 / size) * inverse
        shear8 = jnp.broadcast_to(weight * SHEAR, (8, block))
        shear28 = shear8 * 2.0
        lame8 = jnp.broadcast_to(weight * LAME, (8, block))
        slot = lax.broadcasted_iota(jnp.int32, (1, block), 1) + step * block
        live = (slot < counts_ref[0]).astype(F32)
        scale = size * size * 0.25 * live * yields
        state = [stress_ref[c * 8 : (c + 1) * 8, :] * inverse for c in range(6)]
        deltas = [dot(strain_ref[...], gathered[g]) for g in range(groups)]
        for g in range(groups):
            delta = deltas[g]
            for m in range(GROUP):
                d = [delta[m * 48 + c * 8 : m * 48 + c * 8 + 8, :] for c in range(6)]
                volume = (d[0] + d[1] + d[2]) * lame8
                for c in range(6):
                    rise = d[c] * shear28 + volume if c < 3 else d[c] * shear8
                    state[c] = state[c] + rise - rate8 * jnp.tanh(state[c])
                stresses[g, m * 48 : (m + 1) * 48, :] = jnp.concatenate(state, axis=0).astype(BF16)
            pushed = dot(force_ref[...], stresses[g]) * scale
            if g % 2 == 0:
                before = pushed
                continue
            for a in range(8):
                rows = slice(a * 24, (a + 1) * 24)
                both = jnp.concatenate([before[rows, :], pushed[rows, :]], axis=0)
                page = lax.shift_right_logical(conn_ref[a : a + 1, :], 8)
                for t in range(pages):
                    at_row = t * 3 * TIMES + (g - 1) * 24
                    forces[at_row : at_row + 48, a * block : (a + 1) * block] = jnp.where(
                        page == t, both, 0.0
                    ).astype(BF16)
        stress_out[...] = jnp.concatenate(state, axis=0) * (yields * live)
        rows = total.shape[0] // 2
        for half in (slice(0, rows), slice(rows, 2 * rows)):
            total[half, :] += dot(forces[half, :], folded[...])


def node_forces(total_ref, an_hi_ref, an_lo_ref, page):
    rows = 3 * TIMES
    total = jnp.transpose(total_ref[page * rows : (page + 1) * rows, :])
    high = total.astype(BF16)
    low = (total - high.astype(F32)).astype(BF16)
    return dot(high, an_hi_ref[...]) + dot(high, an_lo_ref[...]) + dot(low, an_hi_ref[...])


def element_update(inner, tail, conn_t, count, params, stress_zero, fold=256, block=512):
    elems = conn_t.shape[1]
    width = inner.shape[0]
    padded = inner.shape[1] + tail.shape[0]
    synth, _, strain, force = host_tables(width // 3)
    synth_hi, synth_lo = two_parts(synth)
    strain = jnp.asarray(strain, BF16)
    force = jnp.asarray(force, BF16)
    whole = lambda x: pl.BlockSpec(x.shape, lambda s: (0,) * x.ndim)
    by_block = lambda r: pl.BlockSpec((r, block), lambda s: (0, s))
    return pl.pallas_call(
        element_kernel,
        grid=(elems // block,),
        out_shape=(
            jax.ShapeDtypeStruct(stress_zero.shape, F32),
            jax.ShapeDtypeStruct((padded // fold * 3 * TIMES, fold), F32),
        ),
        in_specs=[
            pl.BlockSpec(memory_space=pltpu.SMEM),
            whole(inner), whole(tail), by_block(8), by_block(1), by_block(1), by_block(1), by_block(1), by_block(48),
            whole(synth_hi), whole(synth_lo),
            whole(strain), whole(force),
        ],
        out_specs=(by_block(48), pl.BlockSpec((padded // fold * 3 * TIMES, fold), lambda s: (0, 0))),
        scratch_shapes=[
            pltpu.VMEM((6 * TIMES, padded), BF16),
            pltpu.VMEM((padded, 8 * block), BF16),
            pltpu.VMEM((8 * block, fold), BF16),
            pltpu.VMEM((TIMES // GROUP, GROUP * 48, block), BF16),
            pltpu.VMEM((TIMES // GROUP, GROUP * 48, block), BF16),
            pltpu.VMEM((padded // fold * 3 * TIMES, 8 * block), BF16),
        ],
        compiler_params=pltpu.CompilerParams(
            vmem_limit_bytes=28 * 1024 * 1024, dimension_semantics=("arbitrary",)
        ),
        cost_estimate=pl.CostEstimate(flops=25000000000, bytes_accessed=4000000, transcendentals=0),
        name="elements",
    )(count, inner, tail, conn_t, *params, stress_zero, synth_hi, synth_lo, strain, force)


MESH = pl.DeviceIdType.MESH


def pair_hits(map_ref, rows):
    neighbours, slots = map_ref.shape
    listed = jnp.concatenate([map_ref[j : j + 1, :] for j in range(neighbours)], axis=1)
    iota = lax.broadcasted_iota(jnp.int32, (rows, neighbours * slots), 0)
    return (iota == listed).astype(F32)


def send(src, dst, send_sem, recv_sem, peer):
    copy = pltpu.make_async_remote_copy(
        src_ref=src, dst_ref=dst, send_sem=send_sem, recv_sem=recv_sem,
        device_id=peer, device_id_type=MESH,
    )
    copy.start()
    return copy


def halo_kernel(dom, offsets, int_far, if_far, map_far, tail_out, int_ref, if_ref, map_ref, out_block, in_block, fetch_sem, send_sem, recv_sem):
    me = lax.axis_index("dom")
    near = [{"dom": lax.rem(me + off + dom, dom)} for off in offsets]
    fetches = [
        pltpu.make_async_copy(src, dst, fetch_sem.at[n])
        for n, (src, dst) in enumerate(((map_far, map_ref), (if_far, if_ref), (int_far, int_ref)))
    ]
    for fetch in fetches:
        fetch.start()
    barrier = pltpu.get_barrier_semaphore()
    for peer in near:
        pl.semaphore_signal(barrier, inc=1, device_id=peer, device_id_type=MESH)
    width, int_nodes = int_ref.shape
    if_nodes = if_ref.shape[0]
    slots = map_ref.shape[1]
    fetches[0].wait()
    hits = jnp.transpose(pair_hits(map_ref, int_nodes + if_nodes)).astype(BF16)
    fetches[1].wait()
    fetches[2].wait()
    picked = (
        dot_t(hits[:, :int_nodes], int_ref[...]) + dot(hits[:, int_nodes:], if_ref[...])
    ).astype(BF16)
    for j in range(len(offsets)):
        out_block[j] = picked[j * slots : (j + 1) * slots]
    pl.semaphore_wait(barrier, len(near))
    copies = [
        send(out_block.at[j], in_block.at[j], send_sem.at[j], recv_sem.at[j], near[j])
        for j in range(len(offsets))
    ]
    for copy in copies:
        copy.wait()
    parts = [if_ref[...].astype(F32)] + [in_block[j].astype(F32) for j in range(len(offsets))]
    fill = tail_out.shape[0] - if_nodes - len(offsets) * slots
    tail_out[...] = jnp.concatenate(parts + [jnp.zeros((fill, width), F32)], axis=0).astype(BF16)


def halo(u_int_t, u_if, send_map, offsets, dom):
    neighbours, slots = send_map.shape
    width, int_nodes = u_int_t.shape
    used = int_nodes + u_if.shape[0] + neighbours * slots
    padded = -(-used // 256) * 256
    vmem = pl.BlockSpec(memory_space=pltpu.VMEM)
    return pl.pallas_call(
        functools.partial(halo_kernel, dom, offsets),
        out_shape=jax.ShapeDtypeStruct((padded - int_nodes, width), BF16),
        in_specs=[pl.BlockSpec(memory_space=pltpu.HBM)] * 3,
        out_specs=vmem,
        scratch_shapes=[
            pltpu.VMEM(u_int_t.shape, BF16),
            pltpu.VMEM(u_if.shape, BF16),
            pltpu.VMEM(send_map.shape, jnp.int32),
            pltpu.VMEM((neighbours, slots, width), BF16),
            pltpu.VMEM((neighbours, slots, width), BF16),
            pltpu.SemaphoreType.DMA((3,)),
            pltpu.SemaphoreType.DMA((neighbours,)),
            pltpu.SemaphoreType.DMA((neighbours,)),
        ],
        compiler_params=pltpu.CompilerParams(
            collective_id=0, has_side_effects=True, vmem_limit_bytes=56 * 1024 * 1024
        ),
        cost_estimate=pl.CostEstimate(flops=6000000000, bytes_accessed=1000000, transcendentals=0),
        name="halo",
    )(u_int_t, u_if, send_map)


def finish_kernel(
    sizes, offsets, stop,
    total_ref, an_hi_ref, an_lo_ref, map_ref, load_int_ref, load_if_ref, kinv, sinv_t,
    du_int_ref, du_if_ref,
    sinv, out_ret, in_ret, spread, spread_if, rhs_int,
    out_grp, in_grp, flat,
    own1, out1, in1, out2, in2, own3, out3, in3, last,
    ret_sem, grp_sem, sem1, sem2, sem3,
):
    zs, xs, cores, grps = sizes
    started = []

    def launch(*where):
        started.append(send(*where))
        return started[-1]

    dom = zs * xs * cores
    me = lax.axis_index("dom")
    my_grp = lax.axis_index("grp")
    core = lax.rem(me, cores)
    x = lax.rem(me // cores, xs)
    z = me // (cores * xs)
    at = lambda zz, xx, cc: {"dom": (zz * xs + xx) * cores + cc}
    owners = [{"dom": lax.rem(me - off + dom, dom)} for off in offsets]
    groups = [{"grp": lax.rem(my_grp + s, grps)} for s in range(1, grps)]
    sibling = at(z, x, 1 - core)
    along_x = [at(z, lax.rem(x + s, xs), core) for s in range(1, xs)]
    along_z = [at(lax.rem(z + s, zs), x, core) for s in range(1, zs)]
    neighbours, slots = map_ref.shape
    width, int_nodes = load_int_ref.shape
    if_nodes = load_if_ref.shape[0]
    fourier = width // 3
    owned = int_nodes + if_nodes
    peers = owners + groups + [sibling] + along_x + along_z
    barrier = pltpu.get_barrier_semaphore()
    for peer in peers:
        pl.semaphore_signal(barrier, inc=1, device_id=peer, device_id_type=MESH)
    fold = total_ref.shape[1]
    inner = int_nodes // fold
    outer = node_forces(total_ref, an_hi_ref, an_lo_ref, inner)
    for j in range(neighbours):
        out_ret[j] = outer[if_nodes + j * slots : if_nodes + (j + 1) * slots]
    pl.semaphore_wait(barrier, len(peers))
    copies = [
        launch(out_ret.at[j], in_ret.at[j], ret_sem.at[0, j], ret_sem.at[1, j], owners[j])
        for j in range(neighbours)
    ]
    hits = pair_hits(map_ref, owned).astype(BF16)
    own = jnp.concatenate(
        [node_forces(total_ref, an_hi_ref, an_lo_ref, page) for page in range(inner)]
        + [outer[:if_nodes]],
        axis=0,
    )
    load_int = jnp.transpose(load_int_ref[...])
    strip = 384
    for c in range(sinv.shape[0] // strip):
        sinv[c * strip : (c + 1) * strip, :] = jnp.transpose(sinv_t[:, c * strip : (c + 1) * strip])
    for copy in copies:
        copy.wait_recv()
    back = jnp.concatenate([in_ret[j] for j in range(neighbours)], axis=0)
    high = back.astype(BF16)
    low = (back - high.astype(F32)).astype(BF16)
    force = own + dot(hits, high) + dot(hits, low)
    shared = force[int_nodes:]
    out_grp[...] = jnp.concatenate(
        [shared, jnp.zeros((out_grp.shape[0] - if_nodes, width), F32)], axis=0
    ).astype(BF16)
    copies = [
        launch(out_grp, in_grp.at[s], grp_sem.at[0, s], grp_sem.at[1, s], peer)
        for s, peer in enumerate(groups)
    ]
    r_int = load_int - force[:int_nodes]
    for i in range(3):
        spread[pl.ds(i, int_nodes, stride=3), :] = r_int[:, i * fourier : (i + 1) * fourier]
    rhs_int[...] = spread[...].astype(BF16)
    chunk = 256
    chunks = kinv.shape[0] // chunk

    def solve(c, _):
        rows = pl.ds(pl.multiple_of(c * chunk, chunk), chunk)
        spread[rows, :] = dot(kinv[rows, :], rhs_int[...])
        return 0

    lax.fori_loop(0, 3, solve, 0)
    for s, copy in enumerate(copies):
        copy.wait_recv()
        shared = shared + in_grp[s][:if_nodes].astype(F32)
    gathered = (load_if_ref[...] - shared).astype(BF16).astype(F32)
    for i in range(3):
        spread_if[pl.ds(i, if_nodes, stride=3), :] = gathered[:, i * fourier : (i + 1) * fourier]
    rhs_if = spread_if[...]
    empty = jnp.zeros_like(rhs_if)
    left = jnp.concatenate([rhs_if, empty], axis=1).astype(BF16)
    right = jnp.concatenate([empty, rhs_if], axis=1).astype(BF16)
    half = zs // 2
    parts = out1.shape[0]
    each = half // parts
    per_owner = sinv.shape[0] // dom
    per_z = per_owner * xs * cores
    fill = jnp.zeros((out1.shape[2] - each * per_owner, 2 * fourier), F32)
    first_copies = []
    for c in range(parts):
        first_copies.append([])
        for j in range(each):
            start = pl.multiple_of(lax.rem(z + c * each + j + 1, half) * per_z, 16)
            other = pl.multiple_of(start + half * per_z, 16)
            flat[(c * each + j) * per_z : (c * each + j + 1) * per_z, :] = dot(
                sinv[pl.ds(start, per_z), :], left
            ) + dot(sinv[pl.ds(other, per_z), :], right)
        for k in range(xs):
            by_core = []
            for cc in range(cores):
                rows = []
                for j in range(each):
                    at_row = (c * each + j) * per_z + (k * cores + cc) * per_owner
                    rows.append(flat[at_row : at_row + per_owner, :])
                by_core.append(jnp.concatenate(rows + [fill], axis=0))
            own1[c, k] = jnp.where(core == 0, by_core[0], by_core[1])
            out1[c, k] = jnp.where(core == 0, by_core[1], by_core[0]).astype(BF16)
            first_copies[c].append(
                launch(out1.at[c, k], in1.at[c, k], sem1.at[0, c, k], sem1.at[1, c, k], sibling)
            )
    second_copies = []
    for c in range(parts):
        for k in range(xs):
            first_copies[c][k].wait_recv()
            summed = own1[c, k] + in1[c, k].astype(F32)
            own1[c, k] = summed
            out2[c, k] = summed.astype(BF16)
        second_copies.append([
            launch(out2.at[c, lax.rem(x + s + 1, xs)], in2.at[c, s], sem2.at[0, c, s], sem2.at[1, c, s], peer)
            for s, peer in enumerate(along_x)
        ])
    lax.fori_loop(3, chunks, solve, 0)
    short = per_owner // 2
    first = lax.broadcasted_iota(jnp.int32, (short, 2 * fourier), 1) < fourier
    fill = jnp.zeros((out3.shape[3] - short, 2 * fourier), F32)
    third_copies = []
    for c in range(parts):
        summed = own1[c, x]
        for s, copy in enumerate(second_copies[c]):
            copy.wait_recv()
            summed = summed + in2[c, s].astype(F32)
        turned = pltpu.roll(summed, fourier, 1)
        for j in range(each):
            top = slice(j * per_owner, j * per_owner + short)
            low_rows = slice(j * per_owner + short, (j + 1) * per_owner)
            o = c * each + j + 1
            for h, (a, b) in enumerate(((summed, turned), (turned, summed))):
                block = jnp.concatenate([jnp.where(first, a[top], b[low_rows]), fill], axis=0)
                if o == half:
                    own3[h] = block
                out3[c, j, h] = block.astype(BF16)
            for s in (o, o + half):
                if s < zs:
                    target = lax.rem(z + s, zs)
                    third_copies.append(launch(
                        out3.at[c, j, target // half], in3.at[s - 1],
                        sem3.at[0, s - 1], sem3.at[1, s - 1], along_z[s - 1],
                    ))
    for i in range(3):
        du_int_ref[i * fourier : (i + 1) * fourier, :] = jnp.transpose(
            spread[pl.ds(i, int_nodes, stride=3), :]
        )
    for copy in third_copies:
        copy.wait_recv()
    summed = own3[z // half]
    for s in range(zs - 1):
        summed = summed + in3[s].astype(F32)
    last[0] = summed
    last[1] = pltpu.roll(summed, fourier, 1)
    nodes = short // 3
    for h in range(2):
        for i in range(3):
            du_if_ref[h * nodes : (h + 1) * nodes, i * fourier : (i + 1) * fourier] = last[
                h, pl.ds(i, nodes, stride=3), :
            ][:, :fourier]
    for copy in started:
        copy.wait_send()


def finish(total, send_map, load_int_t, load_if, kinv_int, sinv_t, offsets, sizes, stop=99):
    zs, xs, cores, grps = sizes
    neighbours, slots = send_map.shape
    width, int_nodes = load_int_t.shape
    sinv_rows = sinv_t.shape[1]
    if_nodes = load_if.shape[0]
    fourier = width // 3
    dom = zs * xs * cores
    per_owner = sinv_rows // dom
    up = lambda n, k: -(-n // k) * k
    share = up(if_nodes, 16)
    parts = 2
    each = zs // 2 // parts
    rows1 = up(per_owner * each, 16)
    rows3 = up(per_owner // 2, 16)
    vmem = pl.BlockSpec(memory_space=pltpu.VMEM)
    sems = pltpu.SemaphoreType.DMA
    lanes = 2 * fourier
    an_hi, an_lo = two_parts(host_tables(fourier)[1])
    return pl.pallas_call(
        functools.partial(finish_kernel, sizes, offsets, stop),
        out_shape=(
            jax.ShapeDtypeStruct((width, int_nodes), F32),
            jax.ShapeDtypeStruct((per_owner // 3, width), F32),
        ),
        in_specs=[vmem] * 8,
        out_specs=(vmem, vmem),
        scratch_shapes=[
            pltpu.VMEM((sinv_rows, sinv_t.shape[0]), BF16),
            pltpu.VMEM((neighbours, slots, width), F32),
            pltpu.VMEM((neighbours, slots, width), F32),
            pltpu.VMEM((3 * int_nodes, fourier), F32),
            pltpu.VMEM((3 * if_nodes, fourier), F32),
            pltpu.VMEM((3 * int_nodes, fourier), BF16),
            pltpu.VMEM((share, width), BF16),
            pltpu.VMEM((grps - 1, share, width), BF16),
            pltpu.VMEM((sinv_rows // 2, lanes), F32),
            pltpu.VMEM((parts, xs, rows1, lanes), F32),
            pltpu.VMEM((parts, xs, rows1, lanes), BF16),
            pltpu.VMEM((parts, xs, rows1, lanes), BF16),
            pltpu.VMEM((parts, xs, rows1, lanes), BF16),
            pltpu.VMEM((parts, xs - 1, rows1, lanes), BF16),
            pltpu.VMEM((2, rows3, lanes), F32),
            pltpu.VMEM((parts, each, 2, rows3, lanes), BF16),
            pltpu.VMEM((zs - 1, rows3, lanes), BF16),
            pltpu.VMEM((2, rows3, lanes), F32),
            sems((2, neighbours)), sems((2, grps - 1)),
            sems((2, parts, xs)), sems((2, parts, xs - 1)), sems((2, zs - 1)),
        ],
        compiler_params=pltpu.CompilerParams(
            collective_id=1, has_side_effects=True, vmem_limit_bytes=20 * 1024 * 1024
        ),
        cost_estimate=pl.CostEstimate(flops=20000000000, bytes_accessed=9000000, transcendentals=0),
        name="finish",
    )(total, an_hi, an_lo, send_map, load_int_t, load_if, kinv_int, sinv_t)


def per_device(
    u_int, u_if, load_int, load_if, conn, send_map, counts, elem_size, stiffness,
    yield_stress, relax_rate, stress_init, kinv_int, sinv,
):
    reach = send_map.shape[0] // 2
    offsets = list(range(-reach, 0)) + list(range(1, reach + 1))
    dom, grps = lax.axis_size("dom"), lax.axis_size("grp")
    sizes = (dom // 8, 4, 2, grps)
    u_int_t, conn_t = jnp.transpose(u_int), jnp.transpose(conn)
    tail = halo(u_int_t, u_if, send_map, offsets, dom)
    params = [v.reshape(1, -1) for v in (elem_size, stiffness, yield_stress, relax_rate)]
    stress_end, force = element_update(u_int_t, tail, conn_t, counts, params, stress_init)
    du_int_t, du_if = finish(
        force, send_map, jnp.transpose(load_int), load_if, kinv_int, jnp.transpose(sinv), offsets, sizes
    )
    return (jnp.transpose(du_int_t), du_if, stress_end)


def solution(mesh):
    both = ("grp", "dom")
    return jax.shard_map(
        per_device,
        mesh=mesh,
        in_specs=(
            P(both, None), P("dom", None), P(both, None), P("dom", None), P(both, None),
            P(both, None), P(both), P(both), P(both), P(both), P(both), P(None, both),
            P(both, None), P("grp", "dom"),
        ),
        out_specs=(P(both, None), P(both, None), P(None, both)),
        check_vma=False,
    )
```

```python
import functools
import math

import jax
import jax.numpy as jnp
import numpy as np
from jax import lax
from jax.experimental import pallas as pl
from jax.experimental.pallas import tpu as pltpu
from jax.sharding import PartitionSpec as P

TIMES = 32
GROUP = 8
POISSON = 0.3
BF16 = jnp.bfloat16
F32 = jnp.float32


def strain_table():
    gauss = 1.0 / math.sqrt(3.0)
    table = np.zeros((6, 8, 8, 3))
    for point in range(8):
        coords = [((point >> bit & 1) * 2 - 1) * gauss for bit in range(3)]
        for corner in range(8):
            signs = [(corner >> bit & 1) * 2 - 1 for bit in range(3)]
            deriv = []
            for axis in range(3):
                value = signs[axis] / 8.0
                for other in range(3):
                    if other != axis:
                        value = value * (1.0 + signs[other] * coords[other])
                deriv.append(value)
            table[0, point, corner, 0] = deriv[0]
            table[1, point, corner, 1] = deriv[1]
            table[2, point, corner, 2] = deriv[2]
            table[3, point, corner, 0] = deriv[1]
            table[3, point, corner, 1] = deriv[0]
            table[4, point, corner, 1] = deriv[2]
            table[4, point, corner, 2] = deriv[1]
            table[5, point, corner, 2] = deriv[0]
            table[5, point, corner, 0] = deriv[2]
    return np.asarray(np.asarray(table.reshape(48, 24), np.float32), BF16).astype(np.float64)


def time_tables(times, fourier):
    theta = 2.0 * math.pi * (np.arange(times) + 0.3) / times
    synthesis = np.zeros((fourier, times))
    for column in range(fourier):
        harmonic = column // 2
        if column % 2 == 0:
            synthesis[column] = np.cos(harmonic * theta)
        else:
            synthesis[column] = np.sin((harmonic + 1) * theta)
    analysis = synthesis.T * (2.0 / times)
    analysis[:, 0] = 1.0 / times
    return synthesis.astype(np.float32).astype(np.float64), analysis.astype(np.float32).astype(np.float64)


def two_parts(x):
    high = np.asarray(x, np.float32).astype(BF16)
    low = (np.asarray(x, np.float64) - high.astype(np.float64)).astype(BF16)
    return jnp.asarray(high), jnp.asarray(low)


@functools.lru_cache(None)
def host_tables(fourier):
    table = strain_table()
    synthesis, analysis = time_tables(TIMES, fourier)
    groups = TIMES // GROUP
    steps = synthesis - np.roll(synthesis, 1, axis=1)
    synth = np.zeros((groups, 3, GROUP, 3, fourier))
    analyse = np.zeros((groups, 3, GROUP, 3, fourier))
    for g in range(groups):
        for i in range(3):
            for m in range(GROUP):
                synth[g, i, m, i] = steps[:, g * GROUP + m]
                analyse[g, i, m, i] = analysis[g * GROUP + m]
    strain = np.zeros((GROUP, 48, 8, 3, 2, GROUP))
    force = np.zeros((8, 3, GROUP, GROUP, 48))
    shaped = table.reshape(48, 8, 3)
    for m in range(GROUP):
        for part in range(2):
            strain[m, :, :, :, part, m] = shaped
        force[:, :, m, m, :] = np.transpose(shaped, (1, 2, 0))
    width = 3 * fourier
    return (
        synth.reshape(TIMES * 3, width),
        analyse.reshape(TIMES * 3, width),
        strain.reshape(GROUP * 48, GROUP * 48),
        force.reshape(GROUP * 24, GROUP * 48),
    )


def split_rows(x):
    rows, n = x.shape
    high = x.astype(BF16).astype(F32)
    low = x - high
    parts = jnp.concatenate(
        [high.reshape(rows // 8, 1, 8, n), low.reshape(rows // 8, 1, 8, n)], axis=1
    )
    return parts.reshape(rows * 2, n).astype(BF16)


def dot(a, b):
    return lax.dot_general(a, b, (((1,), (0,)), ((), ())), preferred_element_type=F32)


def dot_t(a, b):
    return lax.dot_general(a, b, (((1,), (1,)), ((), ())), preferred_element_type=F32)


LAME = POISSON / ((1.0 + POISSON) * (1.0 - 2.0 * POISSON))
SHEAR = 1.0 / (2.0 * (1.0 + POISSON))


def element_kernel(
    counts_ref, int_ref, tail_ref, conn_ref, size_ref, stiff_ref, yield_ref, rate_ref, stress_ref,
    synth_hi_ref, synth_lo_ref, strain_ref, force_ref,
    stress_out, total,
    nodal, onehot, folded, gathered, stresses, forces,
):
    step = pl.program_id(0)
    block = conn_ref.shape[1]
    nodes = nodal.shape[1]
    groups = TIMES // GROUP

    @pl.when(step == 0)
    def _():
        inner, tail = int_ref[...], tail_ref[...]
        first = inner.shape[1]
        high, low = synth_hi_ref[...], synth_lo_ref[...]
        nodal[:, :first] = split_rows(dot(high, inner) + dot(low, inner))
        nodal[:, first:] = split_rows(dot_t(high, tail) + dot_t(low, tail))
        total[...] = jnp.zeros_like(total)

    fold = total.shape[1]
    pages = total.shape[0] // (3 * TIMES)
    listed = jnp.transpose(conn_ref[...])
    lane = lax.broadcasted_iota(jnp.int32, (block, fold), 1)
    iota = lax.broadcasted_iota(jnp.int16, (nodes, block), 0)
    for a in range(8):
        index = conn_ref[a : a + 1, :].astype(jnp.int16)
        hit = iota == jnp.broadcast_to(index, (nodes, block))
        onehot[:, a * block : (a + 1) * block] = jnp.where(
            hit, jnp.ones((), BF16), jnp.zeros((), BF16)
        )
        place = jnp.broadcast_to((listed[:, a : a + 1] & (fold - 1)), (block, fold))
        folded[a * block : (a + 1) * block, :] = (place == lane).astype(F32).astype(BF16)
    table = nodal[...]
    for a in range(8):
        picked = dot(table, onehot[:, a * block : (a + 1) * block]).astype(BF16)
        for g in range(groups):
            gathered[g, a * 48 : (a + 1) * 48, :] = picked[g * 48 : (g + 1) * 48, :]

    size = size_ref[...]
    stiff = stiff_ref[...]
    yields = yield_ref[...]
    rate8 = jnp.broadcast_to(rate_ref[...], (8, block))
    inverse = 1.0 / yields
    weight = stiff * (2.0 / size) * inverse
    shear8 = jnp.broadcast_to(weight * SHEAR, (8, block))
    shear28 = shear8 * 2.0
    lame8 = jnp.broadcast_to(weight * LAME, (8, block))
    slot = lax.broadcasted_iota(jnp.int32, (1, block), 1) + step * block
    live = (slot < counts_ref[0]).astype(F32)
    scale = size * size * 0.25 * live * yields
    state = [stress_ref[c * 8 : (c + 1) * 8, :] * inverse for c in range(6)]
    deltas = [dot(strain_ref[...], gathered[g]) for g in range(groups)]
    for g in range(groups):
        delta = deltas[g]
        for m in range(GROUP):
            d = [delta[m * 48 + c * 8 : m * 48 + c * 8 + 8, :] for c in range(6)]
            volume = (d[0] + d[1] + d[2]) * lame8
            for c in range(6):
                rise = d[c] * shear28 + volume if c < 3 else d[c] * shear8
                state[c] = state[c] + rise - rate8 * jnp.tanh(state[c])
            stresses[g, m * 48 : (m + 1) * 48, :] = jnp.concatenate(state, axis=0).astype(BF16)
        pushed = dot(force_ref[...], stresses[g]) * scale
        if g % 2 == 0:
            before = pushed
            continue
        for a in range(8):
            rows = slice(a * 24, (a + 1) * 24)
            both = jnp.concatenate([before[rows, :], pushed[rows, :]], axis=0)
            page = lax.shift_right_logical(conn_ref[a : a + 1, :], 8)
            for t in range(pages):
                at_row = t * 3 * TIMES + (g - 1) * 24
                forces[at_row : at_row + 48, a * block : (a + 1) * block] = jnp.where(
                    page == t, both, 0.0
                ).astype(BF16)
    stress_out[...] = jnp.concatenate(state, axis=0) * (yields * live)
    rows = total.shape[0] // 2
    for half in (slice(0, rows), slice(rows, 2 * rows)):
        total[half, :] += dot(forces[half, :], folded[...])


def node_forces(total_ref, an_hi_ref, an_lo_ref, page):
    rows = 3 * TIMES
    total = jnp.transpose(total_ref[page * rows : (page + 1) * rows, :])
    high = total.astype(BF16)
    low = (total - high.astype(F32)).astype(BF16)
    return dot(high, an_hi_ref[...]) + dot(high, an_lo_ref[...]) + dot(low, an_hi_ref[...])


def element_update(inner, tail, conn_t, count, params, stress_zero, fold=256, block=512):
    elems = conn_t.shape[1]
    width = inner.shape[0]
    padded = inner.shape[1] + tail.shape[0]
    synth, _, strain, force = host_tables(width // 3)
    synth_hi, synth_lo = two_parts(synth)
    strain = jnp.asarray(strain, BF16)
    force = jnp.asarray(force, BF16)
    whole = lambda x: pl.BlockSpec(x.shape, lambda s: (0,) * x.ndim)
    by_block = lambda r: pl.BlockSpec((r, block), lambda s: (0, s))
    return pl.pallas_call(
        element_kernel,
        grid=(elems // block,),
        out_shape=(
            jax.ShapeDtypeStruct(stress_zero.shape, F32),
            jax.ShapeDtypeStruct((padded // fold * 3 * TIMES, fold), F32),
        ),
        in_specs=[
            pl.BlockSpec(memory_space=pltpu.SMEM),
            whole(inner), whole(tail), by_block(8), by_block(1), by_block(1), by_block(1), by_block(1), by_block(48),
            whole(synth_hi), whole(synth_lo),
            whole(strain), whole(force),
        ],
        out_specs=(by_block(48), pl.BlockSpec((padded // fold * 3 * TIMES, fold), lambda s: (0, 0))),
        scratch_shapes=[
            pltpu.VMEM((6 * TIMES, padded), BF16),
            pltpu.VMEM((padded, 8 * block), BF16),
            pltpu.VMEM((8 * block, fold), BF16),
            pltpu.VMEM((TIMES // GROUP, GROUP * 48, block), BF16),
            pltpu.VMEM((TIMES // GROUP, GROUP * 48, block), BF16),
            pltpu.VMEM((padded // fold * 3 * TIMES, 8 * block), BF16),
        ],
        compiler_params=pltpu.CompilerParams(
            vmem_limit_bytes=28 * 1024 * 1024, dimension_semantics=("arbitrary",)
        ),
        cost_estimate=pl.CostEstimate(flops=25000000000, bytes_accessed=4000000, transcendentals=0),
        name="elements",
    )(count, inner, tail, conn_t, *params, stress_zero, synth_hi, synth_lo, strain, force)


MESH = pl.DeviceIdType.MESH


def pair_hits(map_ref, rows):
    neighbours, slots = map_ref.shape
    listed = jnp.concatenate([map_ref[j : j + 1, :] for j in range(neighbours)], axis=1)
    iota = lax.broadcasted_iota(jnp.int32, (rows, neighbours * slots), 0)
    return (iota == listed).astype(F32)


def send(src, dst, send_sem, recv_sem, peer):
    copy = pltpu.make_async_remote_copy(
        src_ref=src, dst_ref=dst, send_sem=send_sem, recv_sem=recv_sem,
        device_id=peer, device_id_type=MESH,
    )
    copy.start()
    return copy


def halo_kernel(dom, offsets, int_far, if_far, map_far, tail_out, int_ref, if_ref, map_ref, out_block, in_block, fetch_sem, send_sem, recv_sem):
    me = lax.axis_index("dom")
    near = [{"dom": lax.rem(me + off + dom, dom)} for off in offsets]
    fetches = [
        pltpu.make_async_copy(src, dst, fetch_sem.at[n])
        for n, (src, dst) in enumerate(((map_far, map_ref), (if_far, if_ref), (int_far, int_ref)))
    ]
    for fetch in fetches:
        fetch.start()
    barrier = pltpu.get_barrier_semaphore()
    for peer in near:
        pl.semaphore_signal(barrier, inc=1, device_id=peer, device_id_type=MESH)
    width, int_nodes = int_ref.shape
    if_nodes = if_ref.shape[0]
    slots = map_ref.shape[1]
    fetches[0].wait()
    hits = jnp.transpose(pair_hits(map_ref, int_nodes + if_nodes)).astype(BF16)
    fetches[1].wait()
    fetches[2].wait()
    picked = (
        dot_t(hits[:, :int_nodes], int_ref[...]) + dot(hits[:, int_nodes:], if_ref[...])
    ).astype(BF16)
    for j in range(len(offsets)):
        out_block[j] = picked[j * slots : (j + 1) * slots]
    pl.semaphore_wait(barrier, len(near))
    copies = [
        send(out_block.at[j], in_block.at[j], send_sem.at[j], recv_sem.at[j], near[j])
        for j in range(len(offsets))
    ]
    for copy in copies:
        copy.wait()
    parts = [if_ref[...].astype(F32)] + [in_block[j].astype(F32) for j in range(len(offsets))]
    fill = tail_out.shape[0] - if_nodes - len(offsets) * slots
    tail_out[...] = jnp.concatenate(parts + [jnp.zeros((fill, width), F32)], axis=0).astype(BF16)


def halo(u_int_t, u_if, send_map, offsets, dom):
    neighbours, slots = send_map.shape
    width, int_nodes = u_int_t.shape
    used = int_nodes + u_if.shape[0] + neighbours * slots
    padded = -(-used // 256) * 256
    vmem = pl.BlockSpec(memory_space=pltpu.VMEM)
    return pl.pallas_call(
        functools.partial(halo_kernel, dom, offsets),
        out_shape=jax.ShapeDtypeStruct((padded - int_nodes, width), BF16),
        in_specs=[pl.BlockSpec(memory_space=pltpu.HBM)] * 3,
        out_specs=vmem,
        scratch_shapes=[
            pltpu.VMEM(u_int_t.shape, BF16),
            pltpu.VMEM(u_if.shape, BF16),
            pltpu.VMEM(send_map.shape, jnp.int32),
            pltpu.VMEM((neighbours, slots, width), BF16),
            pltpu.VMEM((neighbours, slots, width), BF16),
            pltpu.SemaphoreType.DMA((3,)),
            pltpu.SemaphoreType.DMA((neighbours,)),
            pltpu.SemaphoreType.DMA((neighbours,)),
        ],
        compiler_params=pltpu.CompilerParams(
            collective_id=0, has_side_effects=True, vmem_limit_bytes=56 * 1024 * 1024
        ),
        cost_estimate=pl.CostEstimate(flops=6000000000, bytes_accessed=1000000, transcendentals=0),
        name="halo",
    )(u_int_t, u_if, send_map)


def finish_kernel(
    sizes, offsets, stop,
    total_ref, an_hi_ref, an_lo_ref, map_ref, load_int_ref, load_if_ref, kinv, sinv_t,
    du_int_ref, du_if_ref,
    sinv, out_ret, in_ret, spread, spread_if, rhs_int,
    out_grp, in_grp, flat,
    own1, out1, in1, out2, in2, own3, out3, in3, last,
    ret_sem, grp_sem, sem1, sem2, sem3,
):
    zs, xs, cores, grps = sizes
    started = []

    def launch(*where):
        started.append(send(*where))
        return started[-1]

    dom = zs * xs * cores
    me = lax.axis_index("dom")
    my_grp = lax.axis_index("grp")
    core = lax.rem(me, cores)
    x = lax.rem(me // cores, xs)
    z = me // (cores * xs)
    at = lambda zz, xx, cc: {"dom": (zz * xs + xx) * cores + cc}
    owners = [{"dom": lax.rem(me - off + dom, dom)} for off in offsets]
    groups = [{"grp": lax.rem(my_grp + s, grps)} for s in range(1, grps)]
    sibling = at(z, x, 1 - core)
    along_x = [at(z, lax.rem(x + s, xs), core) for s in range(1, xs)]
    along_z = [at(lax.rem(z + s, zs), x, core) for s in range(1, zs)]
    neighbours, slots = map_ref.shape
    width, int_nodes = load_int_ref.shape
    if_nodes = load_if_ref.shape[0]
    fourier = width // 3
    owned = int_nodes + if_nodes
    peers = owners + groups + [sibling] + along_x + along_z
    barrier = pltpu.get_barrier_semaphore()
    for peer in peers:
        pl.semaphore_signal(barrier, inc=1, device_id=peer, device_id_type=MESH)
    fold = total_ref.shape[1]
    inner = int_nodes // fold
    outer = node_forces(total_ref, an_hi_ref, an_lo_ref, inner)
    for j in range(neighbours):
        out_ret[j] = outer[if_nodes + j * slots : if_nodes + (j + 1) * slots]
    pl.semaphore_wait(barrier, len(peers))
    copies = [
        launch(out_ret.at[j], in_ret.at[j], ret_sem.at[0, j], ret_sem.at[1, j], owners[j])
        for j in range(neighbours)
    ]
    hits = pair_hits(map_ref, owned).astype(BF16)
    own = jnp.concatenate(
        [node_forces(total_ref, an_hi_ref, an_lo_ref, page) for page in range(inner)]
        + [outer[:if_nodes]],
        axis=0,
    )
    load_int = jnp.transpose(load_int_ref[...])
    strip = 384
    for c in range(sinv.shape[0] // strip):
        sinv[c * strip : (c + 1) * strip, :] = jnp.transpose(sinv_t[:, c * strip : (c + 1) * strip])
    for copy in copies:
        copy.wait_recv()
    back = jnp.concatenate([in_ret[j] for j in range(neighbours)], axis=0)
    high = back.astype(BF16)
    low = (back - high.astype(F32)).astype(BF16)
    force = own + dot(hits, high) + dot(hits, low)
    shared = force[int_nodes:]
    out_grp[...] = jnp.concatenate(
        [shared, jnp.zeros((out_grp.shape[0] - if_nodes, width), F32)], axis=0
    ).astype(BF16)
    copies = [
        launch(out_grp, in_grp.at[s], grp_sem.at[0, s], grp_sem.at[1, s], peer)
        for s, peer in enumerate(groups)
    ]
    r_int = load_int - force[:int_nodes]
    for i in range(3):
        spread[pl.ds(i, int_nodes, stride=3), :] = r_int[:, i * fourier : (i + 1) * fourier]
    rhs_int[...] = spread[...].astype(BF16)
    chunk = 256
    chunks = kinv.shape[0] // chunk

    def solve(c, _):
        rows = pl.ds(pl.multiple_of(c * chunk, chunk), chunk)
        spread[rows, :] = dot(kinv[rows, :], rhs_int[...])
        return 0

    lax.fori_loop(0, 3, solve, 0)
    for s, copy in enumerate(copies):
        copy.wait_recv()
        shared = shared + in_grp[s][:if_nodes].astype(F32)
    gathered = (load_if_ref[...] - shared).astype(BF16).astype(F32)
    for i in range(3):
        spread_if[pl.ds(i, if_nodes, stride=3), :] = gathered[:, i * fourier : (i + 1) * fourier]
    rhs_if = spread_if[...]
    empty = jnp.zeros_like(rhs_if)
    left = jnp.concatenate([rhs_if, empty], axis=1).astype(BF16)
    right = jnp.concatenate([empty, rhs_if], axis=1).astype(BF16)
    half = zs // 2
    parts = out1.shape[0]
    each = half // parts
    per_owner = sinv.shape[0] // dom
    per_z = per_owner * xs * cores
    fill = jnp.zeros((out1.shape[2] - each * per_owner, 2 * fourier), F32)
    first_copies = []
    for c in range(parts):
        first_copies.append([])
        for j in range(each):
            start = pl.multiple_of(lax.rem(z + c * each + j + 1, half) * per_z, 16)
            other = pl.multiple_of(start + half * per_z, 16)
            flat[(c * each + j) * per_z : (c * each + j + 1) * per_z, :] = dot(
                sinv[pl.ds(start, per_z), :], left
            ) + dot(sinv[pl.ds(other, per_z), :], right)
        for k in range(xs):
            by_core = []
            for cc in range(cores):
                rows = []
                for j in range(each):
                    at_row = (c * each + j) * per_z + (k * cores + cc) * per_owner
                    rows.append(flat[at_row : at_row + per_owner, :])
                by_core.append(jnp.concatenate(rows + [fill], axis=0))
            own1[c, k] = jnp.where(core == 0, by_core[0], by_core[1])
            out1[c, k] = jnp.where(core == 0, by_core[1], by_core[0]).astype(BF16)
            first_copies[c].append(
                launch(out1.at[c, k], in1.at[c, k], sem1.at[0, c, k], sem1.at[1, c, k], sibling)
            )
    second_copies = []
    for c in range(parts):
        for k in range(xs):
            first_copies[c][k].wait_recv()
            summed = own1[c, k] + in1[c, k].astype(F32)
            own1[c, k] = summed
            out2[c, k] = summed.astype(BF16)
        second_copies.append([
            launch(out2.at[c, lax.rem(x + s + 1, xs)], in2.at[c, s], sem2.at[0, c, s], sem2.at[1, c, s], peer)
            for s, peer in enumerate(along_x)
        ])
    lax.fori_loop(3, chunks, solve, 0)
    short = per_owner // 2
    first = lax.broadcasted_iota(jnp.int32, (short, 2 * fourier), 1) < fourier
    fill = jnp.zeros((out3.shape[3] - short, 2 * fourier), F32)
    third_copies = []
    for c in range(parts):
        summed = own1[c, x]
        for s, copy in enumerate(second_copies[c]):
            copy.wait_recv()
            summed = summed + in2[c, s].astype(F32)
        turned = pltpu.roll(summed, fourier, 1)
        for j in range(each):
            top = slice(j * per_owner, j * per_owner + short)
            low_rows = slice(j * per_owner + short, (j + 1) * per_owner)
            o = c * each + j + 1
            for h, (a, b) in enumerate(((summed, turned), (turned, summed))):
                block = jnp.concatenate([jnp.where(first, a[top], b[low_rows]), fill], axis=0)
                if o == half:
                    own3[h] = block
                out3[c, j, h] = block.astype(BF16)
            for s in (o, o + half):
                if s < zs:
                    target = lax.rem(z + s, zs)
                    third_copies.append(launch(
                        out3.at[c, j, target // half], in3.at[s - 1],
                        sem3.at[0, s - 1], sem3.at[1, s - 1], along_z[s - 1],
                    ))
    for i in range(3):
        du_int_ref[i * fourier : (i + 1) * fourier, :] = jnp.transpose(
            spread[pl.ds(i, int_nodes, stride=3), :]
        )
    for copy in third_copies:
        copy.wait_recv()
    summed = own3[z // half]
    for s in range(zs - 1):
        summed = summed + in3[s].astype(F32)
    last[0] = summed
    last[1] = pltpu.roll(summed, fourier, 1)
    nodes = short // 3
    for h in range(2):
        for i in range(3):
            du_if_ref[h * nodes : (h + 1) * nodes, i * fourier : (i + 1) * fourier] = last[
                h, pl.ds(i, nodes, stride=3), :
            ][:, :fourier]
    for copy in started:
        copy.wait_send()


def finish(total, send_map, load_int_t, load_if, kinv_int, sinv_t, offsets, sizes, stop=99):
    zs, xs, cores, grps = sizes
    neighbours, slots = send_map.shape
    width, int_nodes = load_int_t.shape
    sinv_rows = sinv_t.shape[1]
    if_nodes = load_if.shape[0]
    fourier = width // 3
    dom = zs * xs * cores
    per_owner = sinv_rows // dom
    up = lambda n, k: -(-n // k) * k
    share = up(if_nodes, 16)
    parts = 2
    each = zs // 2 // parts
    rows1 = up(per_owner * each, 16)
    rows3 = up(per_owner // 2, 16)
    vmem = pl.BlockSpec(memory_space=pltpu.VMEM)
    sems = pltpu.SemaphoreType.DMA
    lanes = 2 * fourier
    an_hi, an_lo = two_parts(host_tables(fourier)[1])
    return pl.pallas_call(
        functools.partial(finish_kernel, sizes, offsets, stop),
        out_shape=(
            jax.ShapeDtypeStruct((width, int_nodes), F32),
            jax.ShapeDtypeStruct((per_owner // 3, width), F32),
        ),
        in_specs=[vmem] * 8,
        out_specs=(vmem, vmem),
        scratch_shapes=[
            pltpu.VMEM((sinv_rows, sinv_t.shape[0]), BF16),
            pltpu.VMEM((neighbours, slots, width), F32),
            pltpu.VMEM((neighbours, slots, width), F32),
            pltpu.VMEM((3 * int_nodes, fourier), F32),
            pltpu.VMEM((3 * if_nodes, fourier), F32),
            pltpu.VMEM((3 * int_nodes, fourier), BF16),
            pltpu.VMEM((share, width), BF16),
            pltpu.VMEM((grps - 1, share, width), BF16),
            pltpu.VMEM((sinv_rows // 2, lanes), F32),
            pltpu.VMEM((parts, xs, rows1, lanes), F32),
            pltpu.VMEM((parts, xs, rows1, lanes), BF16),
            pltpu.VMEM((parts, xs, rows1, lanes), BF16),
            pltpu.VMEM((parts, xs, rows1, lanes), BF16),
            pltpu.VMEM((parts, xs - 1, rows1, lanes), BF16),
            pltpu.VMEM((2, rows3, lanes), F32),
            pltpu.VMEM((parts, each, 2, rows3, lanes), BF16),
            pltpu.VMEM((zs - 1, rows3, lanes), BF16),
            pltpu.VMEM((2, rows3, lanes), F32),
            sems((2, neighbours)), sems((2, grps - 1)),
            sems((2, parts, xs)), sems((2, parts, xs - 1)), sems((2, zs - 1)),
        ],
        compiler_params=pltpu.CompilerParams(
            collective_id=1, has_side_effects=True, vmem_limit_bytes=20 * 1024 * 1024
        ),
        cost_estimate=pl.CostEstimate(flops=20000000000, bytes_accessed=9000000, transcendentals=0),
        name="finish",
    )(total, an_hi, an_lo, send_map, load_int_t, load_if, kinv_int, sinv_t)


def per_device(
    u_int, u_if, load_int, load_if, conn, send_map, counts, elem_size, stiffness,
    yield_stress, relax_rate, stress_init, kinv_int, sinv,
):
    reach = send_map.shape[0] // 2
    offsets = list(range(-reach, 0)) + list(range(1, reach + 1))
    dom, grps = lax.axis_size("dom"), lax.axis_size("grp")
    sizes = (dom // 8, 4, 2, grps)
    u_int_t, conn_t = jnp.transpose(u_int), jnp.transpose(conn)
    tail = halo(u_int_t, u_if, send_map, offsets, dom)
    params = [v.reshape(1, -1) for v in (elem_size, stiffness, yield_stress, relax_rate)]
    stress_end, force = element_update(u_int_t, tail, conn_t, counts, params, stress_init)
    du_int_t, du_if = finish(
        force, send_map, jnp.transpose(load_int), load_if, kinv_int, jnp.transpose(sinv), offsets, sizes
    )
    return (jnp.transpose(du_int_t), du_if, stress_end)


def solution(mesh):
    both = ("grp", "dom")
    return jax.shard_map(
        per_device,
        mesh=mesh,
        in_specs=(
            P(both, None), P("dom", None), P(both, None), P("dom", None), P(both, None),
            P(both, None), P(both), P(both), P(both), P(both), P(both), P(None, both),
            P(both, None), P("grp", "dom"),
        ),
        out_specs=(P(both, None), P(both, None), P(None, both)),
        check_vma=False,
    )
```
